32 devices in a mesh: dp: 8 (over y, x, core), tensor: 4 (over z).
Axes of the slice: x: 2, y: 2, z: 4, core: 2. Of those that a mesh axis runs over, the one named last changes fastest.
Arguments:
- token_ids: int32 [2, 8192], P(None, 'dp'), may hold values from 0 to 50287
- lengths: int32 [2, 8], P(None, 'dp'), may hold values from 170 to 1024, as said below
- loss_pos: int32 [2, 2048], P(None, 'dp'), may hold values from 0 to 1023
- targets: int32 [2, 2048], P(None, 'dp'), may hold values from 0 to 50287
- embed: float32 [12572, 4096], P('tensor', 'dp'), may hold values from -0.375 to 0.375
- embed_m: float32 [12572, 4096], P('tensor', 'dp'), may hold values from -0.001953125 to 0.001953125
- embed_v: float32 [12572, 4096], P('tensor', 'dp'), may hold values from 1.5456417e-08 to 6.1825666e-08
- w_zx: float32 [2, 1024, 2, 2048], P(None, 'dp', None, 'tensor'), may hold values from -0.1875 to 0.1875
- w_zx_m: float32 [2, 1024, 2, 2048], P(None, 'dp', None, 'tensor'), may hold values from -0.001953125 to 0.001953125
- w_zx_v: float32 [2, 1024, 2, 2048], P(None, 'dp', None, 'tensor'), may hold values from 1.5456417e-08 to 6.1825666e-08
- w_bcdt: float32 [2, 1024, 288], P(None, 'dp'), may hold values from -0.1875 to 0.1875
- w_bcdt_m: float32 [2, 1024, 288], P(None, 'dp'), may hold values from -0.001953125 to 0.001953125
- w_bcdt_v: float32 [2, 1024, 288], P(None, 'dp'), may hold values from 1.5456417e-08 to 6.1825666e-08
- w_out: float32 [2, 1024, 2048], P(None, 'dp', 'tensor'), may hold values from -0.125 to 0.125
- w_out_m: float32 [2, 1024, 2048], P(None, 'dp', 'tensor'), may hold values from -0.001953125 to 0.001953125
- w_out_v: float32 [2, 1024, 2048], P(None, 'dp', 'tensor'), may hold values from 1.5456417e-08 to 6.1825666e-08
- channel: float32 [2, 6, 2048], P(None, None, 'tensor'), may hold values from -1 to 1.8
- channel_m: float32 [2, 6, 2048], P(None, None, 'tensor'), may hold values from -0.0078125 to 0.0078125
- channel_v: float32 [2, 6, 2048], P(None, None, 'tensor'), may hold values from 2.4730267e-07 to 9.892107e-07
- per_head: float32 [2, 3, 32], P(None, None, 'tensor'), may hold values from -4.5 to 2.8
- per_head_m: float32 [2, 3, 32], P(None, None, 'tensor'), may hold values from -0.0078125 to 0.0078125
- per_head_v: float32 [2, 3, 32], P(None, None, 'tensor'), may hold values from 2.4730267e-07 to 9.892107e-07
- bc_conv: float32 [2, 5, 256], replicated, may hold values from -1 to 1
- bc_conv_m: float32 [2, 5, 256], replicated, may hold values from -0.0078125 to 0.0078125
- bc_conv_v: float32 [2, 5, 256], replicated, may hold values from 2.4730267e-07 to 9.892107e-07
- gains: float32 [3, 1024], replicated, may hold values from 0.4 to 1.8
- gains_m: float32 [3, 1024], replicated, may hold values from -0.0078125 to 0.0078125
- gains_v: float32 [3, 1024], replicated, may hold values from 2.4730267e-07 to 9.892107e-07
Outputs:
- loss_sum: float32 [], replicated
- loss_count: float32 [], replicated
- grad_norm: float32 [], replicated
- group_norms: float32 [2, 14], replicated
- embed_new: float32 [12572, 4096], P('tensor', 'dp')
- embed_m_new: float32 [12572, 4096], P('tensor', 'dp')
- embed_v_new: float32 [12572, 4096], P('tensor', 'dp')
- w_zx_new: float32 [2, 1024, 2, 2048], P(None, 'dp', None, 'tensor')
- w_zx_m_new: float32 [2, 1024, 2, 2048], P(None, 'dp', None, 'tensor')
- w_zx_v_new: float32 [2, 1024, 2, 2048], P(None, 'dp', None, 'tensor')
- w_bcdt_new: float32 [2, 1024, 288], P(None, 'dp')
- w_bcdt_m_new: float32 [2, 1024, 288], P(None, 'dp')
- w_bcdt_v_new: float32 [2, 1024, 288], P(None, 'dp')
- w_out_new: float32 [2, 1024, 2048], P(None, 'dp', 'tensor')
- w_out_m_new: float32 [2, 1024, 2048], P(None, 'dp', 'tensor')
- w_out_v_new: float32 [2, 1024, 2048], P(None, 'dp', 'tensor')
- channel_new: float32 [2, 6, 2048], P(None, None, 'tensor')
- channel_m_new: float32 [2, 6, 2048], P(None, None, 'tensor')
- channel_v_new: float32 [2, 6, 2048], P(None, None, 'tensor')
- per_head_new: float32 [2, 3, 32], P(None, None, 'tensor')
- per_head_m_new: float32 [2, 3, 32], P(None, None, 'tensor')
- per_head_v_new: float32 [2, 3, 32], P(None, None, 'tensor')
- bc_conv_new: float32 [2, 5, 256], replicated
- bc_conv_m_new: float32 [2, 5, 256], replicated
- bc_conv_v_new: float32 [2, 5, 256], replicated
- gains_new: float32 [3, 1024], replicated
- gains_m_new: float32 [3, 1024], replicated
- gains_v_new: float32 [3, 1024], replicated
The draws below stay inside these ranges and needn't reach their ends.
Inputs may be any that keep to these rules, and one draw needn't show every extreme that they name: Positions at or past a sequence's length are padding; the lengths of each micro-batch sum to exactly 4776.
All inputs are finite; a program needn't handle non-finite values.
Results may differ from the reference program's by a relative error of at most 0.025.
Values may be sent and summed in bfloat16 or wider, within the bound.
No kernel may reach another device: no remote copies, remote signals or barrier semaphores. Data moves between devices by JAX's collectives and lax.ppermute only.
A program may use at most 448 MiB of HBM per device.

```python
import math
import jax
import jax.numpy as jnp
import numpy as np
from jax import lax

D = 1024
INNER = 2048
HEADS = 32
HDIM = 64
STATE = 128
CONV = 4
SPAN = 256
VOCAB = 50288
LAYERS = 2
MICRO = 2
STEP = 5
SEQ = 1024
LOSS_ROWS = 256
GROUPS = 8
TOKENS = 8192
SCORED = 2048
PARAMS = 64698048


def draw_lengths(key, part):
    key = jax.random.fold_in(key, 11)
    first, second = jax.random.split(key)
    lowest = SEQ // 6
    stride = (SEQ - lowest) // (GROUPS - 1)
    ranks = jnp.arange(GROUPS, dtype=jnp.int32)
    base = jnp.where(ranks == GROUPS - 1, SEQ, lowest + stride * ranks).astype(jnp.int32)
    orders = jax.vmap(lambda row_key: jax.random.permutation(row_key, GROUPS))(jax.random.split(first, MICRO)).astype(jnp.int32)
    room = jnp.minimum(base[None, :] - lowest, SEQ - base[orders]).astype(jnp.int32)
    given = jax.random.randint(second, (MICRO, GROUPS), 0, room // 2 + 1, dtype=jnp.int32)
    micro_ids = jnp.arange(MICRO, dtype=jnp.int32)[:, None]
    given = jnp.where((micro_ids == 0) & (ranks[None, :] == GROUPS - 1), 0, given)
    given = jnp.where((micro_ids == MICRO - 1) & (orders == 0), 0, given)
    received = jax.vmap(lambda order, amount: jnp.zeros((GROUPS,), jnp.int32).at[order].add(amount))(orders, given)
    return (base[None, :] - given + received).astype(jnp.int32)


def draw_channel(key, part):
    key = jax.random.fold_in(key, 12)
    first, second, third = jax.random.split(key, 3)
    kernel = jax.random.uniform(first, (LAYERS, CONV, INNER), jnp.float32, -1.0, 1.0)
    offset = jax.random.uniform(second, (LAYERS, 1, INNER), jnp.float32, -0.5, 0.5)
    rising = 0.5 + jnp.arange(INNER, dtype=jnp.float32) / INNER
    norm_gain = rising[None, None, :] * jax.random.uniform(third, (LAYERS, 1, INNER), jnp.float32, 0.8, 1.2)
    return jnp.concatenate([kernel, offset, norm_gain], axis=1)


def draw_per_head(key, part):
    key = jax.random.fold_in(key, 13)
    first, second, third = jax.random.split(key, 3)
    step_bias = jax.random.uniform(first, (LAYERS, 1, HEADS), jnp.float32, -4.5, -1.0)
    log_rate = jax.random.uniform(second, (LAYERS, 1, HEADS), jnp.float32, 0.0, 2.77)
    skip = jax.random.uniform(third, (LAYERS, 1, HEADS), jnp.float32, 0.5, 1.5)
    return jnp.concatenate([step_bias, log_rate, skip], axis=1)


def draw_bc_conv(key, part):
    key = jax.random.fold_in(key, 14)
    first, second = jax.random.split(key)
    kernel = jax.random.uniform(first, (LAYERS, CONV, 2 * STATE), jnp.float32, -1.0, 1.0)
    offset = jax.random.uniform(second, (LAYERS, 1, 2 * STATE), jnp.float32, -0.5, 0.5)
    return jnp.concatenate([kernel, offset], axis=1)


def draw_gains(key, part):
    key = jax.random.fold_in(key, 15)
    rising = 0.5 + jnp.arange(D, dtype=jnp.float32) / D
    return rising[None, :] * jax.random.uniform(key, (LAYERS + 1, D), jnp.float32, 0.8, 1.2)


def draw_embed(key, part):
    key = jax.random.fold_in(key, 16)
    ramp = jnp.arange(VOCAB, dtype=jnp.float32)[:, None] / VOCAB
    values = jnp.clip(jax.random.normal(key, (VOCAB, D), jnp.float32), -4.0, 4.0) * (1.0 + 2.0 * ramp)
    return (values * D ** (-0.5)).reshape(VOCAB // 4, 4 * D)


def set_ends(values, key, smallest, high):
    longest = values.shape.index(max(values.shape))
    spots = []
    for shift in (0, 1):
        where = [jax.random.randint(jax.random.fold_in(key, axis), (), 0, length) for axis, length in enumerate(values.shape)]
        where[longest] = (where[longest] + shift) % values.shape[longest]
        spots.append(tuple(where))
    return values.at[spots[0]].set(smallest).at[spots[1]].set(high)


def shard_levels(own_key, extent, pieces, low, high):
    loudness, own = 1.0, jax.random.fold_in(own_key, 6)
    for position, blocks in pieces:
        draws = jnp.exp(jax.random.uniform(jax.random.fold_in(own, position), (blocks,), jnp.float32, low / len(pieces), high / len(pieces)))
        loudness = loudness * jnp.repeat(draws, extent[position] // blocks).reshape([-1 if axis == position else 1 for axis in range(len(extent))])
    return loudness


def rank_bounds(count, skew):
    portions = [(1 << 20) // math.isqrt(grade ** skew) + 1 for grade in range(1, count + 1)]
    scale = 1 + sum(portions) // (1 << 30)
    return np.cumsum(np.array([max(1, weight // scale) for weight in portions]))


def skewed_ids(stream_key, shape, number_of, skew):
    table = rank_bounds(number_of, skew)
    pick = jax.random.randint(jax.random.fold_in(stream_key, 1), shape, 0, int(table[number_of - 1]))
    rank = jnp.searchsorted(jnp.asarray(table, jnp.int32), pick, side="right")
    return jax.random.permutation(jax.random.fold_in(stream_key, 2), number_of)[rank].astype(jnp.int32)


def bell_draw(rng, dims, scale, reach, pieces=(), kind=jnp.bfloat16):
    entries = jax.random.normal(rng, dims, jnp.float32) * scale
    if len(pieces) > 0:
        entries = shard_levels(rng, dims, pieces, -0.22, 0.18) * entries
    return jnp.clip(entries, min=-reach, max=reach).astype(kind)


def setup_inputs(seed: int = 0) -> dict:
    seeds = jax.random.split(jax.random.key(seed), 29)
    return {
        "token_ids": set_ends(skewed_ids(seeds[0], (MICRO, TOKENS), VOCAB, 2), jax.random.fold_in(seeds[0], 3), 0, VOCAB - 1).astype(jnp.int32),
        "lengths": draw_lengths(jax.random.fold_in(seeds[28], 71), 0),
        "loss_pos": set_ends(jax.random.randint(seeds[2], (MICRO, SCORED), 0, SEQ), jax.random.fold_in(seeds[2], 1), 0, SEQ - 1).astype(jnp.int32),
        "targets": set_ends(skewed_ids(seeds[3], (MICRO, SCORED), VOCAB, 2), jax.random.fold_in(seeds[3], 3), 0, VOCAB - 1).astype(jnp.int32),
        "embed": draw_embed(jax.random.fold_in(seeds[28], 71), 0),
        "embed_m": bell_draw(seeds[5], (VOCAB // 4, 4 * D), (PARAMS ** -0.5), 0.001953125, ((0, 4), (1, 8)), jnp.float32),
        "embed_v": jnp.clip(jnp.exp(math.log(6.18256663642569e-08) - 1.3862944 * jax.random.uniform(seeds[6], (VOCAB // 4, 4 * D), jnp.float32) ** shard_levels(seeds[6], (VOCAB // 4, 4 * D), ((0, 4), (1, 8)), -0.2, 0.2)), 1.5456416591064226e-08, 6.18256663642569e-08),
        "w_zx": bell_draw(seeds[7], (LAYERS, D, 2, INNER), D ** -0.5, 0.1875, ((1, 8), (3, 4)), jnp.float32),
        "w_zx_m": bell_draw(seeds[8], (LAYERS, D, 2, INNER), (PARAMS ** -0.5), 0.001953125, ((1, 8), (3, 4)), jnp.float32),
        "w_zx_v": jnp.clip(jnp.exp(math.log(6.18256663642569e-08) - 1.3862944 * jax.random.uniform(seeds[9], (LAYERS, D, 2, INNER), jnp.float32) ** shard_levels(seeds[9], (LAYERS, D, 2, INNER), ((1, 8), (3, 4)), -0.2, 0.2)), 1.5456416591064226e-08, 6.18256663642569e-08),
        "w_bcdt": bell_draw(seeds[10], (LAYERS, D, 2 * STATE + HEADS), D ** -0.5, 0.1875, ((1, 8),), jnp.float32),
        "w_bcdt_m": bell_draw(seeds[11], (LAYERS, D, 2 * STATE + HEADS), (PARAMS ** -0.5), 0.001953125, ((1, 8),), jnp.float32),
        "w_bcdt_v": jnp.clip(jnp.exp(math.log(6.18256663642569e-08) - 1.3862944 * jax.random.uniform(seeds[12], (LAYERS, D, 2 * STATE + HEADS), jnp.float32) ** shard_levels(seeds[12], (LAYERS, D, 2 * STATE + HEADS), ((1, 8),), -0.2, 0.2)), 1.5456416591064226e-08, 6.18256663642569e-08),
        "w_out": bell_draw(seeds[13], (LAYERS, D, INNER), INNER ** -0.5, 0.125, ((1, 8), (2, 4)), jnp.float32),
        "w_out_m": bell_draw(seeds[14], (LAYERS, D, INNER), (PARAMS ** -0.5), 0.001953125, ((1, 8), (2, 4)), jnp.float32),
        "w_out_v": jnp.clip(jnp.exp(math.log(6.18256663642569e-08) - 1.3862944 * jax.random.uniform(seeds[15], (LAYERS, D, INNER), jnp.float32) ** shard_levels(seeds[15], (LAYERS, D, INNER), ((1, 8), (2, 4)), -0.2, 0.2)), 1.5456416591064226e-08, 6.18256663642569e-08),
        "channel": draw_channel(jax.random.fold_in(seeds[28], 71), 0),
        "channel_m": bell_draw(seeds[17], (LAYERS, 6, INNER), (4.0 * PARAMS ** -0.5), 0.0078125, ((2, 4),), jnp.float32),
        "channel_v": jnp.clip(jnp.exp(math.log(9.892106618281105e-07) - 1.3862944 * jax.random.uniform(seeds[18], (LAYERS, 6, INNER), jnp.float32) ** shard_levels(seeds[18], (LAYERS, 6, INNER), ((2, 4),), -0.2, 0.2)), 2.473026654570276e-07, 9.892106618281105e-07),
        "per_head": draw_per_head(jax.random.fold_in(seeds[28], 71), 0),
        "per_head_m": bell_draw(seeds[20], (LAYERS, 3, HEADS), (4.0 * PARAMS ** -0.5), 0.0078125, ((2, 4),), jnp.float32),
        "per_head_v": jnp.clip(jnp.exp(math.log(9.892106618281105e-07) - 1.3862944 * jax.random.uniform(seeds[21], (LAYERS, 3, HEADS), jnp.float32) ** shard_levels(seeds[21], (LAYERS, 3, HEADS), ((2, 4),), -0.2, 0.2)), 2.473026654570276e-07, 9.892106618281105e-07),
        "bc_conv": draw_bc_conv(jax.random.fold_in(seeds[28], 71), 0),
        "bc_conv_m": bell_draw(seeds[23], (LAYERS, 5, 2 * STATE), (4.0 * PARAMS ** -0.5), 0.0078125, (), jnp.float32),
        "bc_conv_v": jnp.clip(jnp.exp(jax.random.uniform(seeds[24], (LAYERS, 5, 2 * STATE), jnp.float32, math.log(2.473026654570276e-07), math.log(9.892106618281105e-07))), 2.473026654570276e-07, 9.892106618281105e-07),
        "gains": draw_gains(jax.random.fold_in(seeds[28], 71), 0),
        "gains_m": bell_draw(seeds[26], (LAYERS + 1, D), (4.0 * PARAMS ** -0.5), 0.0078125, (), jnp.float32),
        "gains_v": jnp.clip(jnp.exp(jax.random.uniform(seeds[27], (LAYERS + 1, D), jnp.float32, math.log(2.473026654570276e-07), math.log(9.892106618281105e-07))), 2.473026654570276e-07, 9.892106618281105e-07),
    }


precise = lax.Precision.HIGHEST
norm_eps = 1e-05
adam_eps = 1e-06
clip_limit = 1.0
first_decay = 0.5
second_decay = 0.5
learn_rate = 0.3
weight_decay = 0.01

@jax.custom_vjp
def low(v):
    return lax.optimization_barrier(v.astype(jnp.bfloat16)).astype(jnp.float32)

@jax.custom_vjp
def low_back(v):
    return v

def low_keep(v):
    return (low(v), None)

def low_pass(kept, grad):
    return (grad,)

def back_keep(v):
    return (v, None)

def back_low(kept, grad):
    return (low(grad),)
low.defvjp(low_keep, low_pass)
low_back.defvjp(back_keep, back_low)

def rms_scale(values, weights):
    return values * lax.rsqrt(lax.optimization_barrier(jnp.mean(values * values, axis=-1, keepdims=True)) + norm_eps) * weights

def causal_conv(signal, kernel, offset):
    width = kernel.shape[0]
    count = signal.shape[0]
    padded = jnp.pad(signal, ((width - 1, 0), (0, 0)))
    result = offset + padded[:count] * kernel[0]
    for shift_at in range(1, width):
        result = result + padded[shift_at:shift_at + count] * kernel[shift_at]
    return result

def ssd_scan(inputs, step_dt, decay, keys_b, reads_c):
    length, heads, width = inputs.shape
    blocks = length // SPAN
    scaled = (inputs * step_dt[:, :, None]).reshape(blocks, SPAN, heads, width)
    summed = jnp.cumsum(decay.reshape(blocks, SPAN, heads), axis=1)
    keys_q = keys_b.reshape(blocks, SPAN, -1)
    reads_q = reads_c.reshape(blocks, SPAN, -1)
    causal = (jnp.arange(SPAN)[:, None] >= jnp.arange(SPAN)[None, :])[None, :, :, None]
    spread = summed[:, :, None, :] - summed[:, None, :, :]
    fading = jnp.where(causal, jnp.exp(jnp.where(causal, spread, 0.0)), 0.0)
    scores = jnp.einsum('btn,bsn->bts', reads_q, keys_q, precision=precise)
    within = jnp.einsum('bts,btsh,bshp->bthp', scores, fading, scaled, precision=precise)
    to_end = jnp.exp(summed[:, -1:, :] - summed)
    states = jnp.einsum('bsn,bsh,bshp->bhnp', keys_q, to_end, scaled, precision=precise)

    def advance(state, pair):
        fresh, total = pair
        return (state * jnp.exp(total)[:, None, None] + fresh, state)
    _, entering = lax.scan(advance, jnp.zeros_like(states[0]), (states, summed[:, -1, :]))
    across = jnp.einsum('btn,bth,bhnp->bthp', reads_q, jnp.exp(summed), entering, precision=precise)
    return (within + across).reshape(length, heads, width)

def ssd_mixer(gate_in, x_raw, bc_raw, dt_raw, channel, per_head, bc_conv):
    length = gate_in.shape[0]
    heads = per_head.shape[1]
    x_conv = jax.nn.silu(causal_conv(x_raw, channel[:CONV], channel[CONV]))
    bc_out = jax.nn.silu(causal_conv(bc_raw, bc_conv[:CONV], bc_conv[CONV]))
    step_dt = jax.nn.softplus(dt_raw + per_head[0])
    decay = -jnp.exp(per_head[1]) * step_dt
    inputs = x_conv.reshape(length, heads, HDIM)
    mixed = ssd_scan(inputs, step_dt, decay, bc_out[:, :STATE], bc_out[:, STATE:]) + per_head[2][None, :, None] * inputs
    return mixed.reshape(length, -1) * jax.nn.silu(gate_in)

def layer_step(resid, w_zx, w_bcdt, w_out, gain, channel, per_head, bc_conv):
    normed = low(rms_scale(resid, gain))
    zx = low_back(jnp.einsum('td,dki->tki', normed, low(w_zx), precision=precise))
    bcdt = low_back(jnp.dot(normed, low(w_bcdt), precision=precise))
    gated = ssd_mixer(zx[:, 0], zx[:, 1], bcdt[:, :2 * STATE], bcdt[:, 2 * STATE:], channel, per_head, bc_conv)
    scaled = low(gated * lax.rsqrt(lax.optimization_barrier(jnp.mean(gated * gated, axis=-1, keepdims=True)) + norm_eps) * channel[CONV + 1])
    return resid + low_back(jnp.dot(scaled, low(w_out).T, precision=precise))

def sequence_loss(params, token_row, length, positions, target_row):
    embed, w_zx, w_bcdt, w_out, channel, per_head, bc_conv, gains = params
    table = low(embed.reshape(VOCAB, D))
    resid = low_back(table[token_row])
    for depth in range(LAYERS):
        resid = jax.checkpoint(layer_step)(resid, w_zx[depth], w_bcdt[depth], w_out[depth], gains[depth], channel[depth], per_head[depth], bc_conv[depth])
    final = low(rms_scale(resid, gains[LAYERS]))
    logits = low_back(jnp.dot(final[positions], table.T, precision=precise))
    picked = jnp.take_along_axis(logits, target_row[:, None], axis=1)[:, 0]
    counted = (positions < length).astype(jnp.float32)
    return (jnp.sum(counted * (jax.nn.logsumexp(logits, axis=1) - picked)), jnp.sum(counted))

def adapt(weight, first, second, grad):
    first_new = first_decay * first + (1.0 - first_decay) * grad
    second_new = second_decay * second + (1.0 - second_decay) * grad * grad
    update = first_new / (1.0 - first_decay ** STEP) / (jnp.sqrt(second_new / (1.0 - second_decay ** STEP)) + adam_eps) + weight_decay * weight
    return (first_new, second_new, update)

def group_squares(values, stacked):
    if stacked:
        return lax.optimization_barrier(jnp.sum(values * values, axis=tuple(range(1, values.ndim))))
    return jnp.sum(values * values)[None]

def reference(token_ids, lengths, loss_pos, targets, embed, embed_m, embed_v, w_zx, w_zx_m, w_zx_v, w_bcdt, w_bcdt_m, w_bcdt_v, w_out, w_out_m, w_out_v, channel, channel_m, channel_v, per_head, per_head_m, per_head_v, bc_conv, bc_conv_m, bc_conv_v, gains, gains_m, gains_v):
    params = (embed, w_zx, w_bcdt, w_out, channel, per_head, bc_conv, gains)
    items = (token_ids.reshape(MICRO * GROUPS, SEQ), lengths.reshape(MICRO * GROUPS), loss_pos.reshape(MICRO * GROUPS, LOSS_ROWS), targets.reshape(MICRO * GROUPS, LOSS_ROWS))

    def accumulate(carry, item):
        grads, loss_total, count_total = carry
        (loss_part, count_part), pull = jax.vjp(lambda weights: sequence_loss(weights, item[0], item[1], item[2], item[3]), params)
        fresh = pull((jnp.ones((), jnp.float32), jnp.zeros((), jnp.float32)))[0]
        return ((jax.tree.map(jnp.add, grads, fresh), loss_total + loss_part, count_total + count_part), None)
    start = (jax.tree.map(jnp.zeros_like, params), jnp.zeros((), jnp.float32), jnp.zeros((), jnp.float32))
    (grads, loss_sum, loss_count), _ = lax.scan(accumulate, start, items)
    grad_norm = jnp.sqrt(sum((jnp.sum(grad * grad) for grad in grads)))
    scale = jnp.minimum(1.0, clip_limit / grad_norm)
    states = ((embed_m, embed_v), (w_zx_m, w_zx_v), (w_bcdt_m, w_bcdt_v), (w_out_m, w_out_v), (channel_m, channel_v), (per_head_m, per_head_v), (bc_conv_m, bc_conv_v), (gains_m, gains_v))
    layered_kinds = (False, True, True, True, True, True, True, False)
    results = []
    weight_norms = []
    step_norms = []
    for weight, moments, grad, layered in zip(params, states, grads, layered_kinds):
        first_new, second_new, update = adapt(weight, moments[0], moments[1], grad * scale)
        weight_norm = jnp.sqrt(group_squares(weight, layered))
        step_norm = jnp.sqrt(group_squares(update, layered))
        ratio = weight_norm / step_norm
        if layered:
            factor = ratio.reshape((weight.shape[0],) + (1,) * (weight.ndim - 1))
        else:
            factor = ratio[0]
        results += [weight - learn_rate * factor * update, first_new, second_new]
        weight_norms.append(weight_norm)
        step_norms.append(step_norm)
    group_norms = jnp.stack([jnp.concatenate(weight_norms), jnp.concatenate(step_norms)])
    return (loss_sum, loss_count, grad_norm, group_norms, results[0], results[1], results[2], results[3], results[4], results[5], results[6], results[7], results[8], results[9], results[10], results[11], results[12], results[13], results[14], results[15], results[16], results[17], results[18], results[19], results[20], results[21], results[22], results[23])
```

```python
import functools

import jax
import jax.numpy as jnp
from jax import lax
from jax.experimental import pallas as pl
from jax.experimental.pallas import tpu as pltpu
from jax.sharding import Mesh
from jax.sharding import PartitionSpec as P

D = 1024
INNER = 2048
HEADS = 32
HDIM = 64
STATE = 128
CONV = 4
LAYERS = 2
MICRO = 2
STEP = 5

BLOCK = 128
HALO = 16
WIDTH = 512
GROUPS = INNER // WIDTH
LANES = 128
TILE = 640
CLASSES = 4
PAST = 1 << 11

norm_eps = 1e-05
adam_eps = 1e-06
clip_limit = 1.0
first_decay = 0.5
second_decay = 0.5
learn_rate = 0.3
weight_decay = 0.01

f32 = jnp.float32
bf16 = jnp.bfloat16
full = lax.Precision.HIGHEST
DP = ("chip", "core")
VMEM_BYTES = 58 * 1024 * 1024


def dot(left, right, left_dim, right_dim, precision=None):
    return lax.dot_general(
        left,
        right,
        (((left_dim,), (right_dim,)), ((), ())),
        precision=precision,
        preferred_element_type=f32,
    )


def nn(left, right, precision=None):
    return dot(left, right, 1, 0, precision)


def nt(left, right, precision=None):
    return dot(left, right, 1, 1, precision)


def tn(left, right, precision=None):
    return dot(left, right, 0, 0, precision)


def sigmoid(v):
    return 1.0 / (1.0 + jnp.exp(-v))


def softplus(v):
    return jnp.maximum(v, 0.0) + jnp.log1p(jnp.exp(-jnp.abs(v)))


def iota(shape, axis):
    return lax.broadcasted_iota(jnp.int32, shape, axis)


def call(kernel, grid, in_specs, out_specs, out_shape, scratch, prefetch=0, flops=0, bytes_moved=0):
    return pl.pallas_call(
        kernel,
        grid_spec=pltpu.PrefetchScalarGridSpec(
            num_scalar_prefetch=prefetch,
            grid=grid,
            in_specs=in_specs,
            out_specs=out_specs,
            scratch_shapes=scratch,
        ),
        out_shape=out_shape,
        compiler_params=pltpu.CompilerParams(
            vmem_limit_bytes=VMEM_BYTES, dimension_semantics=("arbitrary",) * len(grid)
        ),
        cost_estimate=pl.CostEstimate(
            flops=flops, bytes_accessed=bytes_moved, transcendentals=0
        ),
    )


def whole(shape):
    return pl.BlockSpec(shape, lambda *_: (0,) * len(shape))


def packed_zx(packed):
    rows = D // packed.shape[0]
    return pl.BlockSpec((packed.shape[0], rows, D), lambda g: (0, g, 0))


def unpacked_out(ref, low, rows):
    lines = ref[:, low : low + rows // 2, :]
    both = jnp.concatenate([lines[:, :, :WIDTH], lines[:, :, WIDTH:]], axis=1)
    return both.reshape(D, WIDTH)


def columns(rows, width=WIDTH, at=0):
    return pl.BlockSpec((rows, width), lambda g: (0, g + at))


def struct(shape, dtype=f32):
    return jax.ShapeDtypeStruct(shape, dtype)


def conv_rows(ref, taps, rows, low, width):
    result = taps[CONV : CONV + 1, :]
    for j in range(CONV):
        start = HALO - CONV + 1 + j
        result = result + ref[start : start + rows, low : low + width] * taps[j : j + 1, :]
    return result


def triangle():
    return iota((BLOCK, BLOCK), 0) >= iota((BLOCK, BLOCK), 1)


def spread(group):
    head = iota((LANES, WIDTH), 0)
    lane = iota((LANES, WIDTH), 1)
    return (head == group * (WIDTH // HDIM) + lane // HDIM).astype(f32)


def small_parts(rows, bcdt, headp, bcv, s_b, s_c, s_dt, s_cum, s_cumt, s_g):
    pre = conv_rows(bcdt, bcv, rows, 0, 2 * STATE)
    bc = (pre * sigmoid(pre)).astype(bf16)
    s_b[...] = bc[:, :STATE]
    s_c[...] = bc[:, STATE:]
    dt = softplus(bcdt[HALO:, 2 * STATE :] + headp[0:1, :])
    s_dt[...] = dt
    decay = headp[1:2, :] * dt
    keep = triangle()
    lower = keep.astype(f32)
    for b in range(rows // BLOCK):
        r = slice(b * BLOCK, (b + 1) * BLOCK)
        cum = nn(lower, decay[r], full)
        s_cum[r, :] = cum
        s_cumt[:, r] = cum.T
        s_g[b] = jnp.where(keep, nt(bc[r, STATE:], bc[r, :STATE]), 0.0)


def head_rows(s_cumt, group, r):
    heads = WIDTH // HDIM
    return s_cumt[pl.ds(pl.multiple_of(group * heads, heads), heads), r]


def fading(cum_e, cum_rows, head):
    column = cum_e[:, head * HDIM : head * HDIM + 1]
    return jnp.exp(jnp.minimum(column - cum_rows[head : head + 1, :], 0.0))


def one_head(values, j):
    first = iota(values.shape, 1) < HDIM
    return jnp.where(first if j == 0 else jnp.logical_not(first), values, 0.0).astype(bf16)


def small_scratch(rows):
    return [
        pltpu.VMEM((rows, STATE), bf16),
        pltpu.VMEM((rows, STATE), bf16),
        pltpu.VMEM((rows, LANES), f32),
        pltpu.VMEM((rows, LANES), f32),
        pltpu.VMEM((LANES, rows), f32),
        pltpu.VMEM((rows // BLOCK, BLOCK, BLOCK), f32),
    ]


def scan_kernel(
    nx, w_zx, wb, chan, headp, bcv,
    y_o, gate_o, xraw_o, st_o, bcdt_o, c_o, ecf_o,
    s_b, s_c, s_dt, s_cum, s_cumt, s_g,
):
    rows = y_o.shape[0]
    group = pl.program_id(0)

    @pl.when(group == 0)
    def _():
        bcdt_o[...] = nn(nx[...], wb[...])
        small_parts(rows, bcdt_o, headp, bcv, s_b, s_c, s_dt, s_cum, s_cumt, s_g)
        c_o[...] = s_c[...]
        run = jnp.zeros((1, LANES), f32)
        for b in range(rows // BLOCK):
            r = slice(b * BLOCK, (b + 1) * BLOCK)
            ecf_o[r, :] = jnp.exp(s_cum[r, :] + run)
            run = run + s_cum[(b + 1) * BLOCK - 1 : (b + 1) * BLOCK, :]

    both = w_zx[...].reshape(D, 2 * WIDTH)
    gate_o[...] = nn(nx[HALO:, :], both[:, :WIDTH])
    xraw_o[...] = nn(nx[...], both[:, WIDTH:])
    pre = conv_rows(xraw_o, chan, rows, 0, WIDTH)
    xc = pre * sigmoid(pre)
    expand = spread(group)
    u = xc * nn(s_dt[...], expand, full)
    skip = nn(headp[...], expand, full)[2:3, :]
    state = jnp.zeros((STATE, WIDTH), f32)
    for b in range(rows // BLOCK):
        r = slice(b * BLOCK, (b + 1) * BLOCK)
        cum_e = nn(s_cum[r, :], expand, full)
        total = cum_e[BLOCK - 1 : BLOCK, :]
        keys, reads = s_b[r, :], s_c[r, :]
        y = jnp.exp(cum_e) * nn(reads, state.astype(bf16)) + skip * xc[r]
        cum_rows = head_rows(s_cumt, group, r)
        pieces = []
        for pair in range(WIDTH // LANES):
            both = u[r, pair * LANES : (pair + 1) * LANES]
            piece = jnp.zeros((BLOCK, LANES), f32)
            for j in range(2):
                weights = (fading(cum_e, cum_rows, 2 * pair + j) * s_g[b]).astype(bf16)
                piece = piece + nn(weights, one_head(both, j))
            pieces.append(piece)
        y_o[r, :] = y + jnp.concatenate(pieces, axis=1)
        fresh = tn(keys, (u[r] * jnp.exp(total - cum_e)).astype(bf16))
        state = state * jnp.exp(total) + fresh
    st_o[...] = state


def scan_front(nx, packed, wb, chan, headp, bcv):
    ext = nx.shape[0]
    rows = ext - HALO
    return call(
        scan_kernel,
        (GROUPS,),
        [
            whole((ext, D)),
            packed_zx(packed),
            whole(wb.shape),
            columns(8),
            whole((8, LANES)),
            whole((8, 2 * STATE)),
        ],
        [
            columns(rows),
            columns(rows),
            columns(ext),
            columns(STATE),
            whole((ext, 384)),
            whole((rows, STATE)),
            whole((rows, LANES)),
        ],
        [
            struct((rows, INNER)),
            struct((rows, INNER)),
            struct((ext, INNER)),
            struct((STATE, INNER)),
            struct((ext, 384)),
            struct((rows, STATE), bf16),
            struct((rows, LANES)),
        ],
        small_scratch(rows),
        flops=2 * ext * D * 2 * INNER,
        bytes_moved=2 * D * 2 * INNER + 12 * rows * INNER,
    )(nx, packed, wb, chan, headp, bcv)


def join_kernel(
    y, gate, c, ecf, st, chan, wout, resid, yf_o, scaled_o, inv_o, res_o, s_gated, s_square
):
    group = pl.program_id(0)
    ecf_e = nn(ecf[...], spread(group), full)
    yf = y[...] + ecf_e * nn(c[...], st[...].astype(bf16))
    yf_o[...] = yf
    gated = yf * (gate[...] * sigmoid(gate[...]))
    s_gated[group] = gated
    part = jnp.broadcast_to(jnp.sum(gated * gated, axis=1, keepdims=True), s_square.shape)

    @pl.when(group == 0)
    def _():
        s_square[...] = part

    @pl.when(group > 0)
    def _():
        s_square[...] += part

    @pl.when(group == GROUPS - 1)
    def _():
        inverse = lax.rsqrt(s_square[...] / INNER + norm_eps)
        inv_o[...] = inverse
        res = resid[...]
        for q in range(GROUPS):
            at = slice(q * WIDTH, (q + 1) * WIDTH)
            scaled = (s_gated[q] * inverse[:, :1] * chan[CONV + 1 : CONV + 2, at]).astype(bf16)
            scaled_o[:, at] = scaled
            height = D // wout.shape[0]
            res = res + nt(scaled, unpacked_out(wout, q * height // 2, height))
        res_o[...] = res


def scan_join(y, gate, c, ecf, st, chan, packed, resid):
    rows = y.shape[0]
    height = D // packed.shape[0]
    return call(
        join_kernel,
        (GROUPS,),
        [
            columns(rows),
            columns(rows),
            whole((rows, STATE)),
            whole((rows, LANES)),
            columns(STATE),
            whole((8, INNER)),
            pl.BlockSpec((packed.shape[0], 2 * height, D), lambda g: (0, 2, 0)),
            whole((rows, D)),
        ],
        [columns(rows), whole((rows, INNER)), whole((rows, LANES)), whole((rows, D))],
        [
            struct((rows, INNER)),
            struct((rows, INNER), bf16),
            struct((rows, LANES)),
            struct((rows, D)),
        ],
        [pltpu.VMEM((GROUPS, rows, WIDTH), f32), pltpu.VMEM((rows, LANES), f32)],
        flops=2 * rows * D * INNER,
        bytes_moved=2 * D * INNER + 14 * rows * INNER,
    )(y, gate, c, ecf, st, chan, packed, resid)


def unjoin_kernel(
    dout, wout, y, gate, inv, c, ecf, chan, dy_o, dgate_o, dgain_o, ds_o, s_scaled, s_along
):
    phase = pl.program_id(0)
    group = pl.program_id(1)
    gain = chan[CONV + 1 : CONV + 2, :]
    raw = gate[...]
    sig = sigmoid(raw)
    opened = raw * sig
    gated = y[...] * opened
    inverse = inv[:, :1]

    @pl.when(phase == 0)
    def _():
        dscaled = nn(dout[...], unpacked_out(wout, 0, D // wout.shape[0]))
        s_scaled[group] = dscaled
        part = jnp.sum(dscaled * gain * gated, axis=1, keepdims=True)
        part = jnp.broadcast_to(part, s_along.shape)

        @pl.when(group == 0)
        def _():
            s_along[...] = part

        @pl.when(group > 0)
        def _():
            s_along[...] += part

    @pl.when(phase == 1)
    def _():
        dscaled = s_scaled[group]
        pulled = inverse * inverse * inverse * s_along[:, :1] / INNER
        dgated = inverse * gain * dscaled - gated * pulled
        dgain = jnp.sum(dscaled * gated * inverse, axis=0, keepdims=True)
        dgain_o[...] = jnp.broadcast_to(dgain, dgain_o.shape)
        dy = dgated * opened
        dy_o[...] = dy
        dgate_o[...] = (dgated * y[...] * (sig * (1.0 + raw * (1.0 - sig)))).astype(bf16)
        ecf_e = nn(ecf[...], spread(group), full)
        ds_o[...] = tn(c[...], (ecf_e * dy).astype(bf16))


def scan_unjoin(dout, packed, y, gate, inv, c, ecf, chan):
    rows = y.shape[0]
    shares = packed.shape[0]

    def both(height):
        return pl.BlockSpec((height, WIDTH), lambda p, g: (0, g))

    def second(height):
        return pl.BlockSpec((height, WIDTH), lambda p, g: (0, g * p))

    return call(
        unjoin_kernel,
        (2, GROUPS),
        [
            whole((rows, D)),
            pl.BlockSpec(
                (shares, D // shares // 2, D),
                lambda p, g: (0, 2 * GROUPS + jnp.where(p == 0, g, GROUPS - 1), 0),
            ),
            both(rows),
            both(rows),
            whole((rows, LANES)),
            whole((rows, STATE)),
            whole((rows, LANES)),
            both(8),
        ],
        [second(rows), second(rows), second(8), second(STATE)],
        [
            struct((rows, INNER)),
            struct((rows, INNER), bf16),
            struct((8, INNER)),
            struct((STATE, INNER)),
        ],
        [pltpu.VMEM((GROUPS, rows, WIDTH), f32), pltpu.VMEM((rows, LANES), f32)],
        flops=2 * rows * D * INNER,
        bytes_moved=2 * D * INNER + 22 * rows * INNER,
    )(dout, packed, y, gate, inv, c, ecf, chan)


def head_sums(values, expand):
    if values.shape[0] == 1:
        return nt(jnp.broadcast_to(values, (8, values.shape[1])), expand, full)[0:1, :]
    return nt(values, expand, full)


def conv_back(ref, taps, pad, rows, low, width, taps_o, main, halo):
    grads = [jnp.sum(pad[HALO : HALO + rows, :] * ref[HALO - 3 + j : HALO - 3 + j + rows,
             low : low + width], axis=0, keepdims=True) for j in range(CONV)]
    grads.append(jnp.sum(pad[HALO : HALO + rows, :], axis=0, keepdims=True))
    taps_o[...] = jnp.concatenate(grads + [jnp.zeros((3, width), f32)], axis=0)
    total = jnp.zeros((HALO + rows, width), f32)
    for j in range(CONV):
        shift = CONV - 1 - j
        total = total + pad[shift : shift + HALO + rows, :] * taps[j : j + 1, :]
    halo(total[:HALO])
    main(total[HALO:])


def back_kernel(
    xraw, dy, bcdt, st, dst, chan, headp, bcv,
    dx_o, tail_o, halo_o, dchan_o, dbc_o, dbch_o, dheadp_o, dbcv_o,
    s_b, s_c, s_dt, s_cum, s_cumt, s_g,
    s_db, s_dc, s_dcum, s_ddt, s_dtot, s_dg, s_skip, s_pad, s_state, s_bcpad,
):
    rows = dy.shape[0]
    blocks = rows // BLOCK
    group = pl.program_id(0)

    @pl.when(group == 0)
    def _():
        small_parts(rows, bcdt, headp, bcv, s_b, s_c, s_dt, s_cum, s_cumt, s_g)
        for ref in (s_db, s_dc, s_dcum, s_ddt, s_dtot, s_dg, s_skip, s_pad, s_bcpad):
            ref[...] = jnp.zeros(ref.shape, f32)

    pre = conv_rows(xraw, chan, rows, 0, WIDTH)
    sig = sigmoid(pre)
    xc = pre * sig
    expand = spread(group)
    dt_e = nn(s_dt[...], expand, full)
    u = xc * dt_e
    skip = nn(headp[...], expand, full)[2:3, :]
    state = st[...]
    for b in range(blocks):
        r = slice(b * BLOCK, (b + 1) * BLOCK)
        s_state[b] = state
        if b < blocks - 1:
            cum_e = nn(s_cum[r, :], expand, full)
            total = cum_e[BLOCK - 1 : BLOCK, :]
            fresh = tn(s_b[r, :], (u[r] * jnp.exp(total - cum_e)).astype(bf16))
            state = state * jnp.exp(total) + fresh
    dstate = dst[...]
    dskip = jnp.zeros((1, WIDTH), f32)
    for b in reversed(range(blocks)):
        r = slice(b * BLOCK, (b + 1) * BLOCK)
        cum_e = nn(s_cum[r, :], expand, full)
        total = cum_e[BLOCK - 1 : BLOCK, :]
        keys, reads = s_b[r, :], s_c[r, :]
        to_here, to_end, passed = jnp.exp(cum_e), jnp.exp(total - cum_e), jnp.exp(total)
        u_b, dy_b = u[r], dy[r, :]
        u_low, dy_low = u_b.astype(bf16), dy_b.astype(bf16)
        state_low, dstate_low = s_state[b].astype(bf16), dstate.astype(bf16)
        faded = (dy_b * to_here).astype(bf16)
        y_across = to_here * nn(reads, state_low)
        s_dc[r, :] += nt(faded, state_low)
        du_across = to_end * nn(keys, dstate_low)
        s_db[r, :] += nt((u_b * to_end).astype(bf16), dstate_low)
        cum_rows = head_rows(s_cumt, group, r)
        y_pieces, du_pieces = [], []
        dscores = jnp.zeros((BLOCK, BLOCK), f32)
        for pair in range(WIDTH // LANES):
            at = slice(pair * LANES, (pair + 1) * LANES)
            y_piece = jnp.zeros((BLOCK, LANES), f32)
            du_piece = jnp.zeros((BLOCK, LANES), f32)
            for j in range(2):
                fade = fading(cum_e, cum_rows, 2 * pair + j)
                weights = (fade * s_g[b]).astype(bf16)
                dy_head = one_head(dy_b[:, at], j)
                y_piece = y_piece + nn(weights, one_head(u_b[:, at], j))
                du_piece = du_piece + tn(weights, dy_head)
                dscores = dscores + nt(dy_head, u_low[:, at]) * fade
            y_pieces.append(y_piece)
            du_pieces.append(du_piece)
        y_within = jnp.concatenate(y_pieces, axis=1)
        du_within = jnp.concatenate(du_pieces, axis=1)
        s_dg[b] += dscores
        du = du_within + du_across
        moved = u_b * du_across
        dcum = dy_low.astype(f32) * y_within + dy_b * y_across
        dcum = dcum - u_low.astype(f32) * du_within - moved
        s_dcum[r, :] += head_sums(dcum, expand)
        dtotal = jnp.sum(moved, axis=0, keepdims=True)
        dtotal = dtotal + passed * jnp.sum(s_state[b] * dstate, axis=0, keepdims=True)
        s_dtot[b : b + 1, :] += head_sums(dtotal, expand)
        s_ddt[r, :] += head_sums(du * xc[r], expand)
        dskip = dskip + jnp.sum(dy_b * xc[r], axis=0, keepdims=True)
        dxc = du * dt_e[r] + skip * dy_b
        s_pad[HALO + b * BLOCK : HALO + (b + 1) * BLOCK, :] = dxc * (
            sig[r] * (1.0 + pre[r] * (1.0 - sig[r]))
        )
        dstate = passed * dstate + tn(reads, faded)
    s_skip[0:1, :] += head_sums(dskip, expand)

    def put_main(values):
        dx_o[...] = values.astype(bf16)
        tail_o[...] = values[rows - HALO :]

    def put_halo(values):
        halo_o[...] = values

    conv_back(xraw, chan, s_pad, rows, 0, WIDTH, dchan_o, put_main, put_halo)

    @pl.when(group == GROUPS - 1)
    def _():
        keep = triangle()
        upper = (iota((BLOCK, BLOCK), 0) <= iota((BLOCK, BLOCK), 1)).astype(f32)
        rate = headp[1:2, :]
        bias_sum = jnp.zeros((1, LANES), f32)
        rate_sum = jnp.zeros((1, LANES), f32)
        for b in range(blocks):
            r = slice(b * BLOCK, (b + 1) * BLOCK)
            dscores = jnp.where(keep, s_dg[b], 0.0).astype(bf16)
            s_dc[r, :] += nn(dscores, s_b[r, :])
            s_db[r, :] += tn(dscores, s_c[r, :])
            da = nn(upper, s_dcum[r, :], full) + s_dtot[b : b + 1, :]
            ddt = s_ddt[r, :] + da * rate
            rate_sum = rate_sum + jnp.sum(da * (rate * s_dt[r, :]), axis=0, keepdims=True)
            raw = bcdt[HALO + b * BLOCK : HALO + (b + 1) * BLOCK, 2 * STATE :] + headp[0:1, :]
            ddt = ddt * sigmoid(raw)
            bias_sum = bias_sum + jnp.sum(ddt, axis=0, keepdims=True)
            dbc_o[r, 2 * STATE :] = ddt
        dheadp_o[...] = jnp.concatenate(
            [bias_sum, rate_sum, s_skip[0:1, :], jnp.zeros((5, LANES), f32)], axis=0
        )
        bc_pre = conv_rows(bcdt, bcv, rows, 0, 2 * STATE)
        bc_sig = sigmoid(bc_pre)
        turn = bc_sig * (1.0 + bc_pre * (1.0 - bc_sig))
        s_bcpad[HALO : HALO + rows, :STATE] = s_db[...] * turn[:, :STATE]
        s_bcpad[HALO : HALO + rows, STATE:] = s_dc[...] * turn[:, STATE:]

        def put_bc(values):
            dbc_o[:, : 2 * STATE] = values

        def put_bc_halo(values):
            dbch_o[...] = values

        conv_back(bcdt, bcv, s_bcpad, rows, 0, 2 * STATE, dbcv_o, put_bc, put_bc_halo)


def scan_back(xraw, dy, bcdt, st, dst, chan, headp, bcv):
    rows = dy.shape[0]
    ext = rows + HALO
    blocks = rows // BLOCK
    return call(
        back_kernel,
        (GROUPS,),
        [
            columns(ext),
            columns(rows),
            whole((ext, 384)),
            columns(STATE),
            columns(STATE),
            columns(8),
            whole((8, LANES)),
            whole((8, 2 * STATE)),
        ],
        [
            columns(rows),
            columns(HALO),
            columns(HALO),
            columns(8),
            whole((rows, 384)),
            whole((HALO, 2 * STATE)),
            whole((8, LANES)),
            whole((8, 2 * STATE)),
        ],
        [
            struct((rows, INNER), bf16),
            struct((HALO, INNER)),
            struct((HALO, INNER)),
            struct((8, INNER)),
            struct((rows, 384)),
            struct((HALO, 2 * STATE)),
            struct((8, LANES)),
            struct((8, 2 * STATE)),
        ],
        small_scratch(rows)
        + [
            pltpu.VMEM((rows, STATE), f32),
            pltpu.VMEM((rows, STATE), f32),
            pltpu.VMEM((rows, LANES), f32),
            pltpu.VMEM((rows, LANES), f32),
            pltpu.VMEM((8, LANES), f32),
            pltpu.VMEM((blocks, BLOCK, BLOCK), f32),
            pltpu.VMEM((8, LANES), f32),
            pltpu.VMEM((rows + 2 * HALO, WIDTH), f32),
            pltpu.VMEM((blocks, STATE, WIDTH), f32),
            pltpu.VMEM((rows + 2 * HALO, 2 * STATE), f32),
        ],
        flops=20 * rows * INNER * STATE,
        bytes_moved=12 * rows * INNER,
    )(xraw, dy, bcdt, st, dst, chan, headp, bcv)


SHARE = 3 * WIDTH + LANES


def grads_kernel(
    normed, dout, dgate, dx, tail, back, dbcdt, bc_back, scaled, w_zx, wb, resid, dresid, gain,
    packed_o, dres_o, dgain_o, s_bc, s_sum,
):
    rows = normed.shape[0]
    group = pl.program_id(0)
    edge = slice(rows - HALO, rows)

    @pl.when(group == 0)
    def _():
        s_bc[GROUPS - 1] = jnp.zeros((rows, LANES), bf16)
        for q in range(3):
            at = slice(q * LANES, (q + 1) * LANES)
            s_bc[q] = dbcdt[:, at].astype(bf16)
            if q < 2:
                s_bc[q, edge, :] = (dbcdt[edge, at] + bc_back[:, at]).astype(bf16)
        total = nt(s_bc[0], wb[:, :LANES])
        total = total + nt(s_bc[1], wb[:, LANES : 2 * LANES])
        s_sum[...] = total + nt(s_bc[2], wb[:, 2 * LANES :])

    fixed = (tail[...] + back[...]).astype(bf16)
    dzx = jnp.concatenate(
        [dgate[...], jnp.concatenate([dx[: rows - HALO, :], fixed], axis=0)], axis=1
    )
    s_sum[...] += nt(dzx, w_zx[...].reshape(D, 2 * WIDTH))
    packed_o[:, : 2 * WIDTH] = tn(normed[...], dzx).astype(bf16)
    packed_o[:, 2 * WIDTH : 3 * WIDTH] = tn(dout[...], scaled[...]).astype(bf16)
    packed_o[:, 3 * WIDTH :] = tn(normed[...], s_bc[group]).astype(bf16)

    @pl.when(group == GROUPS - 1)
    def _():
        values, grad, weight = resid[...], s_sum[...], gain[0:1, :]
        inverse = lax.rsqrt(jnp.mean(values * values, axis=1, keepdims=True) + norm_eps)
        along = jnp.mean(grad * weight * values, axis=1, keepdims=True)
        pulled = inverse * inverse * inverse * along
        dres_o[...] = dresid[...] + inverse * weight * grad - values * pulled
        dgain = jnp.sum(grad * values * inverse, axis=0, keepdims=True)
        dgain_o[...] = jnp.broadcast_to(dgain, dgain_o.shape)


def layer_grads(
    normed, dout, dgate, dx, tail, back, dbcdt, bc_back, scaled, packed, wb, resid, dresid, gain
):
    rows = normed.shape[0]
    return call(
        grads_kernel,
        (GROUPS,),
        [
            whole((rows, D)),
            whole((rows, D)),
            columns(rows),
            columns(rows),
            columns(HALO),
            columns(HALO),
            whole((rows, 384)),
            whole((HALO, 2 * STATE)),
            columns(rows),
            packed_zx(packed),
            whole(wb.shape),
            whole((rows, D)),
            whole((rows, D)),
            whole((8, D)),
        ],
        [columns(D, SHARE), whole((rows, D)), whole((8, D))],
        [struct((D, GROUPS * SHARE), bf16), struct((rows, D)), struct((8, D))],
        [pltpu.VMEM((GROUPS, rows, LANES), bf16), pltpu.VMEM((rows, D), f32)],
        flops=10 * rows * D * INNER,
        bytes_moved=26 * D * INNER,
    )(normed, dout, dgate, dx, tail, back, dbcdt, bc_back, scaled, packed, wb, resid, dresid, gain)


def lookup_kernel(keys, starts, table, out, s_rows):
    cls = pl.program_id(0)
    parts, lines, width = table.shape[1:]

    @pl.when(cls == 0)
    def _():
        s_rows[...] = jnp.zeros(s_rows.shape, f32)

    place = iota((16, width), 0)

    def turn(i, carry):
        key = keys[i]
        at = key & (PAST - 1)
        line = (key >> 11) - cls * lines
        base = pl.multiple_of((line >> 4) << 4, 16)
        found = []
        for part in range(parts):
            tile = table[0, part, pl.ds(base, 16), :].astype(f32)
            found.append(
                jnp.sum(jnp.where(place == (line & 15), tile, 0.0), axis=0, keepdims=True)
            )
        s_rows[pl.ds(at, 1), :] = jnp.concatenate(found, axis=1)
        return carry

    lax.fori_loop(starts[cls], starts[cls + 1], turn, 0)

    @pl.when(cls == CLASSES - 1)
    def _():
        out[...] = s_rows[...].astype(bf16)


def lookup(keys, starts, table):
    count = keys.shape[0]
    return call(
        lookup_kernel,
        (CLASSES,),
        [pl.BlockSpec((1,) + table.shape[1:], lambda c, *_: (c, 0, 0, 0))],
        whole((count, D)),
        struct((count, D), bf16),
        [pltpu.VMEM((count, D), f32)],
        prefetch=2,
        bytes_moved=2 * table.size,
    )(keys, starts, table)


def scatter_kernel(keys, starts, table, rows, out, s_rows, s_sum):
    cls = pl.program_id(0)
    piece = pl.program_id(1)
    parts, lines, width = table.shape[1:]

    @pl.when((cls == 0) & (piece == 0))
    def _():
        wide = rows[...].astype(f32)
        for p in range(s_rows.shape[0]):
            s_rows[p] = wide[:, p * WIDTH : (p + 1) * WIDTH]

    for part in range(parts):
        s_sum[:, part * width : (part + 1) * width] = table[0, part].astype(f32)

    def turn(i, carry):
        key = keys[i]
        at = key & (PAST - 1)
        line = (key >> 11) - cls * lines
        s_sum[pl.ds(line, 1), :] += s_rows[piece, pl.ds(at, 1), :]
        return carry

    lax.fori_loop(starts[cls], starts[cls + 1], turn, 0)
    for part in range(parts):
        out[0, part] = s_sum[:, part * width : (part + 1) * width].astype(bf16)


def scatter(keys, starts, table, rows):
    count = keys.shape[0]
    lines, width = table.shape[2:]
    spec = pl.BlockSpec((1, WIDTH // width, lines, width), lambda c, p, *_: (c, p, 0, 0))
    return call(
        scatter_kernel,
        (CLASSES, D // WIDTH),
        [spec, whole((count, D))],
        spec,
        struct(table.shape, bf16),
        [pltpu.VMEM((D // WIDTH, count, WIDTH), f32), pltpu.VMEM((lines, WIDTH), f32)],
        prefetch=2,
        bytes_moved=4 * table.size,
    )(keys, starts, table, rows)


def tile_logits(table, chosen, real):
    parts, height, width = table.shape[1:]
    result = nt(table[0, 0], chosen[:, :width])
    for part in range(1, parts):
        result = result + nt(table[0, part], chosen[:, part * width : (part + 1) * width])
    line = pl.program_id(1) * height + iota(result.shape, 0)
    return jnp.where(line < real, result, -1e30)


def tile_hit(table, lines, wanted):
    height = table.shape[2]
    first = pl.program_id(0) * lines + pl.program_id(1) * height
    return first + iota((height, wanted.shape[1]), 0) == wanted[0:1, :]


def measure_kernel(real, lines, table, chosen, wanted, out, s_stats):
    logits = tile_logits(table, chosen, real)
    hit = tile_hit(table, lines, wanted)
    first = (pl.program_id(0) == 0) & (pl.program_id(1) == 0)

    @pl.when(first)
    def _():
        s_stats[0:1, :] = jnp.full((1, s_stats.shape[1]), -1e30, f32)
        s_stats[1:8, :] = jnp.zeros((7, s_stats.shape[1]), f32)

    old = s_stats[0:1, :]
    top = jnp.maximum(old, jnp.max(logits, axis=0, keepdims=True))
    total = s_stats[1:2, :] * jnp.exp(old - top)
    s_stats[1:2, :] = total + jnp.sum(jnp.exp(logits - top), axis=0, keepdims=True)
    s_stats[2:3, :] += jnp.sum(jnp.where(hit, logits, 0.0), axis=0, keepdims=True)
    s_stats[0:1, :] = top
    out[...] = s_stats[...]


def table_spec(table):
    parts, width = table.shape[1], table.shape[3]
    return pl.BlockSpec((1, parts, TILE, width), lambda c, i: (c, 0, i, 0))


def vocab_measure(table, chosen, wanted, real):
    count = chosen.shape[0]
    lines = table.shape[2]
    return call(
        functools.partial(measure_kernel, real, lines),
        (CLASSES, lines // TILE),
        [table_spec(table), whole((count, D)), whole((8, count))],
        whole((8, count)),
        struct((8, count)),
        [pltpu.VMEM((8, count), f32)],
        flops=2 * count * table.size,
        bytes_moved=2 * table.size,
    )(table, chosen, wanted)


def vocab_kernel(real, lines, table, chosen, wanted, stats, dtable, dchosen, s_sum):
    logits = tile_logits(table, chosen, real)
    hit = tile_hit(table, lines, wanted)
    soft = jnp.exp(logits - stats[0:1, :])
    dlogits = (stats[1:2, :] * (soft - jnp.where(hit, 1.0, 0.0))).astype(bf16)
    step = pl.program_id(0) * pl.num_programs(1) + pl.program_id(1)
    parts, width = table.shape[1], table.shape[3]

    @pl.when(step == 0)
    def _():
        s_sum[...] = jnp.zeros(s_sum.shape, f32)

    for part in range(parts):
        at = slice(part * width, (part + 1) * width)
        dtable[0, part] = nn(dlogits, chosen[:, at]).astype(bf16)
        s_sum[:, at] += tn(dlogits, table[0, part])

    @pl.when(step == CLASSES * pl.num_programs(1) - 1)
    def _():
        dchosen[...] = s_sum[...].astype(bf16)


def vocab_back(table, chosen, wanted, stats, real):
    count = chosen.shape[0]
    lines = table.shape[2]
    return call(
        functools.partial(vocab_kernel, real, lines),
        (CLASSES, lines // TILE),
        [table_spec(table), whole((count, D)), whole((8, count)), whole((8, count))],
        [table_spec(table), whole((count, D))],
        [struct(table.shape, bf16), struct((count, D), bf16)],
        [pltpu.VMEM((count, D), f32)],
        flops=6 * count * table.size,
        bytes_moved=4 * table.size,
    )(table, chosen, wanted, stats)


def shifted(values, axis, by):
    n = lax.axis_size(axis)
    return lax.ppermute(values, axis, [(i, (i + by) % n) for i in range(n)])


def swapped(values):
    return lax.ppermute(values, "core", [(0, 1), (1, 0)])


def to_later(values):
    return lax.ppermute(values, "core", [(0, 1)])


def to_earlier(values):
    return lax.ppermute(values, "core", [(1, 0)])


def everywhere(values, axes, combine=jnp.add):
    for axis in axes:
        reach = 1
        while reach < lax.axis_size(axis):
            n = lax.axis_size(axis)
            other = lax.ppermute(values, axis, [(i, i ^ reach) for i in range(n)])
            values = combine(values, other)
            reach *= 2
    return values


def around(values, axis):
    n = lax.axis_size(axis)
    return jnp.stack([values] + [shifted(values, axis, by) for by in range(1, n)])


def sum_back(blocks, axis):
    n = lax.axis_size(axis)
    result = blocks[0].astype(f32)
    for by in range(1, n):
        result = result + shifted(blocks[by], axis, -by).astype(f32)
    return result


def inverse_rms(values):
    return lax.rsqrt(jnp.mean(values * values, axis=-1, keepdims=True) + norm_eps)


def rms_back(grad, values, gain):
    inverse = inverse_rms(values)
    along = jnp.mean(grad * gain * values, axis=-1, keepdims=True)
    dvalues = inverse * gain * grad - values * (inverse * inverse * inverse * along)
    return (dvalues, jnp.sum(grad * values * inverse, axis=0))


def in_order(blocks, axis):
    n = blocks.shape[axis]
    z = lax.axis_index("tensor")
    taken = [lax.dynamic_index_in_dim(blocks, (z - q) % n, axis, False) for q in range(n)]
    return jnp.stack(taken, axis=axis)


def turn_heads(bcdt):
    rows = bcdt.shape[0]
    steps = bcdt[:, 2 * STATE : 2 * STATE + HEADS].reshape(rows, GROUPS, -1)
    steps = in_order(steps, 1).reshape(rows, HEADS)
    return jnp.concatenate([bcdt[:, : 2 * STATE], steps, bcdt[:, 2 * STATE + HEADS :]], axis=1)


def pack_layer(w_zx, w_bcdt, w_out):
    rows = w_zx.shape[0]
    zx = w_zx.reshape(rows, -1)
    out = jnp.concatenate([w_out[: rows // 2], w_out[rows // 2 :]], axis=1)
    own = jnp.concatenate([zx, out], axis=0).astype(bf16)
    blocks = around(own, "tensor")
    zx = blocks[:, :rows].reshape(-1, D)
    out = blocks[:, rows:].reshape(-1, D)
    lines = -(-rows // 48) * 16
    bcdt = jnp.pad(w_bcdt.astype(bf16), ((0, 3 * lines - rows), (0, LANES - HEADS)))
    bcdt = jnp.pad(bcdt[:, : 2 * STATE + HEADS].reshape(3, lines, -1), ((0, 0), (0, 0), (0, 32)))
    bcdt = jnp.concatenate([bcdt[0], bcdt[1], bcdt[2]], axis=1)
    bcdt = jnp.pad(bcdt, ((0, 0), (0, D - bcdt.shape[1])))
    return jnp.concatenate([zx, out, bcdt], axis=0)


def unpack_bcdt(packed):
    rows = D // packed.shape[0]
    lines = -(-rows // 48) * 16
    width = 2 * STATE + HEADS + 32
    part = packed[:, GROUPS * (rows + rows // 2) :]
    part = jnp.concatenate([part[:, :, i * width : (i + 1) * width] for i in range(3)], axis=1)
    part = part[:, :rows].reshape(D, width)
    return turn_heads(jnp.pad(part, ((0, 0), (0, 2 * STATE + LANES - width))))


def reduce_layer(packed):
    n_tensor = lax.axis_size("tensor")
    mine = lax.psum_scatter(packed, DP, scatter_dimension=0, tiled=True)
    shares = [mine[:, j * SHARE : (j + 1) * SHARE] for j in range(n_tensor)]
    bcdt = turn_heads(jnp.concatenate([share[:, 3 * WIDTH :] for share in shares[:3]], axis=1))
    blocks = []
    for by in range(n_tensor):
        block = jnp.concatenate([shares[-by][:, : 3 * WIDTH], bcdt], axis=1)
        blocks.append(block if by == 0 else shifted(block, "tensor", by))
    blocks = [block.astype(f32) for block in blocks]
    even = functools.reduce(jnp.add, blocks[0::2])
    odd = functools.reduce(jnp.add, blocks[1::2])
    total = even + odd
    return (
        total[:, : 2 * WIDTH].reshape(-1, 2, WIDTH),
        total[:, 2 * WIDTH : 3 * WIDTH],
        total[:, 3 * WIDTH : 3 * WIDTH + 2 * STATE + HEADS],
    )


def layer_forward(resid, gain, packed, wb, smalls):
    chan, headp, bcv = smalls
    normed = (resid * inverse_rms(resid) * gain).astype(bf16)
    nx = jnp.concatenate([to_later(normed[-HALO:]), normed], axis=0)
    y, gate, xraw, st, bcdt, c, ecf = scan_front(nx, packed, wb, chan, headp, bcv)
    before = to_later(st)
    y, scaled, inverse, out = scan_join(y, gate, c, ecf, before, chan, packed, resid)
    return out, (resid, normed, y, gate, xraw, before, bcdt, c, ecf, scaled, inverse)


def layer_backward(dresid, kept, gain, packed, wb, smalls):
    resid, normed, y, gate, xraw, before, bcdt, c, ecf, scaled, inverse = kept
    chan, headp, bcv = smalls
    dout = dresid.astype(bf16)
    dy, dgate, dgain, dstart = scan_unjoin(dout, packed, y, gate, inverse, c, ecf, chan)
    after = to_earlier(dstart)
    dx, tail, halo, dchan, dbcdt, bc_halo, dheadp, dbcv = scan_back(
        xraw, dy, bcdt, before, after, chan, headp, bcv
    )
    back, bc_back = to_earlier(halo), to_earlier(bc_halo)
    gain_rows = jnp.broadcast_to(gain[None, :], (8, D))
    grads, dresid, dnorm_gain = layer_grads(
        normed, dout, dgate, dx, tail, back, dbcdt, bc_back,
        scaled, packed, wb, resid, dresid, gain_rows,
    )
    dchan = jnp.concatenate([dchan[: CONV + 1], dgain[:1]], axis=0)
    smalls = (dnorm_gain[0], dchan, dheadp[:3, :HEADS], dbcv[: CONV + 1])
    return dresid, reduce_layer(grads), smalls


def lse_merge(first, second):
    top = jnp.maximum(first[0], second[0])
    total = first[1] * jnp.exp(first[0] - top) + second[1] * jnp.exp(second[0] - top)
    return jnp.stack([top, total, first[2] + second[2]])


def adapt(weight, first, second, grad):
    first_new = first_decay * first + (1.0 - first_decay) * grad
    second_new = second_decay * second + (1.0 - second_decay) * grad * grad
    update = (
        first_new
        / (1.0 - first_decay**STEP)
        / (jnp.sqrt(second_new / (1.0 - second_decay**STEP)) + adam_eps)
        + weight_decay * weight
    )
    return (first_new, second_new, update)


def group_squares(values, stacked):
    if stacked:
        return jnp.sum(values * values, axis=tuple(range(1, values.ndim)))
    return jnp.sum(values * values)[None]


def body(
    token_ids, lengths, loss_pos, targets,
    embed, embed_m, embed_v,
    w_zx, w_zx_m, w_zx_v,
    w_bcdt, w_bcdt_m, w_bcdt_v,
    w_out, w_out_m, w_out_v,
    channel, channel_m, channel_v,
    per_head, per_head_m, per_head_v,
    bc_conv, bc_conv_m, bc_conv_v,
    gains, gains_m, gains_v,
):
    n_tensor = lax.axis_size("tensor")
    n_data = lax.axis_size("chip") * lax.axis_size("core")
    core = lax.axis_index("core")
    z = lax.axis_index("tensor")
    seq = token_ids.shape[1]
    rows = seq // 2
    scored = loss_pos.shape[1]
    half = scored // 2
    lines = embed.shape[0]
    padded = -(-lines // TILE) * TILE
    vocab = lines * CLASSES

    own_meta = jnp.concatenate([token_ids, loss_pos, targets, lengths], axis=1)
    other_meta = swapped(own_meta)
    meta = jnp.where(
        core == 0,
        jnp.stack([own_meta, other_meta], axis=1),
        jnp.stack([other_meta, own_meta], axis=1),
    ).reshape(n_tensor, -1)
    meta = jnp.stack(
        [
            lax.dynamic_index_in_dim(meta, (z - j) % n_tensor, 0, keepdims=False)
            for j in range(n_tensor)
        ]
    )
    ids = lax.dynamic_slice_in_dim(meta, core * rows, rows, 1)
    length = meta[:, seq + 2 * scored :]
    live = core * rows + jnp.arange(rows)[None, :] < length
    positions = lax.dynamic_slice_in_dim(meta, seq + core * half, half, 1)
    wanted = lax.dynamic_slice_in_dim(meta, seq + scored + core * half, half, 1)
    own_positions = meta[0, seq : seq + scored]

    def place(indices):
        local = indices - z * vocab
        return (local & 3) * padded + (local >> 2), (local >= 0) & (local < vocab)

    key, inside = place(ids)
    count = n_tensor * rows
    key = jnp.where(inside & live, key, CLASSES * padded).reshape(count)
    key = key * PAST + jnp.arange(count)
    rank = jnp.sum((key[None, :] < key[:, None]).astype(jnp.int32), axis=1)
    keys = jnp.sum(jnp.where(rank[None, :] == jnp.arange(count)[:, None], key[None, :], 0), axis=1)
    edges = jnp.arange(8) * (padded * PAST)
    starts = jnp.sum((key[None, :] < edges[:, None]).astype(jnp.int32), axis=1)

    low = jnp.pad(embed.astype(bf16), ((0, padded - lines), (0, 0)))
    table = lax.all_gather(low, DP).reshape(CLASSES, n_data // CLASSES, padded, -1)
    shares = [pack_layer(w_zx[i], w_bcdt[i], w_out[i]) for i in range(LAYERS)]
    packed = [lax.all_gather(share, DP) for share in shares]
    inner = INNER // n_tensor
    heads = HEADS // n_tensor
    small = jnp.concatenate([channel, jnp.pad(per_head, ((0, 0), (0, 0), (0, inner - heads)))], 1)
    small = around(small, "tensor")
    channel_all = small[:, :, : CONV + 2].transpose(1, 2, 0, 3).reshape(LAYERS, CONV + 2, INNER)
    head_all = small[:, :, CONV + 2 :, :heads].transpose(1, 2, 0, 3).reshape(LAYERS, 3, HEADS)
    smalls = []
    for depth in range(LAYERS):
        headp = jnp.stack([head_all[depth, 0], -jnp.exp(head_all[depth, 1]), head_all[depth, 2]])
        smalls.append(
            (
                jnp.pad(channel_all[depth], ((0, 2), (0, 0))),
                jnp.pad(headp, ((0, 5), (0, LANES - HEADS))),
                jnp.pad(bc_conv[depth], ((0, 3), (0, 0))),
            )
        )

    found = lookup(keys, starts, table)
    resid = sum_back(found.reshape(n_tensor, rows, D), "tensor")
    w_small = [unpack_bcdt(packed[depth]) for depth in range(LAYERS)]
    kept = []
    for depth in range(LAYERS):
        resid, saved = layer_forward(
            resid, gains[depth], packed[depth], w_small[depth], smalls[depth]
        )
        kept.append(saved)

    final = (resid * inverse_rms(resid) * gains[LAYERS]).astype(bf16)
    other = swapped(final)
    both = jnp.concatenate(
        [jnp.where(core == 0, final, other), jnp.where(core == 0, other, final)], axis=0
    )
    pick = (positions[0][:, None] == jnp.arange(seq)[None, :]).astype(bf16)
    chosen = around(nn(pick, both).astype(bf16), "tensor").reshape(n_tensor * half, D)
    want, known = place(wanted)
    want = jnp.where(known, want, -1).reshape(1, -1)
    want = jnp.broadcast_to(want, (8, n_tensor * half))
    stats = vocab_measure(table, chosen, want, lines)[:3]
    stats = stats.reshape(3, n_tensor, half)

    ordered = everywhere(in_order(stats, 1), ("tensor",), lse_merge)
    stats = in_order(ordered, 1).reshape(3, -1)
    log_total = stats[0] + jnp.log(stats[1])
    counted = (positions < length).astype(f32).reshape(-1)
    losses = (counted * (log_total - stats[2])).reshape(n_tensor, half).sum(axis=1)
    loss_sum = jnp.sum(in_order(losses, 0))
    loss_count = jnp.sum(counted)
    info = jnp.pad(jnp.stack([log_total, counted]), ((0, 6), (0, 0)))
    dtable, dchosen = vocab_back(table, chosen, want, info, lines)
    dpicked = sum_back(dchosen.reshape(n_tensor, half, D), "tensor").astype(bf16)
    other = swapped(dpicked)
    dpicked = jnp.concatenate(
        [jnp.where(core == 0, dpicked, other), jnp.where(core == 0, other, dpicked)], axis=0
    )
    spots = (core * rows + jnp.arange(rows)[:, None] == own_positions[None, :]).astype(bf16)
    dresid, dfinal_gain = rms_back(nn(spots, dpicked), resid, gains[LAYERS])

    grads = [None] * LAYERS
    small_grads = [None] * LAYERS
    for depth in reversed(range(LAYERS)):
        dresid, grads[depth], small_grads[depth] = layer_backward(
            dresid, kept[depth], gains[depth], packed[depth], w_small[depth], smalls[depth]
        )

    arrived = around(dresid.astype(bf16), "tensor").reshape(count, D)
    dtable = scatter(keys, starts, dtable, arrived)
    dtable = dtable.reshape(n_data, padded, -1)
    grad_table = lax.psum_scatter(dtable, DP, scatter_dimension=0)[:lines].astype(f32)

    grad_zx, grad_out, grad_bcdt = (jnp.stack(parts) for parts in zip(*grads))
    grad_gains = jnp.stack([small_grads[depth][0] for depth in range(LAYERS)] + [dfinal_gain])
    grad_channel = jnp.stack([part[1] for part in small_grads])
    grad_channel = in_order(grad_channel.reshape(LAYERS, CONV + 2, n_tensor, inner), 2)
    grad_channel = grad_channel.reshape(LAYERS, CONV + 2, INNER)
    grad_head = jnp.stack([part[2] for part in small_grads])
    grad_head = in_order(grad_head.reshape(LAYERS, 3, n_tensor, heads), 2)
    grad_bc_conv = jnp.stack([part[3] for part in small_grads])
    flat = jnp.concatenate(
        [
            grad_gains.reshape(-1, LANES),
            grad_channel.reshape(-1, LANES),
            grad_bc_conv.reshape(-1, LANES),
            jnp.pad(grad_head.reshape(LAYERS * 3, HEADS), ((0, 0), (0, LANES - HEADS))),
        ]
    )
    flat = everywhere(flat, ("core", "tensor", "chip"))
    sizes = [grad.size // LANES for grad in (grad_gains, grad_channel, grad_bc_conv)]
    edges = [sizes[0], sizes[0] + sizes[1], sum(sizes)]
    grad_gains = flat[: edges[0]].reshape(grad_gains.shape)
    grad_channel = flat[edges[0] : edges[1]].reshape(grad_channel.shape)
    grad_bc_conv = flat[edges[1] : edges[2]].reshape(grad_bc_conv.shape)
    grad_head = flat[edges[2] :, :HEADS].reshape(LAYERS, 3, HEADS)
    grad_channel = lax.dynamic_slice_in_dim(grad_channel, z * inner, inner, 2)
    grad_head = lax.dynamic_slice_in_dim(grad_head, z * heads, heads, 2)

    everyone = n_tensor * n_data
    kinds = (
        (embed, embed_m, embed_v, grad_table, False, 1),
        (w_zx, w_zx_m, w_zx_v, grad_zx, True, 1),
        (w_bcdt, w_bcdt_m, w_bcdt_v, grad_bcdt, True, n_tensor),
        (w_out, w_out_m, w_out_v, grad_out, True, 1),
        (channel, channel_m, channel_v, grad_channel, True, n_data),
        (per_head, per_head_m, per_head_v, grad_head, True, n_data),
        (bc_conv, bc_conv_m, bc_conv_v, grad_bc_conv, True, everyone),
        (gains, gains_m, gains_v, grad_gains, False, everyone),
    )
    grad_sq = jnp.concatenate([group_squares(kind[3], kind[4]) / kind[5] for kind in kinds])
    weight_sq = jnp.concatenate([group_squares(kind[0], kind[4]) / kind[5] for kind in kinds])
    groups = grad_sq.shape[0]
    totals = jnp.concatenate(
        [grad_sq, weight_sq, jnp.stack([loss_sum, loss_count]) / n_tensor]
    )
    totals = everywhere(jnp.pad(totals, (0, LANES - totals.shape[0])), ("core", "tensor", "chip"))
    grad_sq, weight_sq = totals[:groups], totals[groups : 2 * groups]
    grad_norm = jnp.sqrt(jnp.sum(grad_sq))
    scale = jnp.minimum(1.0, clip_limit / grad_norm)
    moved = [adapt(kind[0], kind[1], kind[2], kind[3] * scale) for kind in kinds]
    step_sq = jnp.concatenate(
        [group_squares(change[2], kind[4]) / kind[5] for change, kind in zip(moved, kinds)]
    )
    step_sq = everywhere(jnp.pad(step_sq, (0, LANES - groups)), ("core", "tensor", "chip"))[:groups]
    weight_norm = jnp.sqrt(weight_sq)
    step_norm = jnp.sqrt(step_sq)
    trust_all = weight_norm / step_norm
    results = []
    offset = 0
    for kind, change in zip(kinds, moved):
        weight = kind[0]
        if kind[4]:
            factor = trust_all[offset : offset + weight.shape[0]].reshape(
                (weight.shape[0],) + (1,) * (weight.ndim - 1)
            )
            offset = offset + weight.shape[0]
        else:
            factor = trust_all[offset]
            offset = offset + 1
        results += [weight - learn_rate * factor * change[2], change[0], change[1]]
    group_norms = jnp.stack([weight_norm, step_norm])
    return (totals[2 * groups], totals[2 * groups + 1], grad_norm, group_norms, *results)


def solution(mesh):
    devices = mesh.devices.reshape(-1, 2, mesh.shape["tensor"])
    inside = Mesh(devices, ("chip", "core", "tensor"))
    by_data = P(None, DP)
    embed = (P("tensor", DP),) * 3
    w_zx = (P(None, DP, None, "tensor"),) * 3
    w_bcdt = (P(None, DP, None),) * 3
    w_out = (P(None, DP, "tensor"),) * 3
    by_tensor = (P(None, None, "tensor"),) * 6
    copied = (P(),) * 6
    states = embed + w_zx + w_bcdt + w_out + by_tensor + copied
    return jax.shard_map(
        body,
        mesh=inside,
        in_specs=(by_data,) * 4 + states,
        out_specs=(P(),) * 4 + states,
        check_vma=False,
    )
```

```python
import functools

import jax
import jax.numpy as jnp
from jax import lax
from jax.experimental import pallas as pl
from jax.experimental.pallas import tpu as pltpu
from jax.sharding import Mesh
from jax.sharding import PartitionSpec as P

D = 1024
INNER = 2048
HEADS = 32
HDIM = 64
STATE = 128
CONV = 4
LAYERS = 2
MICRO = 2
STEP = 5

BLOCK = 128
HALO = 16
WIDTH = 512
GROUPS = INNER // WIDTH
LANES = 128
TILE = 800
CLASSES = 4
PAST = 1 << 11
CAP = 128

norm_eps = 1e-05
adam_eps = 1e-06
clip_limit = 1.0
first_decay = 0.5
second_decay = 0.5
learn_rate = 0.3
weight_decay = 0.01

f32 = jnp.float32
bf16 = jnp.bfloat16
full = lax.Precision.HIGHEST
DP = ("chip", "core")
VMEM_BYTES = 58 * 1024 * 1024


def dot(left, right, left_dim, right_dim, precision=None):
    return lax.dot_general(
        left,
        right,
        (((left_dim,), (right_dim,)), ((), ())),
        precision=precision,
        preferred_element_type=f32,
    )


def nn(left, right, precision=None):
    return dot(left, right, 1, 0, precision)


def nt(left, right, precision=None):
    return dot(left, right, 1, 1, precision)


def tn(left, right, precision=None):
    return dot(left, right, 0, 0, precision)


def sigmoid(v):
    return 1.0 / (1.0 + jnp.exp(-v))


def softplus(v):
    return jnp.maximum(v, 0.0) + jnp.log1p(jnp.exp(-jnp.abs(v)))


def normed(values, gain):
    inverse = lax.rsqrt(jnp.mean(values * values, axis=1, keepdims=True) + norm_eps)
    return (values * inverse * gain).astype(bf16)


def iota(shape, axis):
    return lax.broadcasted_iota(jnp.int32, shape, axis)


def call(kernel, grid, in_specs, out_specs, out_shape, scratch, prefetch=0, flops=0, bytes_moved=0):
    return pl.pallas_call(
        kernel,
        grid_spec=pltpu.PrefetchScalarGridSpec(
            num_scalar_prefetch=prefetch,
            grid=grid,
            in_specs=in_specs,
            out_specs=out_specs,
            scratch_shapes=scratch,
        ),
        out_shape=out_shape,
        compiler_params=pltpu.CompilerParams(
            vmem_limit_bytes=VMEM_BYTES, dimension_semantics=("arbitrary",) * len(grid)
        ),
        cost_estimate=pl.CostEstimate(
            flops=flops, bytes_accessed=bytes_moved, transcendentals=0
        ),
    )


def whole(shape):
    return pl.BlockSpec(shape, lambda *_: (0,) * len(shape))


def packed_zx(packed):
    rows = D // packed.shape[0]
    return pl.BlockSpec((packed.shape[0], rows, D), lambda g: (0, g, 0))


def unpacked_out(ref, low, rows):
    lines = ref[:, low : low + rows // 2, :]
    both = jnp.concatenate([lines[:, :, :WIDTH], lines[:, :, WIDTH:]], axis=1)
    return both.reshape(D, WIDTH)


def columns(rows, width=WIDTH, at=0):
    return pl.BlockSpec((rows, width), lambda g: (0, g + at))


def struct(shape, dtype=f32):
    return jax.ShapeDtypeStruct(shape, dtype)


def conv_rows(ref, taps, rows, low, width):
    result = taps[CONV : CONV + 1, :]
    for j in range(CONV):
        start = HALO - CONV + 1 + j
        result = result + ref[start : start + rows, low : low + width] * taps[j : j + 1, :]
    return result


def triangle():
    return iota((BLOCK, BLOCK), 0) >= iota((BLOCK, BLOCK), 1)


def expanded(values, marks, parts=3, by=nn):
    result = None
    for _ in range(parts):
        part = values.astype(bf16)
        values = values - part.astype(f32)
        term = by(part, marks)
        result = term if result is None else result + term
    return result


def spread(group):
    head = iota((LANES, WIDTH), 0)
    lane = iota((LANES, WIDTH), 1)
    return (head == group * (WIDTH // HDIM) + lane // HDIM).astype(bf16)


def small_parts(rows, bcdt, headp, bcv, s_b, s_c, s_dt, s_cum, s_cumt, s_g):
    pre = conv_rows(bcdt, bcv, rows, 0, 2 * STATE)
    bc = (pre * sigmoid(pre)).astype(bf16)
    s_b[...] = bc[:, :STATE]
    s_c[...] = bc[:, STATE:]
    dt = softplus(bcdt[HALO:, 2 * STATE :] + headp[0:1, :])
    s_dt[...] = dt
    decay = headp[1:2, :] * dt
    keep = triangle()
    lower = keep.astype(f32)
    for b in range(rows // BLOCK):
        r = slice(b * BLOCK, (b + 1) * BLOCK)
        cum = nn(lower, decay[r], full)
        s_cum[r, :] = cum
        s_cumt[:, r] = cum.T
        s_g[b] = jnp.where(keep, nt(bc[r, STATE:], bc[r, :STATE]), 0.0)


def head_rows(s_cumt, group, r):
    heads = WIDTH // HDIM
    return s_cumt[pl.ds(pl.multiple_of(group * heads, heads), heads), r]


def fading(cum_e, cum_rows, head):
    column = cum_e[:, head * HDIM : head * HDIM + 1]
    return jnp.exp(jnp.minimum(column - cum_rows[head : head + 1, :], 0.0))


def one_head(values, j):
    first = iota(values.shape, 1) < HDIM
    return jnp.where(first if j == 0 else jnp.logical_not(first), values, 0.0).astype(bf16)


def small_scratch(rows):
    return [
        pltpu.VMEM((rows, STATE), bf16),
        pltpu.VMEM((rows, STATE), bf16),
        pltpu.VMEM((rows, LANES), f32),
        pltpu.VMEM((rows, LANES), f32),
        pltpu.VMEM((LANES, rows), f32),
        pltpu.VMEM((rows // BLOCK, BLOCK, BLOCK), f32),
    ]


def scan_kernel(
    nx, w_zx, wb, chan, headp, bcv,
    y_o, gate_o, xraw_o, st_o, bcdt_o, c_o, ecf_o,
    s_b, s_c, s_dt, s_cum, s_cumt, s_g,
):
    rows = y_o.shape[0]
    group = pl.program_id(0)

    @pl.when(group == 0)
    def _():
        bcdt_o[...] = nn(nx[...], wb[...])
        small_parts(rows, bcdt_o, headp, bcv, s_b, s_c, s_dt, s_cum, s_cumt, s_g)
        c_o[...] = s_c[...]
        run = jnp.zeros((1, LANES), f32)
        for b in range(rows // BLOCK):
            r = slice(b * BLOCK, (b + 1) * BLOCK)
            ecf_o[r, :] = jnp.exp(s_cum[r, :] + run)
            run = run + s_cum[(b + 1) * BLOCK - 1 : (b + 1) * BLOCK, :]

    both = w_zx[...].reshape(D, 2 * WIDTH)
    gate_o[...] = nn(nx[HALO:, :], both[:, :WIDTH])
    xraw_o[...] = nn(nx[...], both[:, WIDTH:])
    pre = conv_rows(xraw_o, chan, rows, 0, WIDTH)
    xc = pre * sigmoid(pre)
    expand = spread(group)
    u = xc * expanded(s_dt[...], expand)
    skip = expanded(headp[...], expand)[2:3, :]
    state = jnp.zeros((STATE, WIDTH), f32)
    for b in range(rows // BLOCK):
        r = slice(b * BLOCK, (b + 1) * BLOCK)
        cum_e = expanded(s_cum[r, :], expand)
        total = cum_e[BLOCK - 1 : BLOCK, :]
        keys, reads = s_b[r, :], s_c[r, :]
        y = jnp.exp(cum_e) * nn(reads, state.astype(bf16)) + skip * xc[r]
        cum_rows = head_rows(s_cumt, group, r)
        pieces = []
        for pair in range(WIDTH // LANES):
            both = u[r, pair * LANES : (pair + 1) * LANES]
            piece = jnp.zeros((BLOCK, LANES), f32)
            for j in range(2):
                weights = (fading(cum_e, cum_rows, 2 * pair + j) * s_g[b]).astype(bf16)
                piece = piece + nn(weights, one_head(both, j))
            pieces.append(piece)
        y_o[r, :] = y + jnp.concatenate(pieces, axis=1)
        fresh = tn(keys, (u[r] * jnp.exp(total - cum_e)).astype(bf16))
        state = state * jnp.exp(total) + fresh
    st_o[...] = state


def scan_front(nx, packed, wb, chan, headp, bcv):
    ext = nx.shape[0]
    rows = ext - HALO
    return call(
        scan_kernel,
        (GROUPS,),
        [
            whole((ext, D)),
            packed_zx(packed),
            whole(wb.shape),
            columns(8),
            whole((8, LANES)),
            whole((8, 2 * STATE)),
        ],
        [
            columns(rows),
            columns(rows),
            columns(ext),
            columns(STATE),
            whole((ext, 384)),
            whole((rows, STATE)),
            whole((rows, LANES)),
        ],
        [
            struct((rows, INNER)),
            struct((rows, INNER)),
            struct((ext, INNER)),
            struct((STATE, INNER)),
            struct((ext, 384)),
            struct((rows, STATE), bf16),
            struct((rows, LANES)),
        ],
        small_scratch(rows),
        flops=2 * ext * D * 2 * INNER,
        bytes_moved=2 * D * 2 * INNER + 12 * rows * INNER,
    )(nx, packed, wb, chan, headp, bcv)


def join_kernel(
    y, gate, c, ecf, st, chan, wout, resid, gain,
    yf_o, scaled_o, inv_o, res_o, normed_o, s_gated, s_square,
):
    group = pl.program_id(0)
    ecf_e = expanded(ecf[...], spread(group))
    yf = y[...] + ecf_e * nn(c[...], st[...].astype(bf16))
    yf_o[...] = yf
    gated = yf * (gate[...] * sigmoid(gate[...]))
    s_gated[group] = gated
    part = jnp.broadcast_to(jnp.sum(gated * gated, axis=1, keepdims=True), s_square.shape)

    @pl.when(group == 0)
    def _():
        s_square[...] = part

    @pl.when(group > 0)
    def _():
        s_square[...] += part

    @pl.when(group == GROUPS - 1)
    def _():
        inverse = lax.rsqrt(s_square[...] / INNER + norm_eps)
        inv_o[...] = inverse
        res = resid[...]
        for q in range(GROUPS):
            at = slice(q * WIDTH, (q + 1) * WIDTH)
            scaled = (s_gated[q] * inverse[:, :1] * chan[CONV + 1 : CONV + 2, at]).astype(bf16)
            scaled_o[:, at] = scaled
            height = D // wout.shape[0]
            res = res + nt(scaled, unpacked_out(wout, q * height // 2, height))
        res_o[...] = res
        normed_o[...] = normed(res, gain[0:1, :])


def scan_join(y, gate, c, ecf, st, chan, packed, resid, gain):
    rows = y.shape[0]
    height = D // packed.shape[0]
    return call(
        join_kernel,
        (GROUPS,),
        [
            columns(rows),
            columns(rows),
            whole((rows, STATE)),
            whole((rows, LANES)),
            columns(STATE),
            whole((8, INNER)),
            pl.BlockSpec((packed.shape[0], 2 * height, D), lambda g: (0, 2, 0)),
            whole((rows, D)),
            whole((8, D)),
        ],
        [columns(rows), whole((rows, INNER)), whole((rows, LANES))] + [whole((rows, D))] * 2,
        [
            struct((rows, INNER)),
            struct((rows, INNER), bf16),
            struct((rows, LANES)),
            struct((rows, D)),
            struct((rows, D), bf16),
        ],
        [pltpu.VMEM((GROUPS, rows, WIDTH), f32), pltpu.VMEM((rows, LANES), f32)],
        flops=2 * rows * D * INNER,
        bytes_moved=2 * D * INNER + 14 * rows * INNER,
    )(y, gate, c, ecf, st, chan, packed, resid, gain)


def unjoin_kernel(
    dout, wout, y, gate, inv, c, ecf, chan, dy_o, dgate_o, dgain_o, ds_o, s_scaled, s_along
):
    phase = pl.program_id(0)
    group = pl.program_id(1)
    gain = chan[CONV + 1 : CONV + 2, :]
    raw = gate[...]
    sig = sigmoid(raw)
    opened = raw * sig
    gated = y[...] * opened
    inverse = inv[:, :1]

    @pl.when(phase == 0)
    def _():
        dscaled = nn(dout[...], unpacked_out(wout, 0, D // wout.shape[0]))
        s_scaled[group] = dscaled
        part = jnp.sum(dscaled * gain * gated, axis=1, keepdims=True)
        part = jnp.broadcast_to(part, s_along.shape)

        @pl.when(group == 0)
        def _():
            s_along[...] = part

        @pl.when(group > 0)
        def _():
            s_along[...] += part

    @pl.when(phase == 1)
    def _():
        dscaled = s_scaled[group]
        pulled = inverse * inverse * inverse * s_along[:, :1] / INNER
        dgated = inverse * gain * dscaled - gated * pulled
        dgain = jnp.sum(dscaled * gated * inverse, axis=0, keepdims=True)
        dgain_o[...] = jnp.broadcast_to(dgain, dgain_o.shape)
        dy = dgated * opened
        dy_o[...] = dy
        dgate_o[...] = (dgated * y[...] * (sig * (1.0 + raw * (1.0 - sig)))).astype(bf16)
        ecf_e = expanded(ecf[...], spread(group))
        ds_o[...] = tn(c[...], (ecf_e * dy).astype(bf16))


def scan_unjoin(dout, packed, y, gate, inv, c, ecf, chan):
    rows = y.shape[0]
    shares = packed.shape[0]

    def both(height):
        return pl.BlockSpec((height, WIDTH), lambda p, g: (0, g))

    def second(height):
        return pl.BlockSpec((height, WIDTH), lambda p, g: (0, g * p))

    return call(
        unjoin_kernel,
        (2, GROUPS),
        [
            whole((rows, D)),
            pl.BlockSpec(
                (shares, D // shares // 2, D),
                lambda p, g: (0, 2 * GROUPS + jnp.where(p == 0, g, GROUPS - 1), 0),
            ),
            both(rows),
            both(rows),
            whole((rows, LANES)),
            whole((rows, STATE)),
            whole((rows, LANES)),
            both(8),
        ],
        [second(rows), second(rows), second(8), second(STATE)],
        [
            struct((rows, INNER)),
            struct((rows, INNER), bf16),
            struct((8, INNER)),
            struct((STATE, INNER)),
        ],
        [pltpu.VMEM((GROUPS, rows, WIDTH), f32), pltpu.VMEM((rows, LANES), f32)],
        flops=2 * rows * D * INNER,
        bytes_moved=2 * D * INNER + 22 * rows * INNER,
    )(dout, packed, y, gate, inv, c, ecf, chan)


def head_sums(values, expand):
    if values.shape[0] == 1:
        return head_sums(jnp.broadcast_to(values, (8, values.shape[1])), expand)[0:1, :]
    return expanded(values, expand, by=nt)


def conv_back(ref, taps, pad, rows, low, width, taps_o, main, halo):
    grads = [jnp.sum(pad[HALO : HALO + rows, :] * ref[HALO - 3 + j : HALO - 3 + j + rows,
             low : low + width], axis=0, keepdims=True) for j in range(CONV)]
    grads.append(jnp.sum(pad[HALO : HALO + rows, :], axis=0, keepdims=True))
    taps_o[...] = jnp.concatenate(grads + [jnp.zeros((3, width), f32)], axis=0)
    total = jnp.zeros((HALO + rows, width), f32)
    for j in range(CONV):
        shift = CONV - 1 - j
        total = total + pad[shift : shift + HALO + rows, :] * taps[j : j + 1, :]
    halo(total[:HALO])
    main(total[HALO:])


def back_kernel(
    xraw, dy, bcdt, st, dst, chan, headp, bcv,
    dx_o, tail_o, halo_o, dchan_o, dbc_o, dbch_o, dheadp_o, dbcv_o,
    s_b, s_c, s_dt, s_cum, s_cumt, s_g,
    s_db, s_dc, s_dcum, s_ddt, s_dtot, s_dg, s_skip, s_pad, s_state, s_bcpad, s_cume,
):
    rows = dy.shape[0]
    blocks = rows // BLOCK
    group = pl.program_id(0)

    @pl.when(group == 0)
    def _():
        small_parts(rows, bcdt, headp, bcv, s_b, s_c, s_dt, s_cum, s_cumt, s_g)
        for ref in (s_db, s_dc, s_dcum, s_ddt, s_dtot, s_dg, s_skip, s_pad, s_bcpad):
            ref[...] = jnp.zeros(ref.shape, f32)

    pre = conv_rows(xraw, chan, rows, 0, WIDTH)
    sig = sigmoid(pre)
    xc = pre * sig
    expand = spread(group)
    dt_e = expanded(s_dt[...], expand)
    u = xc * dt_e
    skip = expanded(headp[...], expand)[2:3, :]
    state = st[...]
    for b in range(blocks):
        r = slice(b * BLOCK, (b + 1) * BLOCK)
        s_state[b] = state
        cum_e = expanded(s_cum[r, :], expand)
        s_cume[r, :] = cum_e
        if b < blocks - 1:
            total = cum_e[BLOCK - 1 : BLOCK, :]
            fresh = tn(s_b[r, :], (u[r] * jnp.exp(total - cum_e)).astype(bf16))
            state = state * jnp.exp(total) + fresh
    dstate = dst[...]
    dskip = jnp.zeros((1, WIDTH), f32)
    for b in reversed(range(blocks)):
        r = slice(b * BLOCK, (b + 1) * BLOCK)
        cum_e = s_cume[r, :]
        total = cum_e[BLOCK - 1 : BLOCK, :]
        keys, reads = s_b[r, :], s_c[r, :]
        to_here, to_end, passed = jnp.exp(cum_e), jnp.exp(total - cum_e), jnp.exp(total)
        u_b, dy_b = u[r], dy[r, :]
        u_low, dy_low = u_b.astype(bf16), dy_b.astype(bf16)
        state_low, dstate_low = s_state[b].astype(bf16), dstate.astype(bf16)
        faded = (dy_b * to_here).astype(bf16)
        y_across = to_here * nn(reads, state_low)
        s_dc[r, :] += nt(faded, state_low)
        du_across = to_end * nn(keys, dstate_low)
        s_db[r, :] += nt((u_b * to_end).astype(bf16), dstate_low)
        cum_rows = head_rows(s_cumt, group, r)
        y_pieces, du_pieces = [], []
        dscores = jnp.zeros((BLOCK, BLOCK), f32)
        for pair in range(WIDTH // LANES):
            at = slice(pair * LANES, (pair + 1) * LANES)
            y_piece = jnp.zeros((BLOCK, LANES), f32)
            du_piece = jnp.zeros((BLOCK, LANES), f32)
            for j in range(2):
                fade = fading(cum_e, cum_rows, 2 * pair + j)
                weights = (fade * s_g[b]).astype(bf16)
                dy_head = one_head(dy_b[:, at], j)
                y_piece = y_piece + nn(weights, one_head(u_b[:, at], j))
                du_piece = du_piece + tn(weights, dy_head)
                dscores = dscores + nt(dy_head, u_low[:, at]) * fade
            y_pieces.append(y_piece)
            du_pieces.append(du_piece)
        y_within = jnp.concatenate(y_pieces, axis=1)
        du_within = jnp.concatenate(du_pieces, axis=1)
        s_dg[b] += dscores
        du = du_within + du_across
        moved = u_b * du_across
        dcum = dy_low.astype(f32) * y_within + dy_b * y_across
        dcum = dcum - u_low.astype(f32) * du_within - moved
        s_dcum[r, :] += head_sums(dcum, expand)
        dtotal = jnp.sum(moved, axis=0, keepdims=True)
        dtotal = dtotal + passed * jnp.sum(s_state[b] * dstate, axis=0, keepdims=True)
        s_dtot[b : b + 1, :] += head_sums(dtotal, expand)
        s_ddt[r, :] += head_sums(du * xc[r], expand)
        dskip = dskip + jnp.sum(dy_b * xc[r], axis=0, keepdims=True)
        dxc = du * dt_e[r] + skip * dy_b
        s_pad[HALO + b * BLOCK : HALO + (b + 1) * BLOCK, :] = dxc * (
            sig[r] * (1.0 + pre[r] * (1.0 - sig[r]))
        )
        dstate = passed * dstate + tn(reads, faded)
    s_skip[0:1, :] += head_sums(dskip, expand)

    def put_main(values):
        dx_o[...] = values.astype(bf16)
        tail_o[...] = values[rows - HALO :]

    def put_halo(values):
        halo_o[...] = values

    conv_back(xraw, chan, s_pad, rows, 0, WIDTH, dchan_o, put_main, put_halo)

    @pl.when(group == GROUPS - 1)
    def _():
        keep = triangle()
        upper = (iota((BLOCK, BLOCK), 0) <= iota((BLOCK, BLOCK), 1)).astype(f32)
        rate = headp[1:2, :]
        bias_sum = jnp.zeros((1, LANES), f32)
        rate_sum = jnp.zeros((1, LANES), f32)
        for b in range(blocks):
            r = slice(b * BLOCK, (b + 1) * BLOCK)
            dscores = jnp.where(keep, s_dg[b], 0.0).astype(bf16)
            s_dc[r, :] += nn(dscores, s_b[r, :])
            s_db[r, :] += tn(dscores, s_c[r, :])
            da = nn(upper, s_dcum[r, :], full) + s_dtot[b : b + 1, :]
            ddt = s_ddt[r, :] + da * rate
            rate_sum = rate_sum + jnp.sum(da * (rate * s_dt[r, :]), axis=0, keepdims=True)
            raw = bcdt[HALO + b * BLOCK : HALO + (b + 1) * BLOCK, 2 * STATE :] + headp[0:1, :]
            ddt = ddt * sigmoid(raw)
            bias_sum = bias_sum + jnp.sum(ddt, axis=0, keepdims=True)
            dbc_o[r, 2 * STATE :] = ddt
        dheadp_o[...] = jnp.concatenate(
            [bias_sum, rate_sum, s_skip[0:1, :], jnp.zeros((5, LANES), f32)], axis=0
        )
        bc_pre = conv_rows(bcdt, bcv, rows, 0, 2 * STATE)
        bc_sig = sigmoid(bc_pre)
        turn = bc_sig * (1.0 + bc_pre * (1.0 - bc_sig))
        s_bcpad[HALO : HALO + rows, :STATE] = s_db[...] * turn[:, :STATE]
        s_bcpad[HALO : HALO + rows, STATE:] = s_dc[...] * turn[:, STATE:]

        def put_bc(values):
            dbc_o[:, : 2 * STATE] = values

        def put_bc_halo(values):
            dbch_o[...] = values

        conv_back(bcdt, bcv, s_bcpad, rows, 0, 2 * STATE, dbcv_o, put_bc, put_bc_halo)


def scan_back(xraw, dy, bcdt, st, dst, chan, headp, bcv):
    rows = dy.shape[0]
    ext = rows + HALO
    blocks = rows // BLOCK
    return call(
        back_kernel,
        (GROUPS,),
        [
            columns(ext),
            columns(rows),
            whole((ext, 384)),
            columns(STATE),
            columns(STATE),
            columns(8),
            whole((8, LANES)),
            whole((8, 2 * STATE)),
        ],
        [
            columns(rows),
            columns(HALO),
            columns(HALO),
            columns(8),
            whole((rows, 384)),
            whole((HALO, 2 * STATE)),
            whole((8, LANES)),
            whole((8, 2 * STATE)),
        ],
        [
            struct((rows, INNER), bf16),
            struct((HALO, INNER)),
            struct((HALO, INNER)),
            struct((8, INNER)),
            struct((rows, 384)),
            struct((HALO, 2 * STATE)),
            struct((8, LANES)),
            struct((8, 2 * STATE)),
        ],
        small_scratch(rows)
        + [
            pltpu.VMEM((rows, STATE), f32),
            pltpu.VMEM((rows, STATE), f32),
            pltpu.VMEM((rows, LANES), f32),
            pltpu.VMEM((rows, LANES), f32),
            pltpu.VMEM((8, LANES), f32),
            pltpu.VMEM((blocks, BLOCK, BLOCK), f32),
            pltpu.VMEM((8, LANES), f32),
            pltpu.VMEM((rows + 2 * HALO, WIDTH), f32),
            pltpu.VMEM((blocks, STATE, WIDTH), f32),
            pltpu.VMEM((rows + 2 * HALO, 2 * STATE), f32),
            pltpu.VMEM((rows, WIDTH), f32),
        ],
        flops=20 * rows * INNER * STATE,
        bytes_moved=12 * rows * INNER,
    )(xraw, dy, bcdt, st, dst, chan, headp, bcv)


SHARE = 3 * WIDTH + LANES


def grads_kernel(
    normed, dout, dgate, dx, tail, back, dbcdt, bc_back, scaled, w_zx, wb, resid, dresid, gain,
    packed_o, dres_o, dgain_o, s_bc, s_sum,
):
    rows = normed.shape[0]
    group = pl.program_id(0)
    edge = slice(rows - HALO, rows)

    @pl.when(group == 0)
    def _():
        s_bc[GROUPS - 1] = jnp.zeros((rows, LANES), bf16)
        for q in range(3):
            at = slice(q * LANES, (q + 1) * LANES)
            s_bc[q] = dbcdt[:, at].astype(bf16)
            if q < 2:
                s_bc[q, edge, :] = (dbcdt[edge, at] + bc_back[:, at]).astype(bf16)
        total = nt(s_bc[0], wb[:, :LANES])
        total = total + nt(s_bc[1], wb[:, LANES : 2 * LANES])
        s_sum[...] = total + nt(s_bc[2], wb[:, 2 * LANES :])

    fixed = (tail[...] + back[...]).astype(bf16)
    dzx = jnp.concatenate(
        [dgate[...], jnp.concatenate([dx[: rows - HALO, :], fixed], axis=0)], axis=1
    )
    s_sum[...] += nt(dzx, w_zx[...].reshape(D, 2 * WIDTH))
    packed_o[:, : 2 * WIDTH] = tn(normed[...], dzx).astype(bf16)
    packed_o[:, 2 * WIDTH : 3 * WIDTH] = tn(dout[...], scaled[...]).astype(bf16)
    packed_o[:, 3 * WIDTH :] = tn(normed[...], s_bc[group]).astype(bf16)

    @pl.when(group == GROUPS - 1)
    def _():
        values, grad, weight = resid[...], s_sum[...], gain[0:1, :]
        inverse = lax.rsqrt(jnp.mean(values * values, axis=1, keepdims=True) + norm_eps)
        along = jnp.mean(grad * weight * values, axis=1, keepdims=True)
        pulled = inverse * inverse * inverse * along
        dres_o[...] = dresid[...] + inverse * weight * grad - values * pulled
        dgain = jnp.sum(grad * values * inverse, axis=0, keepdims=True)
        dgain_o[...] = jnp.broadcast_to(dgain, dgain_o.shape)


def layer_grads(
    normed, dout, dgate, dx, tail, back, dbcdt, bc_back, scaled, packed, wb, resid, dresid, gain
):
    rows = normed.shape[0]
    return call(
        grads_kernel,
        (GROUPS,),
        [
            whole((rows, D)),
            whole((rows, D)),
            columns(rows),
            columns(rows),
            columns(HALO),
            columns(HALO),
            whole((rows, 384)),
            whole((HALO, 2 * STATE)),
            columns(rows),
            packed_zx(packed),
            whole(wb.shape),
            whole((rows, D)),
            whole((rows, D)),
            whole((8, D)),
        ],
        [columns(D, SHARE), whole((rows, D)), whole((8, D))],
        [struct((D, GROUPS * SHARE), bf16), struct((rows, D)), struct((8, D))],
        [pltpu.VMEM((GROUPS, rows, LANES), bf16), pltpu.VMEM((rows, D), f32)],
        flops=10 * rows * D * INNER,
        bytes_moved=26 * D * INNER,
    )(normed, dout, dgate, dx, tail, back, dbcdt, bc_back, scaled, packed, wb, resid, dresid, gain)


def lookup_kernel(keys, edges, first, second, out, s_rows):
    cls = pl.program_id(0)
    parts, lines, width = first.shape[1:]

    @pl.when(cls == 0)
    def _():
        s_rows[...] = jnp.zeros(s_rows.shape, f32)

    place = iota((16, width), 0)
    for half, table in enumerate((first, second)):

        def turn(i, carry, half=half, table=table):
            key = keys[i]
            at = key & (PAST - 1)
            line = (key >> 11) - (2 * cls + half) * lines
            base = pl.multiple_of((line >> 4) << 4, 16)
            found = []
            for part in range(parts):
                tile = table[0, part, pl.ds(base, 16), :].astype(f32)
                found.append(
                    jnp.sum(jnp.where(place == (line & 15), tile, 0.0), axis=0, keepdims=True)
                )
            s_rows[pl.ds(at, 1), :] = jnp.concatenate(found, axis=1)
            return carry

        lax.fori_loop(edges[2 * cls + half], edges[2 * cls + half + 1], turn, 0)

    @pl.when(cls == CLASSES - 1)
    def _():
        out[...] = s_rows[...].astype(bf16)


def lookup(keys, edges, halves):
    count = keys.shape[0]
    spec = pl.BlockSpec((1,) + halves[0].shape[1:], lambda c, *_: (c, 0, 0, 0))
    return call(
        lookup_kernel,
        (CLASSES,),
        [spec, spec],
        whole((count, D)),
        struct((count, D), bf16),
        [pltpu.VMEM((count, D), f32)],
        prefetch=2,
        bytes_moved=4 * halves[0].size,
    )(keys, edges, *halves)


def place_kernel(spots, packed, *refs):
    *before, gain, out, normed_o, s_packed = refs
    cap = packed.shape[1]
    for j in range(packed.shape[0]):
        s_packed[j * cap : (j + 1) * cap, :] = packed[j].astype(f32)
    s_packed[packed.shape[0] * cap :, :] = jnp.zeros((8, D), f32)

    def turn(i, carry):
        out[pl.ds(i, 1), :] = s_packed[pl.ds(spots[i], 1), :]
        return carry

    lax.fori_loop(0, out.shape[0], turn, 0, unroll=8)
    if before:
        out[...] += before[0][...]
    normed_o[...] = normed(out[...], gain[0:1, :])


def place_rows(spots, packed, before, gain):
    rows = spots.shape[0]
    more = [] if before is None else [before]
    return call(
        place_kernel,
        (1,),
        [whole(packed.shape)] + [whole((rows, D)) for _ in more] + [whole((8, D))],
        [whole((rows, D))] * 2,
        [struct((rows, D)), struct((rows, D), bf16)],
        [pltpu.VMEM((packed.shape[0] * packed.shape[1] + 8, D), f32)],
        prefetch=1,
        bytes_moved=4 * rows * D,
    )(spots, packed, *more, gain)


def send_kernel(spots, grads, out, s_packed):
    cap = out.shape[1]
    s_packed[...] = jnp.zeros(s_packed.shape, f32)

    def turn(i, carry):
        s_packed[pl.ds(spots[i], 1), :] += grads[pl.ds(i, 1), :]
        return carry

    lax.fori_loop(0, grads.shape[0], turn, 0, unroll=8)
    for j in range(out.shape[0]):
        out[j] = s_packed[j * cap : (j + 1) * cap, :].astype(bf16)


def send_rows(spots, grads, n_tensor):
    shape = (n_tensor, CAP, D)
    return call(
        send_kernel,
        (1,),
        [whole(grads.shape)],
        whole(shape),
        struct(shape, bf16),
        [pltpu.VMEM((n_tensor * CAP + 8, D), f32)],
        prefetch=1,
        bytes_moved=8 * grads.size,
    )(spots, grads)


def pack_kernel(keys, ranks, starts, firsts, where, rows, out, s_rows, s_out):
    own, offset = where[0], where[1]
    cap, width = out.shape[1:]
    parts = D // width
    s_rows[...] = rows[...].astype(f32)
    s_out[...] = jnp.zeros(s_out.shape, f32)
    for cls in range(CLASSES):

        def turn(i, carry, cls=cls):
            row = s_rows[pl.ds(keys[i] & (PAST - 1), 1), :]
            slot = ranks[i] - firsts[cls] - offset
            slot = jnp.where((slot >= 0) & (slot < cap), slot, cap)
            for part in range(parts):
                piece = row[:, part * width : (part + 1) * width]
                s_out[own ^ (cls * parts + part), pl.ds(slot, 1), :] += piece
            return carry

        lax.fori_loop(starts[2 * cls], starts[2 * cls + 2], turn, 0)
    out[...] = s_out[:, :cap, :].astype(bf16)


def pack_rows(keys, ranks, starts, firsts, where, rows, n_data):
    count = keys.shape[0]
    shape = (n_data, CAP, D * CLASSES // n_data)
    return call(
        pack_kernel,
        (1,),
        [whole((count, D))],
        whole(shape),
        struct(shape, bf16),
        [pltpu.VMEM((count, D), f32), pltpu.VMEM((n_data, CAP + 8, shape[2]), f32)],
        prefetch=5,
        bytes_moved=2 * count * D,
    )(keys, ranks, starts, firsts, where, rows)


def add_kernel(keys, starts, where, packed, base, out, square, s_packed):
    cls, offset = where[0], where[1]
    lines = base.shape[0]
    count = keys.shape[0] // packed.shape[0]
    cap = packed.shape[1]
    s_packed[...] = packed[...].astype(f32)
    out[...] = base[...].astype(f32)
    for r in range(packed.shape[0]):
        first = starts[8 * r + cls] + offset

        def turn(i, carry):
            line = keys[r * count + i] - cls * lines
            out[pl.ds(line, 1), :] += s_packed[r, pl.ds(i - first, 1), :]
            return carry

        lax.fori_loop(first, jnp.minimum(starts[8 * r + cls + 1], first + cap), turn, 0)
    square[...] = jnp.zeros(square.shape, f32)
    for low in range(0, lines, TILE):
        part = out[low : low + TILE, :]
        square[0:1, :] += jnp.sum(part * part, axis=0, keepdims=True)


def add_rows(keys, starts, where, packed, base):
    return call(
        add_kernel,
        (1,),
        [whole(packed.shape), whole(base.shape)],
        [whole(base.shape), whole((8, base.shape[1]))],
        [struct(base.shape), struct((8, base.shape[1]))],
        [pltpu.VMEM(packed.shape, f32)],
        prefetch=3,
        bytes_moved=8 * base.size,
    )(keys, starts, where, packed, base)


def tile_lines(core, height):
    return (core[0] * 2 + pl.program_id(1)) * height


def tile_logits(core, table, chosen, real):
    parts, height, width = table.shape[1:]
    result = nt(table[0, 0], chosen[:, :width])
    for part in range(1, parts):
        result = result + nt(table[0, part], chosen[:, part * width : (part + 1) * width])
    line = tile_lines(core, height) + iota(result.shape, 0)
    return jnp.where(line < real, result, -1e30)


def tile_hit(core, table, lines, wanted):
    height = table.shape[2]
    first = pl.program_id(0) * lines + tile_lines(core, height)
    return first + iota((height, wanted.shape[1]), 0) == wanted[0:1, :]


def one_half(core, first, second):
    return jnp.where(core[0] == 0, first[...], second[...])


def measure_kernel(real, lines, core, first_half, second_half, chosen, wanted, out, s_stats):
    table = one_half(core, first_half, second_half)
    logits = tile_logits(core, table, chosen, real)
    hit = tile_hit(core, table, lines, wanted)
    first = (pl.program_id(0) == 0) & (pl.program_id(1) == 0)

    @pl.when(first)
    def _():
        s_stats[0:1, :] = jnp.full((1, s_stats.shape[1]), -1e30, f32)
        s_stats[1:8, :] = jnp.zeros((7, s_stats.shape[1]), f32)

    old = s_stats[0:1, :]
    top = jnp.maximum(old, jnp.max(logits, axis=0, keepdims=True))
    total = s_stats[1:2, :] * jnp.exp(old - top)
    s_stats[1:2, :] = total + jnp.sum(jnp.exp(logits - top), axis=0, keepdims=True)
    s_stats[2:3, :] += jnp.sum(jnp.where(hit, logits, 0.0), axis=0, keepdims=True)
    s_stats[0:1, :] = top
    out[...] = s_stats[...]


def table_specs(halves):
    parts, width = halves[0].shape[1], halves[0].shape[3]

    def spec(k):
        def place(c, i, core):
            mine = core[0] == k
            return (jnp.where(mine, c, 0), 0, jnp.where(mine, i, 0), 0)

        return pl.BlockSpec((1, parts, TILE, width), place)

    return [spec(0), spec(1)]


def vocab_measure(core, halves, chosen, wanted, real):
    count = chosen.shape[0]
    lines = 2 * halves[0].shape[2]
    return call(
        functools.partial(measure_kernel, real, lines),
        (CLASSES, lines // TILE // 2),
        table_specs(halves) + [whole((count, D)), whole((8, count))],
        whole((8, count)),
        struct((8, count)),
        [pltpu.VMEM((8, count), f32)],
        prefetch=1,
        flops=2 * count * halves[0].size,
        bytes_moved=2 * halves[0].size,
    )(core, *halves, chosen, wanted)


def vocab_kernel(
    real, lines, core, first_half, second_half, chosen, wanted, stats, dtable, dchosen, s_sum
):
    table = one_half(core, first_half, second_half)
    logits = tile_logits(core, table, chosen, real)
    hit = tile_hit(core, table, lines, wanted)
    soft = jnp.exp(logits - stats[0:1, :])
    dlogits = (stats[1:2, :] * (soft - jnp.where(hit, 1.0, 0.0))).astype(bf16)
    step = pl.program_id(0) * pl.num_programs(1) + pl.program_id(1)
    parts, width = table.shape[1], table.shape[3]

    @pl.when(step == 0)
    def _():
        s_sum[...] = jnp.zeros(s_sum.shape, f32)

    for part in range(parts):
        at = slice(part * width, (part + 1) * width)
        dtable[0, part] = nn(dlogits, chosen[:, at]).astype(bf16)
        s_sum[:, at] += tn(dlogits, table[0, part])

    @pl.when(step == CLASSES * pl.num_programs(1) - 1)
    def _():
        dchosen[...] = s_sum[...].astype(bf16)


def vocab_back(core, halves, chosen, wanted, stats, real):
    count = chosen.shape[0]
    parts, lines, width = halves[0].shape[1:]
    return call(
        functools.partial(vocab_kernel, real, 2 * lines),
        (CLASSES, lines // TILE),
        table_specs(halves) + [whole((count, D)), whole((8, count)), whole((8, count))],
        [
            pl.BlockSpec((1, parts, TILE, width), lambda c, i, core: (c, 0, i, 0)),
            whole((count, D)),
        ],
        [struct(halves[0].shape, bf16), struct((count, D), bf16)],
        [pltpu.VMEM((count, D), f32)],
        prefetch=1,
        flops=6 * count * halves[0].size,
        bytes_moved=4 * halves[0].size,
    )(core, *halves, chosen, wanted, stats)


def shifted(values, axis, by):
    n = lax.axis_size(axis)
    return lax.ppermute(values, axis, [(i, (i + by) % n) for i in range(n)])


def swapped(values):
    return lax.ppermute(values, "core", [(0, 1), (1, 0)])


def to_later(values):
    return lax.ppermute(values, "core", [(0, 1)])


def to_earlier(values):
    return lax.ppermute(values, "core", [(1, 0)])


def crossed(values, axis, by):
    n = lax.axis_size(axis) if isinstance(axis, str) else axis_count(axis)
    return lax.ppermute(values, axis, [(i, i ^ by) for i in range(n)])


def axis_count(axes):
    count = 1
    for axis in axes:
        count *= lax.axis_size(axis)
    return count


def everywhere(values, axes, combine=jnp.add):
    for axis in axes:
        reach = 1
        while reach < lax.axis_size(axis):
            if 2 * reach < lax.axis_size(axis):
                one, two, three = (crossed(values, axis, by * reach) for by in (1, 2, 3))
                values = combine(combine(values, one), combine(two, three))
                reach *= 4
            else:
                values = combine(values, crossed(values, axis, reach))
                reach *= 2
    return values


def relative(values):
    values = values[None]
    for axis in ("core", "chip"):
        reach = 1
        while reach < lax.axis_size(axis):
            values = jnp.concatenate([values, crossed(values, axis, reach)], axis=0)
            reach *= 2
    return values


def exchanged(blocks):
    return jnp.stack([blocks[0]] + [crossed(blocks[r], DP, r) for r in range(1, blocks.shape[0])])


def around(values, axis):
    n = lax.axis_size(axis)
    return jnp.stack([values] + [shifted(values, axis, by) for by in range(1, n)])


def sum_back(blocks, axis):
    n = lax.axis_size(axis)
    result = blocks[0].astype(f32)
    for by in range(1, n):
        result = result + shifted(blocks[by], axis, -by).astype(f32)
    return result


def by_core(own, other, axis=0):
    first = lax.axis_index("core") == 0
    return jnp.concatenate(
        [jnp.where(first, own, other), jnp.where(first, other, own)], axis=axis
    )


def inverse_rms(values):
    return lax.rsqrt(jnp.mean(values * values, axis=-1, keepdims=True) + norm_eps)


def rms_back(grad, values, gain):
    inverse = inverse_rms(values)
    along = jnp.mean(grad * gain * values, axis=-1, keepdims=True)
    dvalues = inverse * gain * grad - values * (inverse * inverse * inverse * along)
    return (dvalues, jnp.sum(grad * values * inverse, axis=0))


def in_order(blocks, axis):
    n = blocks.shape[axis]
    z = lax.axis_index("tensor")
    taken = [lax.dynamic_index_in_dim(blocks, (z - q) % n, axis, False) for q in range(n)]
    return jnp.stack(taken, axis=axis)


def turn_heads(bcdt):
    rows = bcdt.shape[0]
    steps = bcdt[:, 2 * STATE : 2 * STATE + HEADS].reshape(rows, GROUPS, -1)
    steps = in_order(steps, 1).reshape(rows, HEADS)
    return jnp.concatenate([bcdt[:, : 2 * STATE], steps, bcdt[:, 2 * STATE + HEADS :]], axis=1)


def pack_layer(w_zx, w_bcdt, w_out):
    rows = w_zx.shape[0]
    zx = w_zx.reshape(rows, -1)
    out = jnp.concatenate([w_out[: rows // 2], w_out[rows // 2 :]], axis=1)
    own = jnp.concatenate([zx, out], axis=0).astype(bf16)
    blocks = around(own, "tensor")
    zx = blocks[:, :rows].reshape(-1, D)
    out = blocks[:, rows:].reshape(-1, D)
    lines = -(-rows // 48) * 16
    bcdt = jnp.pad(w_bcdt.astype(bf16), ((0, 3 * lines - rows), (0, LANES - HEADS)))
    bcdt = jnp.pad(bcdt[:, : 2 * STATE + HEADS].reshape(3, lines, -1), ((0, 0), (0, 0), (0, 32)))
    bcdt = jnp.concatenate([bcdt[0], bcdt[1], bcdt[2]], axis=1)
    bcdt = jnp.pad(bcdt, ((0, 0), (0, D - bcdt.shape[1])))
    return jnp.concatenate([zx, out, bcdt], axis=0)


def unpack_bcdt(packed):
    rows = D // packed.shape[0]
    lines = -(-rows // 48) * 16
    width = 2 * STATE + HEADS + 32
    part = packed[:, GROUPS * (rows + rows // 2) :]
    part = jnp.concatenate([part[:, :, i * width : (i + 1) * width] for i in range(3)], axis=1)
    part = part[:, :rows].reshape(D, width)
    return turn_heads(jnp.pad(part, ((0, 0), (0, 2 * STATE + LANES - width))))


def reduce_layer(mine):
    n_tensor = lax.axis_size("tensor")
    shares = [mine[:, j * SHARE : (j + 1) * SHARE] for j in range(n_tensor)]
    bcdt = turn_heads(jnp.concatenate([share[:, 3 * WIDTH :] for share in shares[:3]], axis=1))
    blocks = []
    for by in range(n_tensor):
        block = jnp.concatenate([shares[-by][:, : 3 * WIDTH], bcdt], axis=1)
        blocks.append(block if by == 0 else shifted(block, "tensor", by))
    blocks = [block.astype(f32) for block in blocks]
    even = functools.reduce(jnp.add, blocks[0::2])
    odd = functools.reduce(jnp.add, blocks[1::2])
    total = even + odd
    return (
        total[:, : 2 * WIDTH].reshape(-1, 2, WIDTH),
        total[:, 2 * WIDTH : 3 * WIDTH],
        total[:, 3 * WIDTH : 3 * WIDTH + 2 * STATE + HEADS],
    )


def layer_forward(resid, normed, next_gain, packed, wb, smalls):
    chan, headp, bcv = smalls
    nx = jnp.concatenate([to_later(normed[-HALO:]), normed], axis=0)
    y, gate, xraw, st, bcdt, c, ecf = scan_front(nx, packed, wb, chan, headp, bcv)
    before = to_later(st)
    y, scaled, inverse, out, following = scan_join(
        y, gate, c, ecf, before, chan, packed, resid, next_gain
    )
    return out, following, (resid, normed, y, gate, xraw, before, bcdt, c, ecf, scaled, inverse)


def layer_backward(dresid, kept, gain, packed, wb, smalls, done):
    resid, normed, y, gate, xraw, before, bcdt, c, ecf, scaled, inverse = kept
    chan, headp, bcv = smalls
    dout = dresid.astype(bf16)
    dy, dgate, dgain, dstart = scan_unjoin(dout, packed, y, gate, inverse, c, ecf, chan)
    after = to_earlier(dstart)
    dx, tail, halo, dchan, dbcdt, bc_halo, dheadp, dbcv = scan_back(
        xraw, dy, bcdt, before, after, chan, headp, bcv
    )
    dx, done = lax.optimization_barrier((dx, done))
    back, bc_back = to_earlier(halo), to_earlier(bc_halo)
    grads, dresid, dnorm_gain = layer_grads(
        normed, dout, dgate, dx, tail, back, dbcdt, bc_back,
        scaled, packed, wb, resid, dresid, gain,
    )
    dchan = jnp.concatenate([dchan[: CONV + 1], dgain[:1]], axis=0)
    smalls = (dnorm_gain[0], dchan, dheadp[:3, :HEADS], dbcv[: CONV + 1])
    return dresid, grads, smalls, done


def flat_layer(parts, final_gain):
    gain, chan, head, taps = parts
    n_tensor = lax.axis_size("tensor")
    chan = in_order(chan.reshape(CONV + 2, n_tensor, -1), 1)
    head = in_order(head.reshape(3, n_tensor, -1), 1).reshape(3, HEADS)
    rows = [gain.reshape(-1, LANES), chan.reshape(-1, LANES), taps.reshape(-1, LANES)]
    rows.append(jnp.pad(head, ((0, 5), (0, LANES - HEADS))))
    if final_gain is not None:
        rows.append(final_gain.reshape(-1, LANES))
    return jnp.concatenate(rows)


def unflat_layer(flat):
    n_tensor = lax.axis_size("tensor")
    z = lax.axis_index("tensor")
    one, two = D // LANES, (CONV + 2) * INNER // LANES
    three = (CONV + 1) * 2 * STATE // LANES
    gain = flat[:one].reshape(D)
    chan = flat[one : one + two].reshape(CONV + 2, INNER)
    chan = lax.dynamic_slice_in_dim(chan, z * (INNER // n_tensor), INNER // n_tensor, 1)
    taps = flat[one + two : one + two + three].reshape(CONV + 1, 2 * STATE)
    head = flat[one + two + three : one + two + three + 3, :HEADS]
    head = lax.dynamic_slice_in_dim(head, z * (HEADS // n_tensor), HEADS // n_tensor, 1)
    return (gain, chan, head, taps, flat[one + two + three + 8 :].reshape(-1))


def lse_merge(first, second):
    top = jnp.maximum(first[0], second[0])
    total = first[1] * jnp.exp(first[0] - top) + second[1] * jnp.exp(second[0] - top)
    return jnp.stack([top, total, first[2] + second[2]])


def adapt(weight, first, second, grad):
    first_new = first_decay * first + (1.0 - first_decay) * grad
    second_new = second_decay * second + (1.0 - second_decay) * grad * grad
    update = (
        first_new
        / (1.0 - first_decay**STEP)
        / (jnp.sqrt(second_new / (1.0 - second_decay**STEP)) + adam_eps)
        + weight_decay * weight
    )
    return (first_new, second_new, update)


def group_squares(values, stacked):
    if stacked:
        return jnp.sum(values * values, axis=tuple(range(1, values.ndim)))
    return jnp.sum(values * values)[None]


def layer_marks(shape, axis, values):
    result = jnp.full(shape, values[0], f32)
    place = iota(shape, axis or 0)
    for i in range(1, len(values)):
        result = jnp.where(place == i, values[i], result)
    return result


def adapt_kernel(axes, scale, *refs):
    count = len(axes)
    inputs, outputs, squares = refs[: 4 * count], refs[4 * count : 7 * count], refs[-1]
    at = 0
    for k, axis in enumerate(axes):
        weight, first, second, grad = (ref[...] for ref in inputs[4 * k : 4 * k + 4])
        moved = adapt(weight, first, second, grad * scale[0])
        for ref, value in zip(outputs[3 * k : 3 * k + 3], moved):
            ref[...] = value
        square = moved[2] * moved[2]
        if axis is None:
            squares[at] = jnp.sum(square)
            at += 1
        else:
            for i in range(LAYERS):
                squares[at] = jnp.sum(jnp.where(iota(square.shape, axis) == i, square, 0.0))
                at += 1


def step_kernel(axes, factors, *refs):
    count = len(axes)
    weights, changes, outputs = refs[:count], refs[count : 2 * count], refs[2 * count :]
    at = 0
    for k, axis in enumerate(axes):
        values = [factors[at + i] for i in range(1 if axis is None else LAYERS)]
        at += len(values)
        marks = layer_marks(weights[k].shape, axis, values)
        outputs[k][...] = weights[k][...] - marks * changes[k][...]


def at_once(kernel, scalars, arrays, shapes, extra):
    smem = pl.BlockSpec(memory_space=pltpu.SMEM)
    vmem = pl.BlockSpec(memory_space=pltpu.VMEM)
    return pl.pallas_call(
        kernel,
        in_specs=[smem] + [vmem] * len(arrays),
        out_specs=[vmem] * len(shapes) + [smem] * len(extra),
        out_shape=[struct(shape) for shape in shapes + extra],
        compiler_params=pltpu.CompilerParams(vmem_limit_bytes=VMEM_BYTES),
    )(scalars, *arrays)


def body(
    token_ids, lengths, loss_pos, targets,
    embed, embed_m, embed_v,
    w_zx, w_zx_m, w_zx_v,
    w_bcdt, w_bcdt_m, w_bcdt_v,
    w_out, w_out_m, w_out_v,
    channel, channel_m, channel_v,
    per_head, per_head_m, per_head_v,
    bc_conv, bc_conv_m, bc_conv_v,
    gains, gains_m, gains_v,
):
    n_tensor = lax.axis_size("tensor")
    n_data = lax.axis_size("chip") * lax.axis_size("core")
    core = lax.axis_index("core")
    z = lax.axis_index("tensor")
    seq = token_ids.shape[1]
    rows = seq // 2
    scored = loss_pos.shape[1]
    half = scored // 2
    lines = embed.shape[0]
    padded = -(-lines // TILE) * TILE
    vocab = lines * CLASSES

    own_meta = jnp.concatenate([token_ids, loss_pos, targets, lengths], axis=1)
    other_meta = swapped(own_meta)
    meta = jnp.where(
        core == 0,
        jnp.stack([own_meta, other_meta], axis=1),
        jnp.stack([other_meta, own_meta], axis=1),
    ).reshape(n_tensor, -1)
    meta = jnp.stack(
        [
            lax.dynamic_index_in_dim(meta, (z - j) % n_tensor, 0, keepdims=False)
            for j in range(n_tensor)
        ]
    )
    ids = lax.dynamic_slice_in_dim(meta, core * rows, rows, 1)
    length = meta[:, seq + 2 * scored :]
    live = core * rows + jnp.arange(rows)[None, :] < length
    positions = lax.dynamic_slice_in_dim(meta, seq + core * half, half, 1)
    all_positions = meta[:, seq : seq + scored].reshape(n_tensor, 2, half).transpose(1, 0, 2)
    counted = (all_positions < length[None]).astype(f32).reshape(-1)
    all_wanted = meta[:, seq + scored : seq + 2 * scored].reshape(n_tensor, 2, half)
    all_wanted = all_wanted.transpose(1, 0, 2).reshape(1, -1)
    own_positions = meta[0, seq : seq + scored]

    def place(indices):
        local = indices - z * vocab
        return (local & 3) * padded + (local >> 2), (local >= 0) & (local < vocab)

    key, inside = place(ids)
    count = n_tensor * rows
    order = jnp.arange(rows)
    same = (ids[:, :, None] == ids[:, None, :]) & live[:, None, :]
    opening = jnp.min(jnp.where(same, order[None, None, :], rows), axis=2)
    fresh = live & (opening == order[None, :])
    hits = fresh & inside
    before = order[None, None, :] < opening[:, :, None]
    slots = jnp.sum((hits[:, None, :] & before).astype(jnp.int32), axis=2)
    fullest = jnp.max(jnp.sum(hits.astype(jnp.int32), axis=1))
    key = key * PAST + jnp.arange(n_tensor)[:, None] * rows + slots
    past = CLASSES * padded * PAST + jnp.arange(count)
    key = jnp.where(hits.reshape(count), key.reshape(count), past)
    owner = (ids[0] // vocab - z) % n_tensor
    alike = (owner[:, None] == owner[None, :]) & fresh[0][None, :] & before[0]
    spots = owner * rows + jnp.sum(alike.astype(jnp.int32), axis=1)

    def spots_at(offset):
        slot = spots % rows - offset
        here = live[0] & (slot >= 0) & (slot < CAP)
        return jnp.where(here, spots // rows * CAP + slot, n_tensor * CAP)

    every = jnp.arange(count)
    rank = jnp.sum((key[None, :] < key[:, None]).astype(jnp.int32), axis=1)
    keys = jnp.sum(jnp.where(rank[None, :] == every[:, None], key[None, :], 0), axis=1)
    edges = jnp.arange(16) * (padded // 2 * PAST)
    starts = jnp.sum((key[None, :] < edges[:, None]).astype(jnp.int32), axis=1)
    line = keys >> 11
    new = (every < starts[2 * CLASSES]) & (line != jnp.pad(line, (1, 0), constant_values=-1)[:-1])
    ranks = jnp.sum((new[None, :] & (every[None, :] <= every[:, None])).astype(jnp.int32), axis=1)
    ranks = ranks - 1
    opens = new[None, :] & (ranks[None, :] == every[:, None])
    distinct = jnp.sum(jnp.where(opens, line[None, :], 0), axis=1)
    bounds = starts[0 : 2 * CLASSES + 1 : 2]
    firsts = jnp.sum((new[None, :] & (every[None, :] < bounds[:, None])).astype(jnp.int32), axis=1)
    firsts = jnp.pad(firsts, (0, 8 - firsts.shape[0]))

    shared = relative(jnp.concatenate([distinct, firsts]))
    all_lines, all_firsts = shared[:, :count].reshape(-1), shared[:, count:].reshape(-1)
    most = jnp.max(firsts[1 : CLASSES + 1] - firsts[:CLASSES])
    most = jnp.pad(jnp.stack([most, fullest]), (0, LANES - 2))
    most = everywhere(most, ("core", "tensor", "chip"), jnp.maximum)
    most, fullest = most[0], most[1]

    low = jnp.pad(embed.astype(bf16), ((0, padded - lines), (0, 0)))
    halves = [lax.all_gather(low[: padded // 2], DP)]
    shares = [pack_layer(w_zx[i], w_bcdt[i], w_out[i]) for i in range(LAYERS)]
    inner = INNER // n_tensor
    heads = HEADS // n_tensor
    small = jnp.concatenate([channel, jnp.pad(per_head, ((0, 0), (0, 0), (0, inner - heads)))], 1)
    small = around(small, "tensor")
    channel_all = small[:, :, : CONV + 2].transpose(1, 2, 0, 3).reshape(LAYERS, CONV + 2, INNER)
    head_all = small[:, :, CONV + 2 :, :heads].transpose(1, 2, 0, 3).reshape(LAYERS, 3, HEADS)
    smalls = []
    for depth in range(LAYERS):
        headp = jnp.stack([head_all[depth, 0], -jnp.exp(head_all[depth, 1]), head_all[depth, 2]])
        smalls.append(
            (
                jnp.pad(channel_all[depth], ((0, 2), (0, 0))),
                jnp.pad(headp, ((0, 5), (0, LANES - HEADS))),
                jnp.pad(bc_conv[depth], ((0, 3), (0, 0))),
            )
        )

    ready = (shares[0], smalls, keys, starts, spots_at(0), ranks, all_lines, all_firsts, most, fullest)
    second, ready = lax.optimization_barrier((low[padded // 2 :], ready))
    share, smalls, keys, starts, spots_first, ranks, all_lines, all_firsts, most, fullest = ready
    halves.append(lax.all_gather(second, DP))
    share, _ = lax.optimization_barrier((share, halves))
    packed = [lax.all_gather(share, DP)]
    halves = [half.reshape(CLASSES, n_data // CLASSES, padded // 2, -1) for half in halves]
    found = lookup(keys, starts, halves)
    found = found.reshape(n_tensor, rows, D)
    gain_rows = [jnp.broadcast_to(gains[i][None, :], (8, D)) for i in range(LAYERS + 1)]

    def rows_in(offset, before):
        part = found[:, offset : offset + CAP]
        part = [part[0]] + [shifted(part[by], "tensor", -by) for by in range(1, n_tensor)]
        return place_rows(
            spots_at(offset) if offset else spots_first, jnp.stack(part), before, gain_rows[0]
        )

    resid, normed = rows_in(0, None)
    for offset in range(CAP, rows, CAP):
        resid, normed = lax.cond(
            fullest > offset,
            lambda so_far, offset=offset: tuple(rows_in(offset, so_far[0])),
            lambda so_far: so_far,
            (resid, normed),
        )
    for share in shares[1:]:
        share = lax.optimization_barrier((share, packed[-1], resid))[0]
        packed.append(lax.all_gather(share, DP))
    w_small = [unpack_bcdt(packed[depth]) for depth in range(LAYERS)]
    kept = []
    for depth in range(LAYERS):
        resid, normed, saved = layer_forward(
            resid, normed, gain_rows[depth + 1], packed[depth], w_small[depth], smalls[depth]
        )
        kept.append(saved)

    both = by_core(normed, swapped(normed))
    pick = (positions[0][:, None] == jnp.arange(seq)[None, :]).astype(bf16)
    chosen = around(nn(pick, both).astype(bf16), "tensor").reshape(n_tensor * half, D)
    chosen = by_core(chosen, swapped(chosen))
    want, known = place(all_wanted)
    want = jnp.broadcast_to(jnp.where(known, want, -1), (8, n_tensor * scored))
    which = core[None]
    stats = vocab_measure(which, halves, chosen, want, lines)[:3]
    ordered = in_order(stats.reshape(3, 2, n_tensor, half), 2)
    ordered = everywhere(ordered, ("core", "tensor"), lse_merge)
    stats = in_order(ordered, 2).reshape(3, -1)
    log_total = stats[0] + jnp.log(stats[1])
    losses = (counted * (log_total - stats[2])).reshape(2, n_tensor, half).sum(axis=2)
    loss_sum = jnp.sum(in_order(losses, 1))
    loss_count = jnp.sum(counted)
    info = jnp.pad(jnp.stack([log_total, counted]), ((0, 6), (0, 0)))
    dtable, dchosen = vocab_back(which, halves, chosen, want, info, lines)
    dtable = dtable.reshape((-1, 2) + dtable.shape[2:])
    table_part = lax.psum_scatter(dtable, "chip", scatter_dimension=0)

    dchosen = dchosen.reshape(2, n_tensor * half, D)
    mine = jnp.where(core == 0, dchosen[0], dchosen[1])
    other = jnp.where(core == 0, dchosen[1], dchosen[0])
    dchosen = mine.astype(f32) + swapped(other).astype(f32)
    dpicked = sum_back(dchosen.astype(bf16).reshape(n_tensor, half, D), "tensor").astype(bf16)
    dpicked = by_core(dpicked, swapped(dpicked))
    onto = (core * rows + jnp.arange(rows)[:, None] == own_positions[None, :]).astype(bf16)
    dresid, dfinal_gain = rms_back(nn(onto, dpicked), resid, gains[LAYERS])

    shares = [None] * LAYERS
    parts = [None] * LAYERS
    flats = []
    for depth in reversed(range(LAYERS)):
        dresid, grad, parts[depth], flats = layer_backward(
            dresid, kept[depth], gain_rows[depth], packed[depth], w_small[depth], smalls[depth],
            flats,
        )
        grad, table_part, dresid = lax.optimization_barrier((grad, table_part, dresid))
        shares[depth] = lax.psum_scatter(grad, DP, scatter_dimension=0, tiled=True)
        if depth > 0:
            flat = flat_layer(parts[depth], dfinal_gain if depth == LAYERS - 1 else None)
            flats = [everywhere(flat, ("core", "tensor", "chip"))] + flats

    def rows_out(part):
        return jnp.stack(
            [part[0]] + [shifted(part[by], "tensor", by) for by in range(1, n_tensor)]
        )

    sent = send_rows(spots_first, dresid, n_tensor)
    sent, table_part = lax.optimization_barrier((sent, table_part))
    arrived = jnp.pad(rows_out(sent), ((0, 0), (0, rows - CAP), (0, 0)))
    for offset in range(CAP, rows, CAP):
        arrived = lax.cond(
            fullest > offset,
            lambda so_far, offset=offset: lax.dynamic_update_slice(
                so_far,
                rows_out(send_rows(spots_at(offset), dresid, n_tensor)),
                (0, offset, 0),
            ),
            lambda so_far: so_far,
            arrived,
        )
    arrived = arrived.reshape(count, D)
    keep = jnp.where(core == 0, table_part[0], table_part[1])
    give = jnp.where(core == 0, table_part[1], table_part[0])
    table_part = by_core(keep, swapped(give))
    own = lax.axis_index(DP)
    cls = own // (n_data // CLASSES)

    def pack_round(offset):
        where = jnp.stack([own, offset])
        return pack_rows(keys, ranks, starts, firsts, where, arrived, n_data)

    def add_round(offset, recv, total):
        return tuple(add_rows(all_lines, all_firsts, jnp.stack([cls, offset]), recv, total))

    stacked = (False, True, True, True, True, True, True, False)
    everyone = n_tensor * n_data
    copies = (1, 1, n_tensor, 1, n_data, n_data, everyone, everyone)
    weights = (embed, w_zx, w_bcdt, w_out, channel, per_head, bc_conv, gains)
    outgoing, shares[1:], parts[0], late = lax.optimization_barrier(
        (pack_round(0), shares[1:], parts[0], weights)
    )
    recv = exchanged(outgoing)
    grads = [None] + [reduce_layer(share) for share in shares[1:]]
    flats = [everywhere(flat_layer(parts[0], None), ("core", "tensor", "chip"))] + flats
    weight_sq = jnp.concatenate(
        [group_squares(*pair) / shared_by for *pair, shared_by in zip(late, stacked, copies)]
    )
    recv, table_part, grads[1:], flats[0], weight_sq = lax.optimization_barrier(
        (recv, table_part, grads[1:], flats[0], weight_sq)
    )
    added = add_round(0, recv, table_part)
    added = lax.while_loop(
        lambda carry: carry[0] < most,
        lambda carry: (carry[0] + CAP, add_round(carry[0], exchanged(pack_round(carry[0])), carry[1][0])),
        (jnp.int32(CAP), added),
    )[1]
    grad_table, table_sq = added[0][:lines], jnp.sum(added[1])

    grads[0] = reduce_layer(shares[0])
    grad_zx, grad_out, grad_bcdt = (jnp.stack(parts) for parts in zip(*grads))
    small_grads = [unflat_layer(flat) for flat in flats]
    grad_gains = jnp.stack([part[0] for part in small_grads] + [small_grads[-1][4]])
    grad_channel, grad_head, grad_bc_conv = (
        jnp.stack([part[k] for part in small_grads]) for k in (1, 2, 3)
    )

    kinds = (
        (embed, embed_m, embed_v, grad_table),
        (w_zx, w_zx_m, w_zx_v, grad_zx),
        (w_bcdt, w_bcdt_m, w_bcdt_v, grad_bcdt),
        (w_out, w_out_m, w_out_v, grad_out),
        (channel, channel_m, channel_v, grad_channel),
        (per_head, per_head_m, per_head_v, grad_head),
        (bc_conv, bc_conv_m, bc_conv_v, grad_bc_conv),
        (gains, gains_m, gains_v, grad_gains),
    )
    kinds = [kind + pair for kind, pair in zip(kinds, zip(stacked, copies))]
    grad_sq = jnp.concatenate(
        [table_sq[None]] + [group_squares(kind[3], kind[4]) / kind[5] for kind in kinds[1:]]
    )
    groups = grad_sq.shape[0]
    totals = jnp.concatenate(
        [grad_sq, weight_sq, jnp.stack([loss_sum, loss_count]) / (2 * n_tensor)]
    )
    totals = everywhere(jnp.pad(totals, (0, LANES - totals.shape[0])), ("core", "tensor", "chip"))
    grad_sq, weight_sq = totals[:groups], totals[groups : 2 * groups]
    grad_norm = jnp.sqrt(jnp.sum(grad_sq))
    scale = jnp.minimum(1.0, clip_limit / grad_norm)
    rest = kinds[1:]
    sizes = [LAYERS if kind[4] else 1 for kind in rest]
    shares = [1.0 / kind[5] for kind, size in zip(rest, sizes) for _ in range(size)]
    turns = [(0, 1, 2, 3), (0, 2, 1), (0, 1, 2), (1, 0, 2), (1, 0, 2), (1, 0, 2), (0, 1)]
    axes = [0, 0, 0, 1, 1, 1, None]
    arrays = [array.transpose(turn) for kind, turn in zip(rest, turns) for array in kind[:4]]
    shapes = [arrays[4 * k].shape for k in range(len(rest))]
    *moved, squares = at_once(
        functools.partial(adapt_kernel, axes),
        scale[None],
        arrays,
        [shape for shape in shapes for _ in range(3)],
        [(groups - 1,)],
    )
    embed_moved = adapt(embed, embed_m, embed_v, grad_table * scale)
    step_sq = jnp.concatenate(
        [group_squares(embed_moved[2], False), squares * jnp.array(shares, f32)]
    )
    step_sq = everywhere(jnp.pad(step_sq, (0, LANES - groups)), ("core", "tensor", "chip"))[:groups]
    weight_norm = jnp.sqrt(weight_sq)
    step_norm = jnp.sqrt(step_sq)
    factors = learn_rate * (weight_norm / step_norm)
    stepped = at_once(
        functools.partial(step_kernel, axes),
        factors[1:],
        arrays[0::4] + moved[2::3],
        shapes,
        [],
    )
    results = [embed - factors[0] * embed_moved[2], embed_moved[0], embed_moved[1]]
    for k, turn in enumerate(turns):
        parts = (stepped[k], moved[3 * k], moved[3 * k + 1])
        results += [part.transpose(turn) for part in parts]
    group_norms = jnp.stack([weight_norm, step_norm])
    return (totals[2 * groups], totals[2 * groups + 1], grad_norm, group_norms, *results)


def solution(mesh):
    devices = mesh.devices.reshape(-1, 2, mesh.shape["tensor"])
    inside = Mesh(devices, ("chip", "core", "tensor"))
    by_data = P(None, DP)
    embed = (P("tensor", DP),) * 3
    w_zx = (P(None, DP, None, "tensor"),) * 3
    w_bcdt = (P(None, DP, None),) * 3
    w_out = (P(None, DP, "tensor"),) * 3
    by_tensor = (P(None, None, "tensor"),) * 6
    copied = (P(),) * 6
    states = embed + w_zx + w_bcdt + w_out + by_tensor + copied
    return jax.shard_map(
        body,
        mesh=inside,
        in_specs=(by_data,) * 4 + states,
        out_specs=(P(),) * 4 + states,
        check_vma=False,
    )
```

```python
import functools

import jax
import jax.numpy as jnp
from jax import lax
from jax.experimental import pallas as pl
from jax.experimental.pallas import tpu as pltpu
from jax.sharding import Mesh
from jax.sharding import PartitionSpec as P

D = 1024
INNER = 2048
HEADS = 32
HDIM = 64
STATE = 128
CONV = 4
LAYERS = 2
MICRO = 2
STEP = 5

BLOCK = 128
HALO = 16
WIDTH = 512
GROUPS = INNER // WIDTH
LANES = 128
TILE = 1600
CLASSES = 4
PAST = 1 << 11
CAP = 128

norm_eps = 1e-05
adam_eps = 1e-06
clip_limit = 1.0
first_decay = 0.5
second_decay = 0.5
learn_rate = 0.3
weight_decay = 0.01

f32 = jnp.float32
bf16 = jnp.bfloat16
full = lax.Precision.HIGHEST
DP = ("chip", "core")
VMEM_BYTES = 58 * 1024 * 1024


def dot(left, right, left_dim, right_dim, precision=None):
    return lax.dot_general(
        left,
        right,
        (((left_dim,), (right_dim,)), ((), ())),
        precision=precision,
        preferred_element_type=f32,
    )


def nn(left, right, precision=None):
    return dot(left, right, 1, 0, precision)


def nt(left, right, precision=None):
    return dot(left, right, 1, 1, precision)


def tn(left, right, precision=None):
    return dot(left, right, 0, 0, precision)


def sigmoid(v):
    return 0.5 * jnp.tanh(0.5 * v) + 0.5


def small_sigmoid(v):
    return 1.0 / (1.0 + jnp.exp(-v))


def softplus(v):
    return jnp.maximum(v, 0.0) + jnp.log1p(jnp.exp(-jnp.abs(v)))


def normed(values, gain):
    inverse = lax.rsqrt(jnp.mean(values * values, axis=1, keepdims=True) + norm_eps)
    return (values * inverse * gain).astype(bf16)


def iota(shape, axis):
    return lax.broadcasted_iota(jnp.int32, shape, axis)


def call(kernel, grid, in_specs, out_specs, out_shape, scratch, prefetch=0, flops=0, bytes_moved=0):
    return pl.pallas_call(
        kernel,
        grid_spec=pltpu.PrefetchScalarGridSpec(
            num_scalar_prefetch=prefetch,
            grid=grid,
            in_specs=in_specs,
            out_specs=out_specs,
            scratch_shapes=scratch,
        ),
        out_shape=out_shape,
        compiler_params=pltpu.CompilerParams(
            vmem_limit_bytes=VMEM_BYTES, dimension_semantics=("arbitrary",) * len(grid)
        ),
        cost_estimate=pl.CostEstimate(
            flops=flops, bytes_accessed=bytes_moved, transcendentals=0
        ),
    )


def whole(shape):
    return pl.BlockSpec(shape, lambda *_: (0,) * len(shape))


def packed_zx(packed):
    rows = D // packed.shape[0]
    return pl.BlockSpec((packed.shape[0], rows, D), lambda g: (0, g, 0))


def unpacked_out(ref, low, rows):
    lines = ref[:, low : low + rows // 2, :]
    both = jnp.concatenate([lines[:, :, :WIDTH], lines[:, :, WIDTH:]], axis=1)
    return both.reshape(D, WIDTH)


def columns(rows, width=WIDTH, at=0):
    return pl.BlockSpec((rows, width), lambda g: (0, g + at))


def struct(shape, dtype=f32):
    return jax.ShapeDtypeStruct(shape, dtype)


def conv_rows(ref, taps, rows, low, width):
    result = taps[CONV : CONV + 1, :]
    for j in range(CONV):
        start = HALO - CONV + 1 + j
        result = result + ref[start : start + rows, low : low + width] * taps[j : j + 1, :]
    return result


def triangle():
    return iota((BLOCK, BLOCK), 0) >= iota((BLOCK, BLOCK), 1)


def expanded(values, marks, parts=3, by=nn):
    result = None
    for _ in range(parts):
        part = values.astype(bf16)
        values = values - part.astype(f32)
        term = by(part, marks)
        result = term if result is None else result + term
    return result


def spread(group):
    head = iota((LANES, WIDTH), 0)
    lane = iota((LANES, WIDTH), 1)
    return (head == group * (WIDTH // HDIM) + lane // HDIM).astype(bf16)


def small_parts(rows, bcdt, headp, bcv, s_b, s_c, s_dt, s_cum, s_cumt, s_g):
    pre = conv_rows(bcdt, bcv, rows, 0, 2 * STATE)
    bc = (pre * sigmoid(pre)).astype(bf16)
    s_b[...] = bc[:, :STATE]
    s_c[...] = bc[:, STATE:]
    dt = softplus(bcdt[HALO:, 2 * STATE :] + headp[0:1, :])
    s_dt[...] = dt
    decay = headp[1:2, :] * dt
    keep = triangle()
    lower = keep.astype(f32)
    for b in range(rows // BLOCK):
        r = slice(b * BLOCK, (b + 1) * BLOCK)
        cum = nn(lower, decay[r], full)
        s_cum[r, :] = cum
        s_cumt[:, r] = cum.T
        s_g[b] = jnp.where(keep, nt(bc[r, STATE:], bc[r, :STATE]), 0.0)


def head_rows(s_cumt, group, r):
    heads = WIDTH // HDIM
    return s_cumt[pl.ds(pl.multiple_of(group * heads, heads), heads), r]


def fading(cum_e, cum_rows, head):
    column = cum_e[:, head * HDIM : head * HDIM + 1]
    return jnp.exp(jnp.minimum(column - cum_rows[head : head + 1, :], 0.0))


def one_head(values, j):
    first = iota(values.shape, 1) < HDIM
    return jnp.where(first if j == 0 else jnp.logical_not(first), values, 0.0).astype(bf16)


def small_scratch(rows):
    return [
        pltpu.VMEM((rows, STATE), bf16),
        pltpu.VMEM((rows, STATE), bf16),
        pltpu.VMEM((rows, LANES), f32),
        pltpu.VMEM((rows, LANES), f32),
        pltpu.VMEM((LANES, rows), f32),
        pltpu.VMEM((rows // BLOCK, BLOCK, BLOCK), f32),
    ]


def scan_kernel(
    nx, w_zx, wb, chan, headp, bcv,
    y_o, gate_o, xraw_o, st_o, bcdt_o, c_o, ecf_o,
    s_b, s_c, s_dt, s_cum, s_cumt, s_g,
):
    rows = y_o.shape[0]
    group = pl.program_id(0)

    @pl.when(group == 0)
    def _():
        bcdt_o[...] = nn(nx[...], wb[...])
        small_parts(rows, bcdt_o, headp, bcv, s_b, s_c, s_dt, s_cum, s_cumt, s_g)
        c_o[...] = s_c[...]
        run = jnp.zeros((1, LANES), f32)
        for b in range(rows // BLOCK):
            r = slice(b * BLOCK, (b + 1) * BLOCK)
            ecf_o[r, :] = jnp.exp(s_cum[r, :] + run)
            run = run + s_cum[(b + 1) * BLOCK - 1 : (b + 1) * BLOCK, :]

    both = w_zx[...].reshape(D, 2 * WIDTH)
    gate_o[...] = nn(nx[HALO:, :], both[:, :WIDTH])
    xraw_o[...] = nn(nx[...], both[:, WIDTH:])
    pre = conv_rows(xraw_o, chan, rows, 0, WIDTH)
    xc = pre * sigmoid(pre)
    expand = spread(group)
    u = xc * expanded(s_dt[...], expand)
    skip = expanded(headp[...], expand)[2:3, :]
    state = jnp.zeros((STATE, WIDTH), f32)
    for b in range(rows // BLOCK):
        r = slice(b * BLOCK, (b + 1) * BLOCK)
        cum_e = expanded(s_cum[r, :], expand)
        total = cum_e[BLOCK - 1 : BLOCK, :]
        keys, reads = s_b[r, :], s_c[r, :]
        y = jnp.exp(cum_e) * nn(reads, state.astype(bf16)) + skip * xc[r]
        cum_rows = head_rows(s_cumt, group, r)
        pieces = []
        for pair in range(WIDTH // LANES):
            both = u[r, pair * LANES : (pair + 1) * LANES]
            piece = jnp.zeros((BLOCK, LANES), f32)
            for j in range(2):
                weights = (fading(cum_e, cum_rows, 2 * pair + j) * s_g[b]).astype(bf16)
                piece = piece + nn(weights, one_head(both, j))
            pieces.append(piece)
        y_o[r, :] = y + jnp.concatenate(pieces, axis=1)
        fresh = tn(keys, (u[r] * jnp.exp(total - cum_e)).astype(bf16))
        state = state * jnp.exp(total) + fresh
    st_o[...] = state


def scan_front(nx, packed, wb, chan, headp, bcv):
    ext = nx.shape[0]
    rows = ext - HALO
    return call(
        scan_kernel,
        (GROUPS,),
        [
            whole((ext, D)),
            packed_zx(packed),
            whole(wb.shape),
            columns(8),
            whole((8, LANES)),
            whole((8, 2 * STATE)),
        ],
        [
            columns(rows),
            columns(rows),
            columns(ext),
            columns(STATE),
            whole((ext, 384)),
            whole((rows, STATE)),
            whole((rows, LANES)),
        ],
        [
            struct((rows, INNER)),
            struct((rows, INNER)),
            struct((ext, INNER)),
            struct((STATE, INNER)),
            struct((ext, 384)),
            struct((rows, STATE), bf16),
            struct((rows, LANES)),
        ],
        small_scratch(rows),
        flops=2 * ext * D * 2 * INNER,
        bytes_moved=2 * D * 2 * INNER + 12 * rows * INNER,
    )(nx, packed, wb, chan, headp, bcv)


def join_kernel(
    y, gate, c, ecf, st, chan, wout, resid, gain,
    yf_o, scaled_o, inv_o, res_o, normed_o, s_gated, s_square,
):
    group = pl.program_id(0)
    ecf_e = expanded(ecf[...], spread(group))
    yf = y[...] + ecf_e * nn(c[...], st[...].astype(bf16))
    yf_o[...] = yf
    gated = yf * (gate[...] * sigmoid(gate[...]))
    s_gated[group] = gated
    part = jnp.broadcast_to(jnp.sum(gated * gated, axis=1, keepdims=True), s_square.shape)

    @pl.when(group == 0)
    def _():
        s_square[...] = part

    @pl.when(group > 0)
    def _():
        s_square[...] += part

    @pl.when(group == GROUPS - 1)
    def _():
        inverse = lax.rsqrt(s_square[...] / INNER + norm_eps)
        inv_o[...] = inverse
        res = resid[...]
        for q in range(GROUPS):
            at = slice(q * WIDTH, (q + 1) * WIDTH)
            scaled = (s_gated[q] * inverse[:, :1] * chan[CONV + 1 : CONV + 2, at]).astype(bf16)
            scaled_o[:, at] = scaled
            height = D // wout.shape[0]
            res = res + nt(scaled, unpacked_out(wout, q * height // 2, height))
        res_o[...] = res
        normed_o[...] = normed(res, gain[0:1, :])


def scan_join(y, gate, c, ecf, st, chan, packed, resid, gain):
    rows = y.shape[0]
    height = D // packed.shape[0]
    return call(
        join_kernel,
        (GROUPS,),
        [
            columns(rows),
            columns(rows),
            whole((rows, STATE)),
            whole((rows, LANES)),
            columns(STATE),
            whole((8, INNER)),
            pl.BlockSpec((packed.shape[0], 2 * height, D), lambda g: (0, 2, 0)),
            whole((rows, D)),
            whole((8, D)),
        ],
        [columns(rows), whole((rows, INNER)), whole((rows, LANES))] + [whole((rows, D))] * 2,
        [
            struct((rows, INNER)),
            struct((rows, INNER), bf16),
            struct((rows, LANES)),
            struct((rows, D)),
            struct((rows, D), bf16),
        ],
        [pltpu.VMEM((GROUPS, rows, WIDTH), f32), pltpu.VMEM((rows, LANES), f32)],
        flops=2 * rows * D * INNER,
        bytes_moved=2 * D * INNER + 14 * rows * INNER,
    )(y, gate, c, ecf, st, chan, packed, resid, gain)


def unjoin_kernel(
    dout, wout, y, gate, inv, c, ecf, chan, dy_o, dgate_o, dgain_o, ds_o, s_scaled, s_along
):
    phase = pl.program_id(0)
    group = pl.program_id(1)
    gain = chan[CONV + 1 : CONV + 2, :]
    raw = gate[...]
    sig = sigmoid(raw)
    opened = raw * sig
    gated = y[...] * opened
    inverse = inv[:, :1]

    @pl.when(phase == 0)
    def _():
        dscaled = nn(dout[...], unpacked_out(wout, 0, D // wout.shape[0]))
        s_scaled[group] = dscaled
        part = jnp.sum(dscaled * gain * gated, axis=1, keepdims=True)
        part = jnp.broadcast_to(part, s_along.shape)

        @pl.when(group == 0)
        def _():
            s_along[...] = part

        @pl.when(group > 0)
        def _():
            s_along[...] += part

    @pl.when(phase == 1)
    def _():
        dscaled = s_scaled[group]
        pulled = inverse * inverse * inverse * s_along[:, :1] / INNER
        dgated = inverse * gain * dscaled - gated * pulled
        dgain = jnp.sum(dscaled * gated * inverse, axis=0, keepdims=True)
        dgain_o[...] = jnp.broadcast_to(dgain, dgain_o.shape)
        dy = dgated * opened
        dy_o[...] = dy
        dgate_o[...] = (dgated * y[...] * (sig * (1.0 + raw * (1.0 - sig)))).astype(bf16)
        ecf_e = expanded(ecf[...], spread(group))
        ds_o[...] = tn(c[...], (ecf_e * dy).astype(bf16))


def scan_unjoin(dout, packed, y, gate, inv, c, ecf, chan):
    rows = y.shape[0]
    shares = packed.shape[0]

    def both(height):
        return pl.BlockSpec((height, WIDTH), lambda p, g: (0, g))

    def second(height):
        return pl.BlockSpec((height, WIDTH), lambda p, g: (0, g * p))

    return call(
        unjoin_kernel,
        (2, GROUPS),
        [
            whole((rows, D)),
            pl.BlockSpec(
                (shares, D // shares // 2, D),
                lambda p, g: (0, 2 * GROUPS + jnp.where(p == 0, g, GROUPS - 1), 0),
            ),
            both(rows),
            both(rows),
            whole((rows, LANES)),
            whole((rows, STATE)),
            whole((rows, LANES)),
            both(8),
        ],
        [second(rows), second(rows), second(8), second(STATE)],
        [
            struct((rows, INNER)),
            struct((rows, INNER), bf16),
            struct((8, INNER)),
            struct((STATE, INNER)),
        ],
        [pltpu.VMEM((GROUPS, rows, WIDTH), f32), pltpu.VMEM((rows, LANES), f32)],
        flops=2 * rows * D * INNER,
        bytes_moved=2 * D * INNER + 22 * rows * INNER,
    )(dout, packed, y, gate, inv, c, ecf, chan)


def head_sums(values, expand):
    if values.shape[0] == 1:
        return head_sums(jnp.broadcast_to(values, (8, values.shape[1])), expand)[0:1, :]
    return expanded(values, expand, by=nt)


def conv_back(ref, taps, pad, rows, low, width, taps_o, main, halo):
    grads = [jnp.sum(pad[HALO : HALO + rows, :] * ref[HALO - 3 + j : HALO - 3 + j + rows,
             low : low + width], axis=0, keepdims=True) for j in range(CONV)]
    grads.append(jnp.sum(pad[HALO : HALO + rows, :], axis=0, keepdims=True))
    taps_o[...] = jnp.concatenate(grads + [jnp.zeros((3, width), f32)], axis=0)
    total = jnp.zeros((HALO + rows, width), f32)
    for j in range(CONV):
        shift = CONV - 1 - j
        total = total + pad[shift : shift + HALO + rows, :] * taps[j : j + 1, :]
    halo(total[:HALO])
    main(total[HALO:])


def back_kernel(
    xraw, dy, bcdt, st, dst, chan, headp, bcv,
    dx_o, tail_o, halo_o, dchan_o, dbc_o, dbch_o, dheadp_o, dbcv_o,
    s_b, s_c, s_dt, s_cum, s_cumt, s_g,
    s_db, s_dc, s_dcum, s_ddt, s_dtot, s_dg, s_skip, s_pad, s_state, s_bcpad, s_cume,
):
    rows = dy.shape[0]
    blocks = rows // BLOCK
    group = pl.program_id(0)

    @pl.when(group == 0)
    def _():
        small_parts(rows, bcdt, headp, bcv, s_b, s_c, s_dt, s_cum, s_cumt, s_g)
        for ref in (s_db, s_dc, s_dcum, s_ddt, s_dtot, s_dg, s_skip, s_pad, s_bcpad):
            ref[...] = jnp.zeros(ref.shape, f32)

    pre = conv_rows(xraw, chan, rows, 0, WIDTH)
    sig = sigmoid(pre)
    xc = pre * sig
    expand = spread(group)
    dt_e = expanded(s_dt[...], expand)
    u = xc * dt_e
    skip = expanded(headp[...], expand)[2:3, :]
    state = st[...]
    for b in range(blocks):
        r = slice(b * BLOCK, (b + 1) * BLOCK)
        s_state[b] = state
        cum_e = expanded(s_cum[r, :], expand)
        s_cume[r, :] = cum_e
        if b < blocks - 1:
            total = cum_e[BLOCK - 1 : BLOCK, :]
            fresh = tn(s_b[r, :], (u[r] * jnp.exp(total - cum_e)).astype(bf16))
            state = state * jnp.exp(total) + fresh
    dstate = dst[...]
    dskip = jnp.zeros((1, WIDTH), f32)
    for b in reversed(range(blocks)):
        r = slice(b * BLOCK, (b + 1) * BLOCK)
        cum_e = s_cume[r, :]
        total = cum_e[BLOCK - 1 : BLOCK, :]
        keys, reads = s_b[r, :], s_c[r, :]
        to_here, to_end, passed = jnp.exp(cum_e), jnp.exp(total - cum_e), jnp.exp(total)
        u_b, dy_b = u[r], dy[r, :]
        u_low, dy_low = u_b.astype(bf16), dy_b.astype(bf16)
        state_low, dstate_low = s_state[b].astype(bf16), dstate.astype(bf16)
        faded = (dy_b * to_here).astype(bf16)
        y_across = to_here * nn(reads, state_low)
        s_dc[r, :] += nt(faded, state_low)
        du_across = to_end * nn(keys, dstate_low)
        s_db[r, :] += nt((u_b * to_end).astype(bf16), dstate_low)
        cum_rows = head_rows(s_cumt, group, r)
        y_pieces, du_pieces = [], []
        dscores = jnp.zeros((BLOCK, BLOCK), f32)
        for pair in range(WIDTH // LANES):
            at = slice(pair * LANES, (pair + 1) * LANES)
            y_piece = jnp.zeros((BLOCK, LANES), f32)
            du_piece = jnp.zeros((BLOCK, LANES), f32)
            for j in range(2):
                fade = fading(cum_e, cum_rows, 2 * pair + j)
                weights = (fade * s_g[b]).astype(bf16)
                dy_head = one_head(dy_b[:, at], j)
                y_piece = y_piece + nn(weights, one_head(u_b[:, at], j))
                du_piece = du_piece + tn(weights, dy_head)
                dscores = dscores + nt(dy_head, u_low[:, at]) * fade
            y_pieces.append(y_piece)
            du_pieces.append(du_piece)
        y_within = jnp.concatenate(y_pieces, axis=1)
        du_within = jnp.concatenate(du_pieces, axis=1)
        s_dg[b] += dscores
        du = du_within + du_across
        moved = u_b * du_across
        dcum = dy_low.astype(f32) * y_within + dy_b * y_across
        dcum = dcum - u_low.astype(f32) * du_within - moved
        s_dcum[r, :] += head_sums(dcum, expand)
        dtotal = jnp.sum(moved, axis=0, keepdims=True)
        dtotal = dtotal + passed * jnp.sum(s_state[b] * dstate, axis=0, keepdims=True)
        s_dtot[b : b + 1, :] += head_sums(dtotal, expand)
        s_ddt[r, :] += head_sums(du * xc[r], expand)
        dskip = dskip + jnp.sum(dy_b * xc[r], axis=0, keepdims=True)
        dxc = du * dt_e[r] + skip * dy_b
        s_pad[HALO + b * BLOCK : HALO + (b + 1) * BLOCK, :] = dxc * (
            sig[r] * (1.0 + pre[r] * (1.0 - sig[r]))
        )
        dstate = passed * dstate + tn(reads, faded)
    s_skip[0:1, :] += head_sums(dskip, expand)

    def put_main(values):
        dx_o[...] = values.astype(bf16)
        tail_o[...] = values[rows - HALO :]

    def put_halo(values):
        halo_o[...] = values

    conv_back(xraw, chan, s_pad, rows, 0, WIDTH, dchan_o, put_main, put_halo)

    @pl.when(group == GROUPS - 1)
    def _():
        keep = triangle()
        upper = (iota((BLOCK, BLOCK), 0) <= iota((BLOCK, BLOCK), 1)).astype(f32)
        rate = headp[1:2, :]
        bias_sum = jnp.zeros((1, LANES), f32)
        rate_sum = jnp.zeros((1, LANES), f32)
        for b in range(blocks):
            r = slice(b * BLOCK, (b + 1) * BLOCK)
            dscores = jnp.where(keep, s_dg[b], 0.0).astype(bf16)
            s_dc[r, :] += nn(dscores, s_b[r, :])
            s_db[r, :] += tn(dscores, s_c[r, :])
            da = nn(upper, s_dcum[r, :], full) + s_dtot[b : b + 1, :]
            ddt = s_ddt[r, :] + da * rate
            rate_sum = rate_sum + jnp.sum(da * (rate * s_dt[r, :]), axis=0, keepdims=True)
            raw = bcdt[HALO + b * BLOCK : HALO + (b + 1) * BLOCK, 2 * STATE :] + headp[0:1, :]
            ddt = ddt * small_sigmoid(raw)
            bias_sum = bias_sum + jnp.sum(ddt, axis=0, keepdims=True)
            dbc_o[r, 2 * STATE :] = ddt
        dheadp_o[...] = jnp.concatenate(
            [bias_sum, rate_sum, s_skip[0:1, :], jnp.zeros((5, LANES), f32)], axis=0
        )
        bc_pre = conv_rows(bcdt, bcv, rows, 0, 2 * STATE)
        bc_sig = sigmoid(bc_pre)
        turn = bc_sig * (1.0 + bc_pre * (1.0 - bc_sig))
        s_bcpad[HALO : HALO + rows, :STATE] = s_db[...] * turn[:, :STATE]
        s_bcpad[HALO : HALO + rows, STATE:] = s_dc[...] * turn[:, STATE:]

        def put_bc(values):
            dbc_o[:, : 2 * STATE] = values

        def put_bc_halo(values):
            dbch_o[...] = values

        conv_back(bcdt, bcv, s_bcpad, rows, 0, 2 * STATE, dbcv_o, put_bc, put_bc_halo)


def scan_back(xraw, dy, bcdt, st, dst, chan, headp, bcv):
    rows = dy.shape[0]
    ext = rows + HALO
    blocks = rows // BLOCK
    return call(
        back_kernel,
        (GROUPS,),
        [
            columns(ext),
            columns(rows),
            whole((ext, 384)),
            columns(STATE),
            columns(STATE),
            columns(8),
            whole((8, LANES)),
            whole((8, 2 * STATE)),
        ],
        [
            columns(rows),
            columns(HALO),
            columns(HALO),
            columns(8),
            whole((rows, 384)),
            whole((HALO, 2 * STATE)),
            whole((8, LANES)),
            whole((8, 2 * STATE)),
        ],
        [
            struct((rows, INNER), bf16),
            struct((HALO, INNER)),
            struct((HALO, INNER)),
            struct((8, INNER)),
            struct((rows, 384)),
            struct((HALO, 2 * STATE)),
            struct((8, LANES)),
            struct((8, 2 * STATE)),
        ],
        small_scratch(rows)
        + [
            pltpu.VMEM((rows, STATE), f32),
            pltpu.VMEM((rows, STATE), f32),
            pltpu.VMEM((rows, LANES), f32),
            pltpu.VMEM((rows, LANES), f32),
            pltpu.VMEM((8, LANES), f32),
            pltpu.VMEM((blocks, BLOCK, BLOCK), f32),
            pltpu.VMEM((8, LANES), f32),
            pltpu.VMEM((rows + 2 * HALO, WIDTH), f32),
            pltpu.VMEM((blocks, STATE, WIDTH), f32),
            pltpu.VMEM((rows + 2 * HALO, 2 * STATE), f32),
            pltpu.VMEM((rows, WIDTH), f32),
        ],
        flops=20 * rows * INNER * STATE,
        bytes_moved=12 * rows * INNER,
    )(xraw, dy, bcdt, st, dst, chan, headp, bcv)


SHARE = 3 * WIDTH + LANES


def grads_kernel(
    normed, dout, dgate, dx, tail, back, dbcdt, bc_back, scaled, w_zx, wb, resid, dresid, gain,
    packed_o, dres_o, dgain_o, s_bc, s_sum,
):
    rows = normed.shape[0]
    group = pl.program_id(0)
    edge = slice(rows - HALO, rows)

    @pl.when(group == 0)
    def _():
        s_bc[GROUPS - 1] = jnp.zeros((rows, LANES), bf16)
        for q in range(3):
            at = slice(q * LANES, (q + 1) * LANES)
            s_bc[q] = dbcdt[:, at].astype(bf16)
            if q < 2:
                s_bc[q, edge, :] = (dbcdt[edge, at] + bc_back[:, at]).astype(bf16)
        total = nt(s_bc[0], wb[:, :LANES])
        total = total + nt(s_bc[1], wb[:, LANES : 2 * LANES])
        s_sum[...] = total + nt(s_bc[2], wb[:, 2 * LANES :])

    fixed = (tail[...] + back[...]).astype(bf16)
    dzx = jnp.concatenate(
        [dgate[...], jnp.concatenate([dx[: rows - HALO, :], fixed], axis=0)], axis=1
    )
    s_sum[...] += nt(dzx, w_zx[...].reshape(D, 2 * WIDTH))
    packed_o[:, : 2 * WIDTH] = tn(normed[...], dzx).astype(bf16)
    packed_o[:, 2 * WIDTH : 3 * WIDTH] = tn(dout[...], scaled[...]).astype(bf16)
    packed_o[:, 3 * WIDTH :] = tn(normed[...], s_bc[group]).astype(bf16)

    @pl.when(group == GROUPS - 1)
    def _():
        values, grad, weight = resid[...], s_sum[...], gain[0:1, :]
        inverse = lax.rsqrt(jnp.mean(values * values, axis=1, keepdims=True) + norm_eps)
        along = jnp.mean(grad * weight * values, axis=1, keepdims=True)
        pulled = inverse * inverse * inverse * along
        dres_o[...] = dresid[...] + inverse * weight * grad - values * pulled
        dgain = jnp.sum(grad * values * inverse, axis=0, keepdims=True)
        dgain_o[...] = jnp.broadcast_to(dgain, dgain_o.shape)


def layer_grads(
    normed, dout, dgate, dx, tail, back, dbcdt, bc_back, scaled, packed, wb, resid, dresid, gain
):
    rows = normed.shape[0]
    return call(
        grads_kernel,
        (GROUPS,),
        [
            whole((rows, D)),
            whole((rows, D)),
            columns(rows),
            columns(rows),
            columns(HALO),
            columns(HALO),
            whole((rows, 384)),
            whole((HALO, 2 * STATE)),
            columns(rows),
            packed_zx(packed),
            whole(wb.shape),
            whole((rows, D)),
            whole((rows, D)),
            whole((8, D)),
        ],
        [columns(D, SHARE), whole((rows, D)), whole((8, D))],
        [struct((D, GROUPS * SHARE), bf16), struct((rows, D)), struct((8, D))],
        [pltpu.VMEM((GROUPS, rows, LANES), bf16), pltpu.VMEM((rows, D), f32)],
        flops=10 * rows * D * INNER,
        bytes_moved=26 * D * INNER,
    )(normed, dout, dgate, dx, tail, back, dbcdt, bc_back, scaled, packed, wb, resid, dresid, gain)


def lookup_kernel(keys, edges, first, second, out, s_rows):
    cls = pl.program_id(0)
    parts, lines, width = first.shape[1:]

    @pl.when(cls == 0)
    def _():
        s_rows[...] = jnp.zeros(s_rows.shape, f32)

    place = iota((16, width), 0)
    for half, table in enumerate((first, second)):

        def turn(i, carry, half=half, table=table):
            key = keys[i]
            at = key & (PAST - 1)
            line = (key >> 11) - (2 * cls + half) * lines
            base = pl.multiple_of((line >> 4) << 4, 16)
            found = []
            for part in range(parts):
                tile = table[0, part, pl.ds(base, 16), :].astype(f32)
                found.append(
                    jnp.sum(jnp.where(place == (line & 15), tile, 0.0), axis=0, keepdims=True)
                )
            s_rows[pl.ds(at, 1), :] = jnp.concatenate(found, axis=1)
            return carry

        lax.fori_loop(edges[2 * cls + half], edges[2 * cls + half + 1], turn, 0)

    @pl.when(cls == CLASSES - 1)
    def _():
        out[...] = s_rows[...].astype(bf16)


def lookup(keys, edges, halves):
    count = keys.shape[0]
    spec = pl.BlockSpec((1,) + halves[0].shape[1:], lambda c, *_: (c, 0, 0, 0))
    return call(
        lookup_kernel,
        (CLASSES,),
        [spec, spec],
        whole((count, D)),
        struct((count, D), bf16),
        [pltpu.VMEM((count, D), f32)],
        prefetch=2,
        bytes_moved=4 * halves[0].size,
    )(keys, edges, *halves)


def place_kernel(spots, packed, *refs):
    *before, gain, out, normed_o, s_packed = refs
    cap = packed.shape[1]
    for j in range(packed.shape[0]):
        s_packed[j * cap : (j + 1) * cap, :] = packed[j].astype(f32)
    s_packed[packed.shape[0] * cap :, :] = jnp.zeros((8, D), f32)

    def turn(i, carry):
        out[pl.ds(i, 1), :] = s_packed[pl.ds(spots[i], 1), :]
        return carry

    lax.fori_loop(0, out.shape[0], turn, 0, unroll=8)
    if before:
        out[...] += before[0][...]
    normed_o[...] = normed(out[...], gain[0:1, :])


def place_rows(spots, packed, before, gain):
    rows = spots.shape[0]
    more = [] if before is None else [before]
    return call(
        place_kernel,
        (1,),
        [whole(packed.shape)] + [whole((rows, D)) for _ in more] + [whole((8, D))],
        [whole((rows, D))] * 2,
        [struct((rows, D)), struct((rows, D), bf16)],
        [pltpu.VMEM((packed.shape[0] * packed.shape[1] + 8, D), f32)],
        prefetch=1,
        bytes_moved=4 * rows * D,
    )(spots, packed, *more, gain)


def send_kernel(spots, grads, out, s_packed):
    cap = out.shape[1]
    s_packed[...] = jnp.zeros(s_packed.shape, f32)

    def turn(i, carry):
        s_packed[pl.ds(spots[i], 1), :] += grads[pl.ds(i, 1), :]
        return carry

    lax.fori_loop(0, grads.shape[0], turn, 0, unroll=8)
    for j in range(out.shape[0]):
        out[j] = s_packed[j * cap : (j + 1) * cap, :].astype(bf16)


def send_rows(spots, grads, n_tensor):
    shape = (n_tensor, CAP, D)
    return call(
        send_kernel,
        (1,),
        [whole(grads.shape)],
        whole(shape),
        struct(shape, bf16),
        [pltpu.VMEM((n_tensor * CAP + 8, D), f32)],
        prefetch=1,
        bytes_moved=8 * grads.size,
    )(spots, grads)


def pack_kernel(keys, ranks, starts, firsts, where, rows, out, s_rows, s_out):
    own, offset = where[0], where[1]
    cap, width = out.shape[1:]
    parts = D // width
    s_rows[...] = rows[...].astype(f32)
    s_out[...] = jnp.zeros(s_out.shape, f32)
    for cls in range(CLASSES):

        def turn(i, carry, cls=cls):
            row = s_rows[pl.ds(keys[i] & (PAST - 1), 1), :]
            slot = ranks[i] - firsts[cls] - offset
            slot = jnp.where((slot >= 0) & (slot < cap), slot, cap)
            for part in range(parts):
                piece = row[:, part * width : (part + 1) * width]
                s_out[own ^ (cls * parts + part), pl.ds(slot, 1), :] += piece
            return carry

        lax.fori_loop(starts[2 * cls], starts[2 * cls + 2], turn, 0)
    out[...] = s_out[:, :cap, :].astype(bf16)


def pack_rows(keys, ranks, starts, firsts, where, rows, n_data):
    count = keys.shape[0]
    shape = (n_data, CAP, D * CLASSES // n_data)
    return call(
        pack_kernel,
        (1,),
        [whole((count, D))],
        whole(shape),
        struct(shape, bf16),
        [pltpu.VMEM((count, D), f32), pltpu.VMEM((n_data, CAP + 8, shape[2]), f32)],
        prefetch=5,
        bytes_moved=2 * count * D,
    )(keys, ranks, starts, firsts, where, rows)


def add_kernel(keys, starts, where, packed, base, out, square, s_packed):
    cls, offset = where[0], where[1]
    lines = base.shape[0]
    count = keys.shape[0] // packed.shape[0]
    cap = packed.shape[1]
    s_packed[...] = packed[...].astype(f32)
    out[...] = base[...].astype(f32)
    for r in range(packed.shape[0]):
        first = starts[8 * r + cls] + offset

        def turn(i, carry):
            line = keys[r * count + i] - cls * lines
            out[pl.ds(line, 1), :] += s_packed[r, pl.ds(i - first, 1), :]
            return carry

        lax.fori_loop(first, jnp.minimum(starts[8 * r + cls + 1], first + cap), turn, 0)
    square[...] = jnp.zeros(square.shape, f32)
    for low in range(0, lines, TILE):
        part = out[low : low + TILE, :]
        square[0:1, :] += jnp.sum(part * part, axis=0, keepdims=True)


def add_rows(keys, starts, where, packed, base):
    return call(
        add_kernel,
        (1,),
        [whole(packed.shape), whole(base.shape)],
        [whole(base.shape), whole((8, base.shape[1]))],
        [struct(base.shape), struct((8, base.shape[1]))],
        [pltpu.VMEM(packed.shape, f32)],
        prefetch=3,
        bytes_moved=8 * base.size,
    )(keys, starts, where, packed, base)


def tile_lines(core, height):
    return (core[0] * pl.num_programs(1) + pl.program_id(1)) * height


def tile_logits(core, table, chosen, real):
    parts, height, width = table.shape[1:]
    result = nt(table[0, 0], chosen[:, :width])
    for part in range(1, parts):
        result = result + nt(table[0, part], chosen[:, part * width : (part + 1) * width])
    line = tile_lines(core, height) + iota(result.shape, 0)
    return jnp.where(line < real, result, -1e30)


def tile_hit(core, table, lines, wanted):
    height = table.shape[2]
    first = pl.program_id(0) * lines + tile_lines(core, height)
    return iota((height, wanted.shape[1]), 0) == wanted[0:1, :] - first


def one_half(core, first, second):
    return jnp.where(core[0] == 0, first[...], second[...])


def measure_kernel(real, lines, core, first_half, second_half, chosen, wanted, out, s_stats):
    table = one_half(core, first_half, second_half)
    first = (pl.program_id(0) == 0) & (pl.program_id(1) == 0)

    @pl.when(first)
    def _():
        s_stats[0:1, :] = jnp.full((1, s_stats.shape[1]), -1e30, f32)
        s_stats[1:8, :] = jnp.zeros((7, s_stats.shape[1]), f32)

    old, total, picked = s_stats[0:1, :], s_stats[1:2, :], s_stats[2:3, :]
    logits = tile_logits(core, table, chosen, real)
    hit = tile_hit(core, table, lines, wanted)
    top = jnp.maximum(old, jnp.max(logits, axis=0, keepdims=True))
    total = total * jnp.exp(old - top)
    total = total + jnp.sum(jnp.exp(logits - top), axis=0, keepdims=True)
    picked = picked + jnp.sum(jnp.where(hit, logits, 0.0), axis=0, keepdims=True)
    s_stats[0:1, :], s_stats[1:2, :], s_stats[2:3, :] = top, total, picked
    out[...] = s_stats[...]


def table_specs(halves):
    parts, width = halves[0].shape[1], halves[0].shape[3]

    def spec(k):
        def place(c, i, core):
            mine = core[0] == k
            return (jnp.where(mine, c, 0), 0, jnp.where(mine, i, 0), 0)

        return pl.BlockSpec((1, parts, TILE, width), place)

    return [spec(0), spec(1)]


def vocab_measure(core, halves, chosen, wanted, real):
    count = chosen.shape[0]
    lines = 2 * halves[0].shape[2]
    return call(
        functools.partial(measure_kernel, real, lines),
        (CLASSES, lines // TILE // 2),
        table_specs(halves) + [whole((count, D)), whole((8, count))],
        whole((8, count)),
        struct((8, count)),
        [pltpu.VMEM((8, count), f32)],
        prefetch=1,
        flops=2 * count * halves[0].size,
        bytes_moved=2 * halves[0].size,
    )(core, *halves, chosen, wanted)


def vocab_kernel(
    real, lines, core, first_half, second_half, chosen, wanted, stats, dtable, dchosen, s_sum
):
    table = one_half(core, first_half, second_half)
    step = pl.program_id(0) * pl.num_programs(1) + pl.program_id(1)
    parts, width = table.shape[1], table.shape[3]

    @pl.when(step == 0)
    def _():
        s_sum[...] = jnp.zeros(s_sum.shape, f32)

    soft = jnp.exp(tile_logits(core, table, chosen, real) - stats[0:1, :])
    hit = tile_hit(core, table, lines, wanted)
    dlogits = (stats[1:2, :] * jnp.where(hit, soft - 1.0, soft)).astype(bf16)
    for part in range(parts):
        columns = slice(part * width, (part + 1) * width)
        dtable[0, part] = nn(dlogits, chosen[:, columns]).astype(bf16)
        s_sum[:, columns] += tn(dlogits, table[0, part])

    @pl.when(step == CLASSES * pl.num_programs(1) - 1)
    def _():
        dchosen[...] = s_sum[...].astype(bf16)


def vocab_back(core, halves, chosen, wanted, stats, real):
    count = chosen.shape[0]
    parts, lines, width = halves[0].shape[1:]
    return call(
        functools.partial(vocab_kernel, real, 2 * lines),
        (CLASSES, lines // TILE),
        table_specs(halves) + [whole((count, D)), whole((8, count)), whole((8, count))],
        [
            pl.BlockSpec((1, parts, TILE, width), lambda c, i, core: (c, 0, i, 0)),
            whole((count, D)),
        ],
        [struct(halves[0].shape, bf16), struct((count, D), bf16)],
        [pltpu.VMEM((count, D), f32)],
        prefetch=1,
        flops=6 * count * halves[0].size,
        bytes_moved=4 * halves[0].size,
    )(core, *halves, chosen, wanted, stats)


def shifted(values, axis, by):
    n = lax.axis_size(axis)
    return lax.ppermute(values, axis, [(i, (i + by) % n) for i in range(n)])


def swapped(values):
    return lax.ppermute(values, "core", [(0, 1), (1, 0)])


def to_later(values):
    return lax.ppermute(values, "core", [(0, 1)])


def to_earlier(values):
    return lax.ppermute(values, "core", [(1, 0)])


def crossed(values, axis, by):
    n = lax.axis_size(axis) if isinstance(axis, str) else axis_count(axis)
    return lax.ppermute(values, axis, [(i, i ^ by) for i in range(n)])


def axis_count(axes):
    count = 1
    for axis in axes:
        count *= lax.axis_size(axis)
    return count


def everywhere(values, axes, combine=jnp.add):
    for axis in axes:
        reach = 1
        while reach < lax.axis_size(axis):
            if 2 * reach < lax.axis_size(axis):
                one, two, three = (crossed(values, axis, by * reach) for by in (1, 2, 3))
                values = combine(combine(values, one), combine(two, three))
                reach *= 4
            else:
                values = combine(values, crossed(values, axis, reach))
                reach *= 2
    return values


def relative(values):
    values = values[None]
    for axis in ("core", "chip"):
        reach = 1
        while reach < lax.axis_size(axis):
            values = jnp.concatenate([values, crossed(values, axis, reach)], axis=0)
            reach *= 2
    return values


def exchanged(blocks):
    return jnp.stack([blocks[0]] + [crossed(blocks[r], DP, r) for r in range(1, blocks.shape[0])])


def around(values, axis):
    n = lax.axis_size(axis)
    return jnp.stack([values] + [shifted(values, axis, by) for by in range(1, n)])


def sum_back(blocks, axis):
    n = lax.axis_size(axis)
    result = blocks[0].astype(f32)
    for by in range(1, n):
        result = result + shifted(blocks[by], axis, -by).astype(f32)
    return result


def by_core(own, other, axis=0):
    first = lax.axis_index("core") == 0
    return jnp.concatenate(
        [jnp.where(first, own, other), jnp.where(first, other, own)], axis=axis
    )


def inverse_rms(values):
    return lax.rsqrt(jnp.mean(values * values, axis=-1, keepdims=True) + norm_eps)


def rms_back(grad, values, gain):
    inverse = inverse_rms(values)
    along = jnp.mean(grad * gain * values, axis=-1, keepdims=True)
    dvalues = inverse * gain * grad - values * (inverse * inverse * inverse * along)
    return (dvalues, jnp.sum(grad * values * inverse, axis=0))


def in_order(blocks, axis):
    n = blocks.shape[axis]
    z = lax.axis_index("tensor")
    taken = [lax.dynamic_index_in_dim(blocks, (z - q) % n, axis, False) for q in range(n)]
    return jnp.stack(taken, axis=axis)


def turn_heads(bcdt):
    rows = bcdt.shape[0]
    steps = bcdt[:, 2 * STATE : 2 * STATE + HEADS].reshape(rows, GROUPS, -1)
    steps = in_order(steps, 1).reshape(rows, HEADS)
    return jnp.concatenate([bcdt[:, : 2 * STATE], steps, bcdt[:, 2 * STATE + HEADS :]], axis=1)


def pack_layer(w_zx, w_bcdt, w_out):
    rows = w_zx.shape[0]
    zx = w_zx.reshape(rows, -1)
    out = jnp.concatenate([w_out[: rows // 2], w_out[rows // 2 :]], axis=1)
    own = jnp.concatenate([zx, out], axis=0).astype(bf16)
    blocks = around(own, "tensor")
    zx = blocks[:, :rows].reshape(-1, D)
    out = blocks[:, rows:].reshape(-1, D)
    lines = -(-rows // 48) * 16
    bcdt = jnp.pad(w_bcdt.astype(bf16), ((0, 3 * lines - rows), (0, LANES - HEADS)))
    bcdt = jnp.pad(bcdt[:, : 2 * STATE + HEADS].reshape(3, lines, -1), ((0, 0), (0, 0), (0, 32)))
    bcdt = jnp.concatenate([bcdt[0], bcdt[1], bcdt[2]], axis=1)
    bcdt = jnp.pad(bcdt, ((0, 0), (0, D - bcdt.shape[1])))
    return jnp.concatenate([zx, out, bcdt], axis=0)


def unpack_bcdt(packed):
    rows = D // packed.shape[0]
    lines = -(-rows // 48) * 16
    width = 2 * STATE + HEADS + 32
    part = packed[:, GROUPS * (rows + rows // 2) :]
    part = jnp.concatenate([part[:, :, i * width : (i + 1) * width] for i in range(3)], axis=1)
    part = part[:, :rows].reshape(D, width)
    return turn_heads(jnp.pad(part, ((0, 0), (0, 2 * STATE + LANES - width))))


def split_kernel(z, mine, *outs):
    n = len(outs)
    source, target = iota((LANES, LANES), 0), iota((LANES, LANES), 1)
    heads = HEADS // n
    group = (z[0] + n - target // heads) % n
    turn = (source == group * heads + target % heads) & (target < HEADS)
    steps = nn(mine[:, 2 * SHARE + 3 * WIDTH : 3 * SHARE], turn.astype(bf16)).astype(bf16)
    for by, out in enumerate(outs):
        at = (n - by) % n * SHARE
        out[:, : 3 * WIDTH] = mine[:, at : at + 3 * WIDTH]
        for part in range(2):
            low = 3 * WIDTH + part * LANES
            at = part * SHARE + 3 * WIDTH
            out[:, low : low + LANES] = mine[:, at : at + LANES]
        out[:, 3 * WIDTH + 2 * LANES :] = steps


def exchange_layer(mine):
    n_tensor = lax.axis_size("tensor")
    shape = (mine.shape[0], 3 * WIDTH + 3 * LANES)
    blocks = call(
        split_kernel,
        (1,),
        [whole(mine.shape)],
        [whole(shape)] * n_tensor,
        [struct(shape, bf16)] * n_tensor,
        [],
        prefetch=1,
        bytes_moved=4 * mine.size,
    )(lax.axis_index("tensor")[None], mine)
    return [blocks[0]] + [shifted(blocks[by], "tensor", by) for by in range(1, n_tensor)]


def sum_layer(blocks):
    blocks = [block.astype(f32) for block in blocks]
    even = functools.reduce(jnp.add, blocks[0::2])
    odd = functools.reduce(jnp.add, blocks[1::2])
    total = even + odd
    return (
        total[:, : 2 * WIDTH].reshape(-1, 2, WIDTH),
        total[:, 2 * WIDTH : 3 * WIDTH],
        total[:, 3 * WIDTH : 3 * WIDTH + 2 * STATE + HEADS],
    )


def layer_forward(resid, normed, next_gain, packed, wb, smalls):
    chan, headp, bcv = smalls
    nx = jnp.concatenate([to_later(normed[-HALO:]), normed], axis=0)
    y, gate, xraw, st, bcdt, c, ecf = scan_front(nx, packed, wb, chan, headp, bcv)
    before = to_later(st)
    y, scaled, inverse, out, following = scan_join(
        y, gate, c, ecf, before, chan, packed, resid, next_gain
    )
    return out, following, (resid, normed, y, gate, xraw, before, bcdt, c, ecf, scaled, inverse)


def layer_backward(dresid, kept, gain, packed, wb, smalls):
    resid, normed, y, gate, xraw, before, bcdt, c, ecf, scaled, inverse = kept
    chan, headp, bcv = smalls
    dout = dresid.astype(bf16)
    dy, dgate, dgain, dstart = scan_unjoin(dout, packed, y, gate, inverse, c, ecf, chan)
    after = to_earlier(dstart)
    dx, tail, halo, dchan, dbcdt, bc_halo, dheadp, dbcv = scan_back(
        xraw, dy, bcdt, before, after, chan, headp, bcv
    )
    back, bc_back = to_earlier(halo), to_earlier(bc_halo)
    grads, dresid, dnorm_gain = layer_grads(
        normed, dout, dgate, dx, tail, back, dbcdt, bc_back,
        scaled, packed, wb, resid, dresid, gain,
    )
    dchan = jnp.concatenate([dchan[: CONV + 1], dgain[:1]], axis=0)
    smalls = (dnorm_gain[0], dchan, dheadp[:3, :HEADS], dbcv[: CONV + 1])
    return dresid, grads, smalls


def flat_layer(parts, final_gain):
    gain, chan, head, taps = parts
    n_tensor = lax.axis_size("tensor")
    chan = in_order(chan.reshape(CONV + 2, n_tensor, -1), 1)
    head = in_order(head.reshape(3, n_tensor, -1), 1).reshape(3, HEADS)
    rows = [gain.reshape(-1, LANES), chan.reshape(-1, LANES), taps.reshape(-1, LANES)]
    rows.append(jnp.pad(head, ((0, 5), (0, LANES - HEADS))))
    if final_gain is not None:
        rows.append(final_gain.reshape(-1, LANES))
    return jnp.concatenate(rows)


def unflat_layer(flat):
    n_tensor = lax.axis_size("tensor")
    z = lax.axis_index("tensor")
    one, two = D // LANES, (CONV + 2) * INNER // LANES
    three = (CONV + 1) * 2 * STATE // LANES
    gain = flat[:one].reshape(D)
    chan = flat[one : one + two].reshape(CONV + 2, INNER)
    chan = lax.dynamic_slice_in_dim(chan, z * (INNER // n_tensor), INNER // n_tensor, 1)
    taps = flat[one + two : one + two + three].reshape(CONV + 1, 2 * STATE)
    head = flat[one + two + three : one + two + three + 3, :HEADS]
    head = lax.dynamic_slice_in_dim(head, z * (HEADS // n_tensor), HEADS // n_tensor, 1)
    return (gain, chan, head, taps, flat[one + two + three + 8 :].reshape(-1))


def lse_merge(first, second):
    top = jnp.maximum(first[0], second[0])
    total = first[1] * jnp.exp(first[0] - top) + second[1] * jnp.exp(second[0] - top)
    return jnp.stack([top, total, first[2] + second[2]])


def adapt(weight, first, second, grad):
    first_new = first_decay * first + (1.0 - first_decay) * grad
    second_new = second_decay * second + (1.0 - second_decay) * grad * grad
    update = (
        first_new
        / (1.0 - first_decay**STEP)
        / (jnp.sqrt(second_new / (1.0 - second_decay**STEP)) + adam_eps)
        + weight_decay * weight
    )
    return (first_new, second_new, update)


def group_squares(values, stacked):
    if stacked:
        return jnp.sum(values * values, axis=tuple(range(1, values.ndim)))
    return jnp.sum(values * values)[None]


def layer_marks(shape, axis, values):
    result = jnp.full(shape, values[0], f32)
    place = iota(shape, axis or 0)
    for i in range(1, len(values)):
        result = jnp.where(place == i, values[i], result)
    return result


def adapt_kernel(axes, scale, *refs):
    count = len(axes)
    inputs, outputs, squares = refs[: 4 * count], refs[4 * count : 7 * count], refs[-1]
    at = 0
    for k, axis in enumerate(axes):
        weight, first, second, grad = (ref[...] for ref in inputs[4 * k : 4 * k + 4])
        moved = adapt(weight, first, second, grad * scale[0])
        for ref, value in zip(outputs[3 * k : 3 * k + 3], moved):
            ref[...] = value
        square = moved[2] * moved[2]
        if axis is None:
            squares[at] = jnp.sum(square)
            at += 1
        else:
            for i in range(LAYERS):
                squares[at] = jnp.sum(jnp.where(iota(square.shape, axis) == i, square, 0.0))
                at += 1


def step_kernel(axes, factors, *refs):
    count = len(axes)
    weights, changes, outputs = refs[:count], refs[count : 2 * count], refs[2 * count :]
    at = 0
    for k, axis in enumerate(axes):
        values = [factors[at + i] for i in range(1 if axis is None else LAYERS)]
        at += len(values)
        marks = layer_marks(weights[k].shape, axis, values)
        outputs[k][...] = weights[k][...] - marks * changes[k][...]


def at_once(kernel, scalars, arrays, shapes, extra):
    smem = pl.BlockSpec(memory_space=pltpu.SMEM)
    vmem = pl.BlockSpec(memory_space=pltpu.VMEM)
    return pl.pallas_call(
        kernel,
        in_specs=[smem] + [vmem] * len(arrays),
        out_specs=[vmem] * len(shapes) + [smem] * len(extra),
        out_shape=[struct(shape) for shape in shapes + extra],
        compiler_params=pltpu.CompilerParams(vmem_limit_bytes=VMEM_BYTES),
    )(scalars, *arrays)


def body(
    token_ids, lengths, loss_pos, targets,
    embed, embed_m, embed_v,
    w_zx, w_zx_m, w_zx_v,
    w_bcdt, w_bcdt_m, w_bcdt_v,
    w_out, w_out_m, w_out_v,
    channel, channel_m, channel_v,
    per_head, per_head_m, per_head_v,
    bc_conv, bc_conv_m, bc_conv_v,
    gains, gains_m, gains_v,
):
    n_tensor = lax.axis_size("tensor")
    n_data = lax.axis_size("chip") * lax.axis_size("core")
    core = lax.axis_index("core")
    z = lax.axis_index("tensor")
    seq = token_ids.shape[1]
    rows = seq // 2
    scored = loss_pos.shape[1]
    half = scored // 2
    lines = embed.shape[0]
    padded = -(-lines // (2 * TILE)) * (2 * TILE)
    vocab = lines * CLASSES

    own_meta = jnp.concatenate([token_ids, loss_pos, targets, lengths], axis=1)
    other_meta = swapped(own_meta)
    meta = jnp.where(
        core == 0,
        jnp.stack([own_meta, other_meta], axis=1),
        jnp.stack([other_meta, own_meta], axis=1),
    ).reshape(n_tensor, -1)
    meta = jnp.stack(
        [
            lax.dynamic_index_in_dim(meta, (z - j) % n_tensor, 0, keepdims=False)
            for j in range(n_tensor)
        ]
    )
    ids = lax.dynamic_slice_in_dim(meta, core * rows, rows, 1)
    length = meta[:, seq + 2 * scored :]
    live = core * rows + jnp.arange(rows)[None, :] < length
    positions = lax.dynamic_slice_in_dim(meta, seq + core * half, half, 1)
    all_positions = meta[:, seq : seq + scored].reshape(n_tensor, 2, half).transpose(1, 0, 2)
    counted = (all_positions < length[None]).astype(f32).reshape(-1)
    all_wanted = meta[:, seq + scored : seq + 2 * scored].reshape(n_tensor, 2, half)
    all_wanted = all_wanted.transpose(1, 0, 2).reshape(1, -1)
    own_positions = meta[0, seq : seq + scored]

    def place(indices):
        local = indices - z * vocab
        return (local & 3) * padded + (local >> 2), (local >= 0) & (local < vocab)

    key, inside = place(ids)
    count = n_tensor * rows
    order = jnp.arange(rows)
    same = (ids[:, :, None] == ids[:, None, :]) & live[:, None, :]
    opening = jnp.min(jnp.where(same, order[None, None, :], rows), axis=2)
    fresh = live & (opening == order[None, :])
    hits = fresh & inside
    before = order[None, None, :] < opening[:, :, None]
    slots = jnp.sum((hits[:, None, :] & before).astype(jnp.int32), axis=2)
    fullest = jnp.max(jnp.sum(hits.astype(jnp.int32), axis=1))
    key = key * PAST + jnp.arange(n_tensor)[:, None] * rows + slots
    past = CLASSES * padded * PAST + jnp.arange(count)
    key = jnp.where(hits.reshape(count), key.reshape(count), past)
    owner = (ids[0] // vocab - z) % n_tensor
    alike = (owner[:, None] == owner[None, :]) & fresh[0][None, :] & before[0]
    spots = owner * rows + jnp.sum(alike.astype(jnp.int32), axis=1)

    def spots_at(offset):
        slot = spots % rows - offset
        here = live[0] & (slot >= 0) & (slot < CAP)
        return jnp.where(here, spots // rows * CAP + slot, n_tensor * CAP)

    every = jnp.arange(count)
    rank = jnp.sum((key[None, :] < key[:, None]).astype(jnp.int32), axis=1)
    keys = jnp.sum(jnp.where(rank[None, :] == every[:, None], key[None, :], 0), axis=1)
    edges = jnp.arange(16) * (padded // 2 * PAST)
    starts = jnp.sum((key[None, :] < edges[:, None]).astype(jnp.int32), axis=1)
    line = keys >> 11
    new = (every < starts[2 * CLASSES]) & (line != jnp.pad(line, (1, 0), constant_values=-1)[:-1])
    ranks = jnp.sum((new[None, :] & (every[None, :] <= every[:, None])).astype(jnp.int32), axis=1)
    ranks = ranks - 1
    opens = new[None, :] & (ranks[None, :] == every[:, None])
    distinct = jnp.sum(jnp.where(opens, line[None, :], 0), axis=1)
    bounds = starts[0 : 2 * CLASSES + 1 : 2]
    firsts = jnp.sum((new[None, :] & (every[None, :] < bounds[:, None])).astype(jnp.int32), axis=1)
    firsts = jnp.pad(firsts, (0, 8 - firsts.shape[0]))

    shared = relative(jnp.concatenate([distinct, firsts]))
    all_lines, all_firsts = shared[:, :count].reshape(-1), shared[:, count:].reshape(-1)
    most = jnp.max(firsts[1 : CLASSES + 1] - firsts[:CLASSES])
    most = jnp.pad(jnp.stack([most, fullest]), (0, LANES - 2))
    most = everywhere(most, ("core", "tensor", "chip"), jnp.maximum)
    most, fullest = most[0], most[1]

    low = jnp.pad(embed.astype(bf16), ((0, padded - lines), (0, 0)))
    halves = [lax.all_gather(low[: padded // 2], DP)]
    shares = [pack_layer(w_zx[i], w_bcdt[i], w_out[i]) for i in range(LAYERS)]
    inner = INNER // n_tensor
    heads = HEADS // n_tensor
    small = jnp.concatenate([channel, jnp.pad(per_head, ((0, 0), (0, 0), (0, inner - heads)))], 1)
    small = around(small, "tensor")
    channel_all = small[:, :, : CONV + 2].transpose(1, 2, 0, 3).reshape(LAYERS, CONV + 2, INNER)
    head_all = small[:, :, CONV + 2 :, :heads].transpose(1, 2, 0, 3).reshape(LAYERS, 3, HEADS)
    smalls = []
    for depth in range(LAYERS):
        headp = jnp.stack([head_all[depth, 0], -jnp.exp(head_all[depth, 1]), head_all[depth, 2]])
        smalls.append(
            (
                jnp.pad(channel_all[depth], ((0, 2), (0, 0))),
                jnp.pad(headp, ((0, 5), (0, LANES - HEADS))),
                jnp.pad(bc_conv[depth], ((0, 3), (0, 0))),
            )
        )

    ready = (shares[0], smalls, keys, starts, spots_at(0), ranks, all_lines, all_firsts, most, fullest)
    second, ready = lax.optimization_barrier((low[padded // 2 :], ready))
    share, smalls, keys, starts, spots_first, ranks, all_lines, all_firsts, most, fullest = ready
    halves.append(lax.all_gather(second, DP))
    share, _ = lax.optimization_barrier((share, halves))
    packed = [lax.all_gather(share, DP)]
    halves = [half.reshape(CLASSES, n_data // CLASSES, padded // 2, -1) for half in halves]
    found = lookup(keys, starts, halves)
    stacked = (False, True, True, True, True, True, True, False)
    everyone = n_tensor * n_data
    copies = (1, 1, n_tensor, 1, n_data, n_data, everyone, everyone)
    weights = (embed, w_zx, w_bcdt, w_out, channel, per_head, bc_conv, gains)
    found, late = lax.optimization_barrier((found, weights))
    weight_sq = jnp.concatenate(
        [group_squares(*pair) / shared_by for *pair, shared_by in zip(late, stacked, copies)]
    )
    found = found.reshape(n_tensor, rows, D)
    gain_rows = [jnp.broadcast_to(gains[i][None, :], (8, D)) for i in range(LAYERS + 1)]

    def rows_in(offset, before):
        part = found[:, offset : offset + CAP]
        part = [part[0]] + [shifted(part[by], "tensor", -by) for by in range(1, n_tensor)]
        return place_rows(
            spots_at(offset) if offset else spots_first, jnp.stack(part), before, gain_rows[0]
        )

    resid, normed = rows_in(0, None)
    for offset in range(CAP, rows, CAP):
        resid, normed = lax.cond(
            fullest > offset,
            lambda so_far, offset=offset: tuple(rows_in(offset, so_far[0])),
            lambda so_far: so_far,
            (resid, normed),
        )
    resid, weight_sq = lax.optimization_barrier((resid, weight_sq))
    for share in shares[1:]:
        share = lax.optimization_barrier((share, packed[-1], resid))[0]
        packed.append(lax.all_gather(share, DP))
    w_small = [unpack_bcdt(packed[depth]) for depth in range(LAYERS)]
    kept = []
    for depth in range(LAYERS):
        resid, normed, saved = layer_forward(
            resid, normed, gain_rows[depth + 1], packed[depth], w_small[depth], smalls[depth]
        )
        kept.append(saved)

    pick = (own_positions[:, None] - core * rows == jnp.arange(rows)[None, :]).astype(bf16)
    picked = nn(pick, normed).astype(bf16).reshape(2, half, D)
    mine = jnp.where(core == 0, picked[0], picked[1])
    other = jnp.where(core == 0, picked[1], picked[0])
    chosen = around(mine + swapped(other), "tensor").reshape(n_tensor * half, D)
    chosen = by_core(chosen, swapped(chosen))
    want, known = place(all_wanted)
    want = jnp.broadcast_to(jnp.where(known, want, -1), (8, n_tensor * scored))
    which = core[None]
    stats = vocab_measure(which, halves, chosen, want, lines)[:3]
    ordered = in_order(stats.reshape(3, 2, n_tensor, half), 2)
    ordered = everywhere(ordered, ("core", "tensor"), lse_merge)
    stats = in_order(ordered, 2).reshape(3, -1)
    log_total = stats[0] + jnp.log(stats[1])
    losses = (counted * (log_total - stats[2])).reshape(2, n_tensor, half).sum(axis=2)
    loss_sum = jnp.sum(in_order(losses, 1))
    loss_count = jnp.sum(counted)
    info = jnp.pad(jnp.stack([log_total, counted]), ((0, 6), (0, 0)))
    dtable, dchosen = vocab_back(which, halves, chosen, want, info, lines)
    dtable = dtable.reshape((-1, 2) + dtable.shape[2:])
    table_part = lax.psum_scatter(dtable, "chip", scatter_dimension=0)

    dchosen = dchosen.reshape(2, n_tensor * half, D)
    mine = jnp.where(core == 0, dchosen[0], dchosen[1])
    other = jnp.where(core == 0, dchosen[1], dchosen[0])
    dchosen = mine.astype(f32) + swapped(other).astype(f32)
    dpicked = sum_back(dchosen.astype(bf16).reshape(n_tensor, half, D), "tensor").astype(bf16)
    dpicked = by_core(dpicked, swapped(dpicked))
    onto = (core * rows + jnp.arange(rows)[:, None] == own_positions[None, :]).astype(bf16)
    dresid, dfinal_gain = rms_back(nn(onto, dpicked), resid, gains[LAYERS])

    shares = [None] * LAYERS
    parts = [None] * LAYERS
    for depth in reversed(range(LAYERS)):
        dresid, grad, parts[depth] = layer_backward(
            dresid, kept[depth], gain_rows[depth], packed[depth], w_small[depth], smalls[depth]
        )
        grad, table_part, dresid = lax.optimization_barrier((grad, table_part, dresid))
        shares[depth] = lax.psum_scatter(grad, DP, scatter_dimension=0, tiled=True)

    def rows_out(part):
        return jnp.stack(
            [part[0]] + [shifted(part[by], "tensor", by) for by in range(1, n_tensor)]
        )

    sent = send_rows(spots_first, dresid, n_tensor)
    sent, share = lax.optimization_barrier((sent, shares[1]))
    last = exchange_layer(share)
    arrived = jnp.pad(rows_out(sent), ((0, 0), (0, rows - CAP), (0, 0)))
    for offset in range(CAP, rows, CAP):
        arrived = lax.cond(
            fullest > offset,
            lambda so_far, offset=offset: lax.dynamic_update_slice(
                so_far,
                rows_out(send_rows(spots_at(offset), dresid, n_tensor)),
                (0, offset, 0),
            ),
            lambda so_far: so_far,
            arrived,
        )
    arrived = arrived.reshape(count, D)
    own = lax.axis_index(DP)
    cls = own // (n_data // CLASSES)

    def pack_round(offset):
        where = jnp.stack([own, offset])
        return pack_rows(keys, ranks, starts, firsts, where, arrived, n_data)

    def add_round(offset, recv, total):
        return tuple(add_rows(all_lines, all_firsts, jnp.stack([cls, offset]), recv, total))

    outgoing, last, parts, table_part = lax.optimization_barrier(
        (pack_round(0), last, parts, table_part)
    )
    recv = exchanged(outgoing)
    blocks = [exchange_layer(shares[0]), last]
    flat = jnp.concatenate([flat_layer(*pair) for pair in zip(parts, [None, dfinal_gain])])
    flat = everywhere(flat, ("core", "tensor", "chip"))
    keep = jnp.where(core == 0, table_part[0], table_part[1])
    give = jnp.where(core == 0, table_part[1], table_part[0])
    table_part = by_core(keep, swapped(give))
    recv, table_part, blocks, flat = lax.optimization_barrier((recv, table_part, blocks, flat))
    added = add_round(0, recv, table_part)
    added = lax.while_loop(
        lambda carry: carry[0] < most,
        lambda carry: (carry[0] + CAP, add_round(carry[0], exchanged(pack_round(carry[0])), carry[1][0])),
        (jnp.int32(CAP), added),
    )[1]
    grad_table, table_sq = added[0][:lines], jnp.sum(added[1])

    grads = [sum_layer(block) for block in blocks]
    grad_zx, grad_out, grad_bcdt = (jnp.stack(layers) for layers in zip(*grads))
    height = (flat.shape[0] - D // LANES) // LAYERS
    flats = [flat[:height], flat[height:]]
    small_grads = [unflat_layer(flat) for flat in flats]
    grad_gains = jnp.stack([part[0] for part in small_grads] + [small_grads[-1][4]])
    grad_channel, grad_head, grad_bc_conv = (
        jnp.stack([part[k] for part in small_grads]) for k in (1, 2, 3)
    )

    kinds = (
        (embed, embed_m, embed_v, grad_table),
        (w_zx, w_zx_m, w_zx_v, grad_zx),
        (w_bcdt, w_bcdt_m, w_bcdt_v, grad_bcdt),
        (w_out, w_out_m, w_out_v, grad_out),
        (channel, channel_m, channel_v, grad_channel),
        (per_head, per_head_m, per_head_v, grad_head),
        (bc_conv, bc_conv_m, bc_conv_v, grad_bc_conv),
        (gains, gains_m, gains_v, grad_gains),
    )
    kinds = [kind + pair for kind, pair in zip(kinds, zip(stacked, copies))]
    grad_sq = jnp.concatenate(
        [table_sq[None]] + [group_squares(kind[3], kind[4]) / kind[5] for kind in kinds[1:]]
    )
    groups = grad_sq.shape[0]
    totals = jnp.concatenate(
        [grad_sq, weight_sq, jnp.stack([loss_sum, loss_count]) / (2 * n_tensor)]
    )
    totals = everywhere(jnp.pad(totals, (0, LANES - totals.shape[0])), ("core", "tensor", "chip"))
    grad_sq, weight_sq = totals[:groups], totals[groups : 2 * groups]
    grad_norm = jnp.sqrt(jnp.sum(grad_sq))
    scale = jnp.minimum(1.0, clip_limit / grad_norm)
    rest = kinds[1:]
    sizes = [LAYERS if kind[4] else 1 for kind in rest]
    shares = [1.0 / kind[5] for kind, size in zip(rest, sizes) for _ in range(size)]
    turns = [(0, 1, 2, 3), (0, 2, 1), (0, 1, 2), (1, 0, 2), (1, 0, 2), (1, 0, 2), (0, 1)]
    axes = [0, 0, 0, 1, 1, 1, None]
    arrays = [array.transpose(turn) for kind, turn in zip(rest, turns) for array in kind[:4]]
    shapes = [arrays[4 * k].shape for k in range(len(rest))]
    *moved, squares = at_once(
        functools.partial(adapt_kernel, axes),
        scale[None],
        arrays,
        [shape for shape in shapes for _ in range(3)],
        [(groups - 1,)],
    )
    embed_moved = adapt(embed, embed_m, embed_v, grad_table * scale)
    step_sq = jnp.concatenate(
        [group_squares(embed_moved[2], False), squares * jnp.array(shares, f32)]
    )
    step_sq = everywhere(jnp.pad(step_sq, (0, LANES - groups)), ("core", "tensor", "chip"))[:groups]
    weight_norm = jnp.sqrt(weight_sq)
    step_norm = jnp.sqrt(step_sq)
    factors = learn_rate * (weight_norm / step_norm)
    stepped = at_once(
        functools.partial(step_kernel, axes),
        factors[1:],
        arrays[0::4] + moved[2::3],
        shapes,
        [],
    )
    results = [embed - factors[0] * embed_moved[2], embed_moved[0], embed_moved[1]]
    for k, turn in enumerate(turns):
        parts = (stepped[k], moved[3 * k], moved[3 * k + 1])
        results += [part.transpose(turn) for part in parts]
    group_norms = jnp.stack([weight_norm, step_norm])
    return (totals[2 * groups], totals[2 * groups + 1], grad_norm, group_norms, *results)


def solution(mesh):
    devices = mesh.devices.reshape(-1, 2, mesh.shape["tensor"])
    inside = Mesh(devices, ("chip", "core", "tensor"))
    by_data = P(None, DP)
    embed = (P("tensor", DP),) * 3
    w_zx = (P(None, DP, None, "tensor"),) * 3
    w_bcdt = (P(None, DP, None),) * 3
    w_out = (P(None, DP, "tensor"),) * 3
    by_tensor = (P(None, None, "tensor"),) * 6
    copied = (P(),) * 6
    states = embed + w_zx + w_bcdt + w_out + by_tensor + copied
    return jax.shard_map(
        body,
        mesh=inside,
        in_specs=(by_data,) * 4 + states,
        out_specs=(P(),) * 4 + states,
        check_vma=False,
    )
```
